32 devices in a mesh: fsdp: 8 (over z, y), rep: 4 (over x, core).
Axes of the slice: x: 2, y: 2, z: 4, core: 2. Of those that a mesh axis runs over, the one named last changes fastest.
Arguments:
- hidden_in: bfloat16 [8192, 2048], P(('fsdp', 'rep')), may hold values from -6 to 6
- segment_ids: int32 [8192], P(('fsdp', 'rep')), may hold values from 0 to 8191, as said below
- w_attn: bfloat16 [2048, 5120], P(('fsdp', 'rep'))
- w_ffn: bfloat16 [2048, 24576], P(('fsdp', 'rep'))
- gains: bfloat16 [2, 2048], P(None, ('fsdp', 'rep')), may hold values from 0.25 to 1.75
- out_grad: bfloat16 [8192, 2048], P(('fsdp', 'rep')), may hold values from -6 to 6
Outputs:
- hidden_out: bfloat16 [8192, 2048], P(('fsdp', 'rep'))
- in_grad: bfloat16 [8192, 2048], P(('fsdp', 'rep'))
- attn_grad: float32 [2048, 5120], P(('fsdp', 'rep'))
- ffn_grad: float32 [2048, 24576], P(('fsdp', 'rep'))
- gains_grad: float32 [2, 2048], P(None, ('fsdp', 'rep'))
The draws below stay inside these ranges and needn't reach their ends.
Inputs may be any that keep to these rules, and one draw needn't show every extreme that they name: `segment_ids`: each id is the index of its segment's first token, so ids never fall; a segment has 1 to 512 tokens and meets at most two of the aligned blocks of 256 tokens; some segment has exactly 512 tokens, and the last token is a segment of its own.
All inputs are finite; a program needn't handle non-finite values.
Results may differ from the reference program's by a relative error of at most 0.014.
Values may be sent and summed in bfloat16 or wider, within the bound.
No kernel may reach another device: no remote copies, remote signals or barrier semaphores. Data moves between devices by JAX's collectives and lax.ppermute only.
A program may use at most 832 MiB of HBM per device.

```python
import jax
import jax.numpy as jnp
from jax import lax

D = 2048
H = 32
KV = 8
HD = 64
FF = 8192
TOK_DEV = 256
TOKENS = 8192


def scaled_base(key, shape):
    return jax.random.normal(key, shape, jnp.float32)


def draw_w_attn(key, part):
    columns = 2 * D + 2 * KV * HD
    places = jnp.arange(columns)
    factor = jnp.where(places < D + 2 * KV * HD, D ** (-0.5), 8.0 * D ** (-0.5))
    return (scaled_base(jax.random.fold_in(key, 11), (D, columns)) * factor[None, :]).astype(jnp.bfloat16)


def draw_w_ffn(key, part):
    places = jnp.arange(3 * FF)
    factor = jnp.where(places < 2 * FF, D ** (-0.5), FF ** (-0.5))
    return (scaled_base(jax.random.fold_in(key, 13), (D, 3 * FF)) * factor[None, :]).astype(jnp.bfloat16)


def draw_segment_ids(key, part):
    blocks = TOKENS // TOK_DEV
    first_key, second_key, third_key, fourth_key = jax.random.split(jax.random.fold_in(key, 17), 4)
    block_index = jnp.arange(blocks, dtype=jnp.int32)[:, None]
    places = jnp.arange(TOK_DEV, dtype=jnp.int32)[None, :]
    cuts = jax.random.randint(first_key, (blocks, TOK_DEV), 0, 64) == 0
    start_cut = jax.random.randint(second_key, (blocks, 1), 0, 2) == 0
    inner_place = jax.random.randint(third_key, (blocks, 1), 1, TOK_DEV)
    whole = jax.random.randint(fourth_key, (), 0, blocks - 2)
    cuts = cuts | (places == inner_place) | (places == 0) & start_cut
    cuts = cuts | (places == 0) & (block_index == 0)
    cuts = cuts | (block_index == blocks - 1) & (places == TOK_DEV - 1)
    cuts = jnp.where(block_index == whole, places == 0, cuts)
    cuts = jnp.where(block_index == whole + 1, False, cuts)
    cuts = cuts | (block_index == whole + 2) & (places == 0)
    global_index = jnp.arange(TOKENS, dtype=jnp.int32)
    starts = lax.cummax(jnp.where(cuts.reshape(TOKENS), global_index, 0), axis=0)
    return starts.astype(jnp.int32)


def level_of(rng, shape, cuts, least, top_value):
    gain = 1.0
    for axis_at, shards_of in cuts:
        draws = jax.random.uniform(jax.random.fold_in(jax.random.fold_in(rng, 6), axis_at), (shards_of,), jnp.float32, least / len(cuts), top_value / len(cuts))
        gain = gain * jnp.repeat(jnp.exp(draws), shape[axis_at] // shards_of).reshape((-1,) + (1,) * (len(shape) - 1 - axis_at))
    return gain


def scatter_about(rng, extent, scale, limit, cuts=(), held_as=jnp.bfloat16):
    gain = level_of(rng, extent, cuts, -0.22, 0.18) if cuts else 1.0
    result = jax.random.normal(rng, extent, jnp.float32) * scale * gain
    return jnp.minimum(jnp.maximum(result, -limit), limit).astype(held_as)


def setup_inputs(seed: int = 0) -> dict:
    seeds = jax.random.split(jax.random.key(seed), 7)
    return {
        "hidden_in": scatter_about(seeds[0], (TOKENS, D), 1.0, 6.0, ((0, 32),)),
        "segment_ids": draw_segment_ids(jax.random.fold_in(seeds[6], 71), 0),
        "w_attn": draw_w_attn(jax.random.fold_in(seeds[6], 71), 0),
        "w_ffn": draw_w_ffn(jax.random.fold_in(seeds[6], 71), 0),
        "gains": jnp.clip(1.0 + 0.15 * jax.random.normal(seeds[4], (2, D), jnp.float32), 0.25, 1.75).astype(jnp.bfloat16),
        "out_grad": scatter_about(seeds[5], (TOKENS, D), 1.0, 6.0, ((0, 32),)),
    }


NORM_EPS = 1e-05
ROPE_BASE = 500000.0

@jax.custom_vjp
def low(v):
    return lax.optimization_barrier(v.astype(jnp.bfloat16)).astype(jnp.float32)

@jax.custom_vjp
def low_back(v):
    return v

def low_keep(v):
    return (low(v), None)

def low_pass(kept, grad):
    return (grad,)

def back_keep(v):
    return (v, None)

def back_low(kept, grad):
    return (low(grad),)
low.defvjp(low_keep, low_pass)
low_back.defvjp(back_keep, back_low)

def matmul(left, right):
    return jnp.dot(left, right, precision=lax.Precision.HIGHEST, preferred_element_type=jnp.float32)

def rms_norm(values, scales):
    return values * lax.rsqrt(lax.optimization_barrier(jnp.mean(values * values, axis=-1, keepdims=True)) + NORM_EPS) * scales

def rotary(positions):
    freqs = 1.0 / ROPE_BASE ** (jnp.arange(HD // 2, dtype=jnp.float32) * (2.0 / HD))
    angles = positions.astype(jnp.float32)[..., None] * freqs
    cosine = jnp.concatenate([jnp.cos(angles), jnp.cos(angles)], axis=-1)
    sine = jnp.concatenate([jnp.sin(angles), jnp.sin(angles)], axis=-1)
    return (cosine, sine)

def rotate(values, cosine, sine):
    halfway = values.shape[-1] // 2
    turned = jnp.concatenate([-values[..., halfway:], values[..., :halfway]], axis=-1)
    return values * cosine + turned * sine

def attend_block(item):
    q_blk, k_two, v_two, allowed = item
    scores = low_back(jnp.einsum('tkrd,skd->krts', q_blk, k_two, precision=lax.Precision.HIGHEST) * HD ** (-0.5))
    scores = jnp.where(allowed[None, None], scores, -1e+30)
    expo = jnp.exp(scores - lax.optimization_barrier(jnp.max(scores, axis=-1, keepdims=True)))
    probs = low(expo / lax.optimization_barrier(jnp.sum(expo, axis=-1, keepdims=True)))
    return jnp.einsum('krts,skd->tkrd', probs, v_two, precision=lax.Precision.HIGHEST)

def with_previous(blocked):
    earlier = jnp.concatenate([jnp.zeros_like(blocked[:1]), blocked[:-1]], axis=0)
    return jnp.concatenate([earlier, blocked], axis=1)

def forward(inputs, w_attn, w_ffn, gains, cosine, sine, allowed):
    blocks = allowed.shape[0]
    length = allowed.shape[1]
    total_rows = inputs.shape[0]
    qkv_cols = D + 2 * KV * HD
    group = H // KV
    normed = low(rms_norm(inputs, gains[0]))
    query = low_back(matmul(normed, w_attn[:, :D]))
    keys = low_back(matmul(normed, w_attn[:, D:D + KV * HD]))
    values = low(low_back(matmul(normed, w_attn[:, D + KV * HD:qkv_cols])))
    query = query.reshape(total_rows, KV, group, HD)
    keys = keys.reshape(total_rows, KV, HD)
    values = values.reshape(blocks, length, KV, HD)
    q_rot = low(rotate(query, cosine[:, None, None], sine[:, None, None])).reshape(blocks, length, KV, group, HD)
    k_rot = low(rotate(keys, cosine[:, None], sine[:, None])).reshape(blocks, length, KV, HD)
    mixed = lax.map(jax.checkpoint(attend_block), (q_rot, with_previous(k_rot), with_previous(values), allowed))
    mixed = low(low_back(mixed.reshape(total_rows, D)))
    attended = low_back(matmul(mixed, w_attn[:, qkv_cols:].T))
    residual = inputs + attended
    normed_two = low(rms_norm(residual, gains[1]))
    gate = low_back(matmul(normed_two, w_ffn[:, :FF]))
    upward = low_back(matmul(normed_two, w_ffn[:, FF:2 * FF]))
    hidden = low(gate * jax.nn.sigmoid(gate) * upward)
    return residual + low_back(matmul(hidden, w_ffn[:, 2 * FF:].T))

def reference(hidden_in, segment_ids, w_attn, w_ffn, gains, out_grad):
    blocks = TOKENS // TOK_DEV
    places = jnp.arange(TOKENS, dtype=jnp.int32)
    positions = places - segment_ids
    cosine, sine = rotary(positions)
    query_index = places.reshape(blocks, TOK_DEV)
    key_index = query_index[:, :1] - TOK_DEV + jnp.arange(2 * TOK_DEV, dtype=jnp.int32)[None, :]
    segs = segment_ids.reshape(blocks, TOK_DEV)
    allowed = (segs[:, :, None] <= key_index[:, None, :]) & (key_index[:, None, :] <= query_index[:, :, None])
    inputs = hidden_in.astype(jnp.float32)
    cotan = out_grad.astype(jnp.float32)
    attn_f = w_attn.astype(jnp.float32)
    ffn_f = w_ffn.astype(jnp.float32)
    gains_f = gains.astype(jnp.float32)

    def local(a_in, a_attn, a_ffn, a_gains):
        return forward(a_in, a_attn, a_ffn, a_gains, cosine, sine, allowed)
    output, pull = jax.vjp(local, inputs, attn_f, ffn_f, gains_f)
    d_inputs, d_attn, d_ffn, d_gains = pull(cotan)
    return (output.astype(jnp.bfloat16), d_inputs.astype(jnp.bfloat16), d_attn, d_ffn, d_gains)
```

```python
import jax
import jax.numpy as jnp
from jax import lax
from jax.sharding import Mesh, PartitionSpec as P

D = 2048
H = 32
KV = 8
HD = 64
FF = 8192
GROUP = H // KV
TP = 8
CHUNKS = 4

NORM_EPS = 1e-05
ROPE_BASE = 500000.0

PLANE = ("y", "x", "c")
EVERY = ("z", "y", "x", "c")
BF = jnp.bfloat16
F32 = jnp.float32


def swap(value, rel):
    return lax.ppermute(value, PLANE, [(i, i ^ rel) for i in range(TP)])


def gather_plane(own):
    half = own.shape[0] // 2
    blk = [own] + [None] * 7
    blk[2] = swap(own, 2)
    blk[4] = swap(own, 4)
    blk[1] = swap(own, 1)
    first = swap(blk[2][:half], 4)
    second = swap(blk[4][half:], 2)
    blk[3] = swap(blk[2], 1)
    blk[5] = swap(blk[4], 1)
    blk[6] = jnp.concatenate([first, second], axis=0)
    blk[7] = swap(blk[6], 1)
    return blk


def scatter_plane(parts):
    half = parts.shape[1] // 2
    arrived = swap(parts[1::2], 1)
    both = (parts[0::2].astype(F32) + arrived.astype(F32)).astype(BF)
    from_x = swap(both[3, :half], 2)
    from_y = swap(both[3, half:], 4)
    x_first = swap(both[1, :half], 2)
    y_second = swap(both[2, half:], 4)
    y_first = swap((both[2, :half].astype(F32) + from_x.astype(F32)).astype(BF), 4)
    x_second = swap((both[1, half:].astype(F32) + from_y.astype(F32)).astype(BF), 2)
    x_part = jnp.concatenate([x_first, x_second], axis=0).astype(F32)
    y_part = jnp.concatenate([y_first, y_second], axis=0).astype(F32)
    return both[0].astype(F32) + x_part + y_part


def exchange(blocks):
    return [blocks[0]] + [swap(blocks[r], r) for r in range(1, TP)]


def along_z(value, steps):
    count = lax.axis_size("z")
    return lax.ppermute(
        value, "z", [(i, i + steps) for i in range(count) if 0 <= i + steps < count]
    )


def fetch(pieces):
    rows, cols = pieces.shape[1:]
    mine = lax.all_to_all(pieces, PLANE, 0, 0, tiled=True).reshape(TP * rows, cols)
    return lax.all_gather(mine, "z", axis=0, tiled=True)


def give_back(grad):
    cols = grad.shape[1]
    summed = lax.psum_scatter(grad.astype(BF), "z", scatter_dimension=0, tiled=True)
    return lax.all_to_all(
        summed.reshape(TP, summed.shape[0] // TP, cols), PLANE, 0, 0, tiled=True
    )


def rms_norm(values, scales):
    return values * lax.rsqrt(jnp.mean(values * values, axis=-1, keepdims=True) + NORM_EPS) * scales


def rotary(positions):
    freqs = 1.0 / ROPE_BASE ** (jnp.arange(HD // 2, dtype=F32) * (2.0 / HD))
    angles = positions.astype(F32)[..., None] * freqs
    return jnp.cos(angles), jnp.sin(angles)


def turn(first, second, cosine, sine):
    return first * cosine - second * sine, second * cosine + first * sine


def mm(left, right, dims):
    return lax.dot_general(left, right, (dims, ((), ())), preferred_element_type=F32)


def on_device(hidden_in, segment_ids, w_attn, w_ffn, gains, out_grad):
    tok = hidden_in.shape[0]
    rows = w_attn.shape[0]
    me = lax.axis_index(PLANE)
    z = lax.axis_index("z")
    kv_cols = KV * HD
    qkv_cols = D + 2 * kv_cols
    tokens = TP * tok
    rel = me ^ jnp.arange(TP, dtype=jnp.int32)

    w_q = w_attn[:, :D].reshape(rows, TP, GROUP, 2, HD // 2).transpose(1, 0, 3, 2, 4)
    w_q = w_q.reshape(TP, rows, GROUP * HD)
    w_k = w_attn[:, D : D + kv_cols].reshape(rows, TP, HD).transpose(1, 0, 2)
    w_v = w_attn[:, D + kv_cols : qkv_cols].reshape(rows, TP, HD).transpose(1, 0, 2)
    w_o = w_attn[:, qkv_cols:].reshape(rows, TP, GROUP * HD).transpose(1, 0, 2)
    wqkv = fetch(jnp.concatenate([w_q, w_k, w_v], axis=2))
    wo = fetch(w_o)
    step = FF // TP // CHUNKS
    ffn_cut = w_ffn.reshape(rows, 3, CHUNKS, TP, step).transpose(2, 3, 0, 1, 4)
    ffn = [fetch(ffn_cut[j].reshape(TP, rows, 3 * step)) for j in range(CHUNKS)]

    gains_full = lax.all_gather(gains, EVERY, axis=1, tiled=True).astype(F32)
    seg_all = lax.all_gather(segment_ids, PLANE, axis=0, tiled=True).reshape(TP, tok)
    seg_rel = jnp.take(seg_all, rel, axis=0)
    starts = (z * TP + rel) * tok
    positions = starts[:, None] + jnp.arange(tok, dtype=jnp.int32)[None] - seg_rel
    cosine, sine = rotary(positions.reshape(tokens))

    x_all = jnp.concatenate(gather_plane(hidden_in), axis=0).astype(F32)
    normed = rms_norm(x_all, gains_full[0]).astype(BF)
    qkv = mm(normed, wqkv, ((1,), (0,)))
    half = HD // 2
    q4 = qkv[:, : GROUP * HD].reshape(tokens, 2, GROUP, half)
    qa, qb = turn(q4[:, 0], q4[:, 1], cosine[:, None], sine[:, None])
    q_rot = jnp.concatenate([qa, qb], axis=-1).astype(BF)
    k_raw = qkv[:, GROUP * HD : GROUP * HD + HD]
    ka, kb = turn(k_raw[:, :half], k_raw[:, half:], cosine, sine)
    k_rot = jnp.concatenate([ka, kb], axis=-1).astype(BF)
    v = qkv[:, GROUP * HD + HD :].astype(BF)
    kv = jnp.concatenate([k_rot, v], axis=1).reshape(TP, tok, 2 * HD)
    last = jnp.take(kv, me ^ (TP - 1), axis=0)
    before = along_z(last, 1)
    kv9 = jnp.concatenate([kv, before[None]], axis=0)
    prev_at = jnp.where(rel == 0, TP, (rel - 1) ^ me)
    kv_prev = jnp.take(kv9, prev_at, axis=0)
    kv_two = jnp.concatenate([kv_prev, kv], axis=1)
    k_two, v_two = kv_two[..., :HD], kv_two[..., HD:]
    lo = seg_rel - starts[:, None] + tok
    key_at = jnp.arange(2 * tok, dtype=jnp.int32)
    allowed = (lo[:, :, None] <= key_at) & (key_at <= jnp.arange(tok, dtype=jnp.int32)[:, None] + tok)
    q_blk = q_rot.reshape(TP, tok, GROUP, HD)

    def scores():
        s = jnp.einsum("btrd,bsd->brts", q_blk, k_two, preferred_element_type=F32) * HD ** (-0.5)
        return jnp.where(allowed[:, None], s, -1e30)

    s = scores()
    row_max = jnp.max(s, axis=-1, keepdims=True)
    expo = jnp.exp(s - row_max)
    total = jnp.sum(expo, axis=-1, keepdims=True)
    lse = row_max + jnp.log(total)
    probs = (expo / total).astype(BF)
    mixed = jnp.einsum("brts,bsd->btrd", probs, v_two, preferred_element_type=F32)
    mixed = mixed.astype(BF).reshape(TP, tok, GROUP * HD)

    wo_rel = jnp.concatenate(gather_plane(wo), axis=1)
    o_mine = jnp.concatenate(exchange([mixed[r] for r in range(TP)]), axis=1)
    x_own = hidden_in.astype(F32)
    residual = x_own + mm(o_mine, wo_rel, ((1,), (1,)))
    normed_two, norm_two_back = jax.vjp(rms_norm, residual, gains_full[1])
    n2 = jnp.concatenate(gather_plane(normed_two.astype(BF)), axis=0)
    dy = jnp.concatenate(gather_plane(out_grad), axis=0)

    acts, d_gus, ffn_grads = [], [], []
    for w in ffn:
        gate_up = mm(n2, w[:, : 2 * step], ((1,), (0,)))
        d_act = mm(dy, w[:, 2 * step :], ((1,), (0,)))
        g, u = gate_up[:, :step], gate_up[:, step:]
        sg = jax.nn.sigmoid(g)
        act = (g * sg * u).astype(BF)
        d_g = (d_act * u * (sg * (1.0 + g * (1.0 - sg)))).astype(BF)
        d_u = (d_act * g * sg).astype(BF)
        d_gu = jnp.concatenate([d_g, d_u], axis=1)
        acts.append(act)
        d_gus.append(d_gu)
        grad = jnp.concatenate([mm(n2, d_gu, ((0,), (0,))), mm(dy, act, ((0,), (0,)))], axis=1)
        ffn_grads.append(give_back(grad))
    w_all = jnp.concatenate([w[:, : 2 * step] for w in ffn], axis=1)
    wd_all = jnp.concatenate([w[:, 2 * step :] for w in ffn], axis=1)
    d_n2 = mm(jnp.concatenate(d_gus, axis=1), w_all, ((1,), (1,))).astype(BF)
    d_normed_two = scatter_plane(d_n2.reshape(TP, tok, D))
    f_out = mm(jnp.concatenate(acts, axis=1), wd_all, ((1,), (1,))).astype(BF)
    hidden_out = (residual + scatter_plane(f_out.reshape(TP, tok, D))).astype(BF)

    d_resid_norm, d_gain_two = norm_two_back(d_normed_two)
    d_resid = out_grad.astype(F32) + d_resid_norm
    d_att = d_resid.astype(BF)
    d_mixed = mm(d_att, wo_rel, ((1,), (0,))).astype(BF).reshape(tok, TP, GROUP * HD)
    d_o = jnp.stack(exchange([d_mixed[:, r] for r in range(TP)]), axis=0)
    d_att_all = jnp.concatenate(gather_plane(d_att), axis=0)
    wo_grad = give_back(mm(d_att_all, mixed.reshape(tokens, GROUP * HD), ((0,), (0,))))

    d_o = d_o.reshape(TP, tok, GROUP, HD)
    p_full = jnp.exp(scores() - lse)
    d_p = jnp.einsum("btrd,bsd->brts", d_o, v_two, preferred_element_type=F32)
    d_v_two = jnp.einsum("brts,btrd->bsd", p_full.astype(BF), d_o, preferred_element_type=F32)
    shift = jnp.sum(d_p * p_full, axis=-1, keepdims=True)
    d_s = (p_full * (d_p - shift)).astype(BF)
    d_q = jnp.einsum("brts,bsd->btrd", d_s, k_two, preferred_element_type=F32) * HD ** (-0.5)
    d_k_two = jnp.einsum("brts,btrd->bsd", d_s, q_blk, preferred_element_type=F32) * HD ** (-0.5)
    d_kv_two = jnp.concatenate([d_k_two, d_v_two], axis=2)
    d_prev = d_kv_two[:, :tok]
    back = along_z(jnp.take(d_prev, me, axis=0).astype(BF), -1).astype(F32)
    d_prev9 = jnp.concatenate([d_prev, back[None]], axis=0)
    next_at = jnp.where(rel == TP - 1, TP, (rel + 1) ^ me)
    d_kv = (d_kv_two[:, tok:] + jnp.take(d_prev9, next_at, axis=0)).reshape(tokens, 2 * HD)
    d_q = d_q.reshape(tokens, GROUP, HD)
    dqa, dqb = turn(d_q[..., :half], d_q[..., half:], cosine[:, None], -sine[:, None])
    dka, dkb = turn(d_kv[:, :half], d_kv[:, half:HD], cosine, -sine)
    d_qkv = jnp.concatenate(
        [
            dqa.reshape(tokens, GROUP * half),
            dqb.reshape(tokens, GROUP * half),
            dka,
            dkb,
            d_kv[:, HD:],
        ],
        axis=1,
    ).astype(BF)
    d_n1 = mm(d_qkv, wqkv, ((1,), (1,))).astype(BF)
    d_normed = scatter_plane(d_n1.reshape(TP, tok, D))
    qkv_grad = give_back(mm(normed, d_qkv, ((0,), (0,))))
    unused, norm_one_back = jax.vjp(rms_norm, x_own, gains_full[0])
    d_in_norm, d_gain_one = norm_one_back(d_normed)
    in_grad = (d_resid + d_in_norm).astype(BF)
    gains_grad = lax.psum_scatter(
        jnp.stack([d_gain_one, d_gain_two]), EVERY, scatter_dimension=1, tiled=True
    )

    g_q = qkv_grad[:, :, : GROUP * HD].reshape(TP, rows, 2, GROUP, half).transpose(1, 0, 3, 2, 4)
    g_k = qkv_grad[:, :, GROUP * HD : GROUP * HD + HD].transpose(1, 0, 2)
    g_v = qkv_grad[:, :, GROUP * HD + HD :].transpose(1, 0, 2)
    attn_grad = jnp.concatenate(
        [
            g_q.reshape(rows, D),
            g_k.reshape(rows, kv_cols),
            g_v.reshape(rows, kv_cols),
            wo_grad.transpose(1, 0, 2).reshape(rows, D),
        ],
        axis=1,
    ).astype(F32)
    f_stack = jnp.stack(ffn_grads, axis=0).reshape(CHUNKS, TP, rows, 3, step)
    ffn_grad = f_stack.transpose(2, 3, 0, 1, 4).reshape(rows, 3 * FF).astype(F32)
    return hidden_out, in_grad, attn_grad, ffn_grad, gains_grad


def solution(mesh):
    fine = Mesh(mesh.devices.reshape(-1, 2, 2, 2), EVERY)
    rows = P(EVERY, None)
    in_specs = (rows, P(EVERY), rows, rows, P(None, EVERY), rows)
    out_specs = (rows, rows, rows, rows, P(None, EVERY))
    return jax.shard_map(
        on_device, mesh=fine, in_specs=in_specs, out_specs=out_specs, check_vma=False
    )
```

```python
import functools

import jax
import jax.numpy as jnp
from jax import lax
from jax.experimental import pallas as pl
from jax.experimental.pallas import tpu as pltpu
from jax.sharding import Mesh, PartitionSpec as P

D = 2048
H = 32
KV = 8
HD = 64
FF = 8192
GROUP = H // KV
TP = 8
WIDTHS = (512, 512)
CHUNKS = len(WIDTHS)
HALF = HD // 2
QW = GROUP * HD
STARTS = [TP * sum(WIDTHS[:k]) for k in range(CHUNKS)]
EXTRA = 8
AW = 2 * QW + 2 * HD

NORM_EPS = 1e-05
ROPE_BASE = 500000.0
SCALE = HD ** (-0.5)

PLANE = ("y", "x", "c")
EVERY = ("z", "y", "x", "c")
BF = jnp.bfloat16
F32 = jnp.float32
ANY = pl.BlockSpec(memory_space=pl.ANY)
VMEM = pl.BlockSpec(memory_space=pltpu.VMEM)
SMEM = pl.BlockSpec(memory_space=pltpu.SMEM)
BIG = pltpu.CompilerParams(vmem_limit_bytes=56 * 1024 * 1024)


def cost(flops, size):
    return pl.CostEstimate(flops=int(flops), bytes_accessed=int(size), transcendentals=0)


def mm(left, right, dims):
    return lax.dot_general(left, right, (dims, ((), ())), preferred_element_type=F32)


NN = ((1,), (0,))
NT = ((1,), (1,))
TN = ((0,), (0,))


def swap(value, rel):
    return lax.ppermute(value, PLANE, [(i, i ^ rel) for i in range(TP)])


def swap_across(value):
    return lax.ppermute(value, PLANE, [(i, i ^ (2 + 2 * (i % 2))) for i in range(TP)])


def on_first():
    return lax.axis_index(PLANE) % 2 == 0


def gather_begin(own):
    return own, swap(own, 2), swap(own, 4), swap(own, 1)


def gather_end(own, from_x, from_y, from_c):
    across = swap_across(jnp.where(on_first(), from_y, from_x))
    return [own, from_c, from_x, swap(from_x, 1), from_y, swap(from_y, 1), across, swap(across, 1)]


def gather_plane(own):
    return gather_end(*gather_begin(own))


def add(left, right):
    return (left.astype(F32) + right.astype(F32)).astype(BF)


def scatter_plane(part):
    even, odd = part((3, 2))
    both = add(even, swap(odd, 1))
    across, over_y = swap_across(both[0]), both[1]
    even, odd = part((1, 0))
    both = add(even, swap(odd, 1))
    over_x, own = both[0], both[1]
    first = on_first()
    over_x = jnp.where(first, over_x, add(over_x, across))
    over_y = jnp.where(first, add(over_y, across), over_y)
    return own, swap(over_x, 2), swap(over_y, 4)


def total(own, from_x, from_y):
    return own.astype(F32) + from_x.astype(F32) + from_y.astype(F32)


def trade(blocks):
    return lax.all_to_all(blocks, PLANE, 0, 0, tiled=True)


def along_z(value, steps):
    count = lax.axis_size("z")
    return lax.ppermute(
        value, "z", [(i, i + steps) for i in range(count) if 0 <= i + steps < count]
    )


def gather_z(own):
    return lax.all_gather(own, "z", axis=0, tiled=True)


def start_rows(refs, dst, sems, first=0):
    each = dst.shape[0] // TP
    for r, ref in enumerate(refs):
        pltpu.make_async_copy(ref.at[pl.ds(first, each)], dst.at[pl.ds(r * each, each)], sems.at[r]).start()


def wait_rows(r, dst, sems):
    each = dst.shape[0] // TP
    part = dst.at[pl.ds(pl.multiple_of(r * each, each), each)]
    pltpu.make_async_copy(part, part, sems.at[r]).wait()


def fold_order():
    old = jnp.arange(QW, dtype=jnp.int32)
    new = (old // HALF) % 2 * (GROUP * HALF) + old // HD * HALF + old % HALF
    return (new[:, None] == jnp.arange(QW, dtype=jnp.int32)[None, :]).astype(BF)


def cut_attn_kernel(w_ref, perm_ref, out):
    kv_cols = KV * HD
    for i in range(TP):
        q = jnp.dot(w_ref[:, QW * i : QW * (i + 1)], perm_ref[...], preferred_element_type=F32)
        out[i, :, :QW] = q.astype(BF)
        k = w_ref[:, D + HD * i : D + HD * (i + 1)]
        v = w_ref[:, D + kv_cols + HD * i : D + kv_cols + HD * (i + 1)]
        out[i, :, QW : QW + 2 * HD] = jnp.concatenate([k, v], axis=1)
        out[i, :, QW + 2 * HD :] = w_ref[:, D + 2 * kv_cols + QW * i : D + 2 * kv_cols + QW * (i + 1)]


def cut_attn(w_attn, perm):
    rows = w_attn.shape[0]
    return pl.pallas_call(
        cut_attn_kernel,
        out_shape=jax.ShapeDtypeStruct((TP, rows, AW), BF),
        in_specs=[VMEM, VMEM],
        out_specs=VMEM,
        cost_estimate=cost(0, 2 * w_attn.size * 2),
        name="cut_attn",
    )(w_attn, perm)


def cut_ffn_kernel(w_ref, *outs):
    for k, width in enumerate(WIDTHS):
        for i in range(TP):
            for n in range(3):
                at = n * FF + STARTS[k] + i * width
                outs[k][i, :, n * width : (n + 1) * width] = w_ref[:, at : at + width]


def cut_ffn(w_ffn):
    rows = w_ffn.shape[0]
    return pl.pallas_call(
        cut_ffn_kernel,
        out_shape=[jax.ShapeDtypeStruct((TP, rows, 3 * width), BF) for width in WIDTHS],
        in_specs=[VMEM],
        out_specs=[VMEM] * CHUNKS,
        cost_estimate=cost(0, 2 * w_ffn.size * 2),
        compiler_params=BIG,
        name="cut_ffn",
    )(w_ffn)


def paste_ffn_kernel(*refs):
    pieces, w, out, term = refs[:CHUNKS], *refs[CHUNKS:]
    each = min(WIDTHS)
    total = jnp.zeros((w.shape[0], each), F32)
    for k, width in enumerate(WIDTHS):
        for i in range(TP):
            for n in range(3):
                for part in range(0, width, each):
                    at = n * FF + STARTS[k] + i * width + part
                    grad = pieces[k][i, :, n * width + part : n * width + part + each].astype(F32)
                    out[:, at : at + each] = grad
                    if n < 2:
                        total += grad * w[:, at : at + each].astype(F32)
    term[...] = jnp.sum(total, axis=-1, keepdims=True)


def paste_ffn(pieces, w_ffn):
    rows = w_ffn.shape[0]
    return pl.pallas_call(
        paste_ffn_kernel,
        out_shape=(jax.ShapeDtypeStruct(w_ffn.shape, F32), jax.ShapeDtypeStruct((rows, 1), F32)),
        in_specs=[VMEM] * (CHUNKS + 1),
        out_specs=(VMEM, VMEM),
        cost_estimate=cost(0, 8 * w_ffn.size),
        compiler_params=BIG,
        name="paste_ffn",
    )(*pieces, w_ffn)


def paste_attn_kernel(piece, w, perm, out, term):
    kv_cols = KV * HD
    ones = jnp.zeros((w.shape[0], QW), F32)
    small = jnp.zeros((w.shape[0], HD), F32)
    for i in range(TP):
        q = mm(piece[i, :, :QW], perm[...], NT)
        out[:, QW * i : QW * (i + 1)] = q
        ones += q * w[:, QW * i : QW * (i + 1)].astype(F32)
        kv = piece[i, :, QW : QW + 2 * HD].astype(F32)
        for at, part in ((D + HD * i, kv[:, :HD]), (D + kv_cols + HD * i, kv[:, HD:])):
            out[:, at : at + HD] = part
            small += part * w[:, at : at + HD].astype(F32)
        at = D + 2 * kv_cols + QW * i
        out[:, at : at + QW] = piece[i, :, QW + 2 * HD :].astype(F32)
    term[...] = jnp.sum(ones, axis=-1, keepdims=True) + jnp.sum(small, axis=-1, keepdims=True)


def paste_attn(piece, w_attn, perm):
    rows = w_attn.shape[0]
    return pl.pallas_call(
        paste_attn_kernel,
        out_shape=(jax.ShapeDtypeStruct(w_attn.shape, F32), jax.ShapeDtypeStruct((rows, 1), F32)),
        in_specs=[VMEM] * 3,
        out_specs=(VMEM, VMEM),
        cost_estimate=cost(0, 8 * w_attn.size),
        compiler_params=BIG,
        name="paste_attn",
    )(piece, w_attn, perm)


def turn_kernel(x, out):
    rows = out.shape[1]
    turned = x[...].astype(F32).T.astype(BF)
    for i in range(TP):
        out[i] = turned[rows * i : rows * (i + 1)]


def turn(x):
    cols, wide = x.shape
    return pl.pallas_call(
        turn_kernel,
        out_shape=jax.ShapeDtypeStruct((TP, wide // TP, cols), BF),
        in_specs=[VMEM],
        out_specs=VMEM,
        cost_estimate=cost(0, 4 * x.size),
        compiler_params=BIG,
        name="turn",
    )(x)


def qkv_kernel(count, *refs):
    blocks = refs[:count]
    gain, w_all, cos, sin, n1, q_out, kv_out, x_s, w_s, sems, w_sem = refs[count:]
    w_copy = pltpu.make_async_copy(w_all.at[:, pl.ds(0, w_s.shape[1]), pl.ds(0, w_s.shape[2])], w_s, w_sem)
    w_copy.start()
    start_rows(blocks, x_s, sems)
    each = x_s.shape[0] // TP
    lane = lax.broadcasted_iota(jnp.int32, (each, 2 * HD), 1)
    w_copy.wait()

    def step(r, carry):
        at = pl.ds(pl.multiple_of(r * each, each), each)
        wait_rows(r, x_s, sems)
        x = x_s[at, :].astype(F32)
        scale = lax.rsqrt(jnp.mean(x * x, axis=-1, keepdims=True) + NORM_EPS)
        normed = (x * scale * gain[...]).astype(BF)
        n1[at, :] = normed
        qkv = jnp.dot(normed, w_s[...].reshape(D, QW + 2 * HD), preferred_element_type=F32)
        c, s = cos[at, :], sin[at, :]
        a, b = qkv[:, : QW // 2], qkv[:, QW // 2 : QW]
        q_out[at, : QW // 2] = (a * c - b * s).astype(BF)
        q_out[at, QW // 2 :] = (b * c + a * s).astype(BF)
        kv = qkv[:, QW:]
        ahead = pltpu.roll(kv, 2 * HD - HALF, 1)
        behind = pltpu.roll(kv, HALF, 1)
        turned = kv * c + jnp.where(lane < HALF, -ahead, behind) * s
        kv_out[at, :] = jnp.where(lane < HD, turned, kv).astype(BF)
        return carry

    lax.fori_loop(0, TP, step, 0)


def norm_qkv(blocks, gain, w_all, cos, sin):
    each = w_all.shape[1] - EXTRA
    tokens = cos.shape[0]
    return pl.pallas_call(
        functools.partial(qkv_kernel, len(blocks)),
        out_shape=(
            jax.ShapeDtypeStruct((tokens, D), BF),
            jax.ShapeDtypeStruct((tokens, QW), BF),
            jax.ShapeDtypeStruct((tokens, 2 * HD), BF),
        ),
        in_specs=[ANY] * len(blocks) + [VMEM, ANY, VMEM, VMEM],
        out_specs=(VMEM, VMEM, VMEM),
        scratch_shapes=[
            pltpu.VMEM((tokens, D), BF),
            pltpu.VMEM((w_all.shape[0], each, QW + 2 * HD), BF),
            pltpu.SemaphoreType.DMA((TP,)),
            pltpu.SemaphoreType.DMA,
        ],
        cost_estimate=cost(2 * tokens * D * (QW + 2 * HD), 4 * tokens * D),
        compiler_params=BIG,
        name="norm_qkv",
    )(*blocks, gain, w_all, cos, sin)


def spread_kv():
    src = jnp.arange(2 * HD, dtype=jnp.int32)[:, None]
    col = jnp.arange(QW, dtype=jnp.int32)[None, :]
    key = (src == col // (GROUP * HALF) * HALF + col % HALF).astype(BF)
    value = (src == HD + col % HD).astype(BF)
    return key, value


def attend_kernel(prev_at, index, q_ref, prev_ref, here_ref, lo_ref, ek, ev, o_ref, o_index_ref):
    tok = q_ref.shape[0]
    two = jnp.concatenate([prev_ref[...], here_ref[...]], axis=0)
    keys = jnp.dot(two, ek[...], preferred_element_type=F32).astype(BF)
    values = jnp.dot(two, ev[...], preferred_element_type=F32).astype(BF)
    q = q_ref[...]
    key_at = lax.broadcasted_iota(jnp.int32, (tok, 2 * tok), 1)
    row_at = lax.broadcasted_iota(jnp.int32, (tok, 2 * tok), 0)
    allowed = (lo_ref[...] <= key_at) & (key_at <= row_at + tok)
    q_lane = lax.broadcasted_iota(jnp.int32, (tok, QW), 1)
    v_lane = lax.broadcasted_iota(jnp.int32, (2 * tok, QW), 1)
    total = jnp.zeros((tok, QW), F32)
    for h in range(GROUP):
        mine = jnp.where((q_lane // HALF) % GROUP == h, q, jnp.zeros_like(q))
        s = jnp.where(allowed, mm(mine, keys, NT) * SCALE, -1e30)
        expo = jnp.exp(s - jnp.max(s, axis=-1, keepdims=True))
        probs = (expo / jnp.sum(expo, axis=-1, keepdims=True)).astype(BF)
        total += mm(probs, jnp.where(v_lane // HD == h, values, jnp.zeros_like(values)), NN)
    o_ref[...] = total.astype(BF)
    o_index_ref[0] = o_ref[...]


def attend(prev_at, index, q, kv9, lo_col, ek, ev):
    tokens = q.shape[0]
    tok = tokens // TP
    full = lambda shape: pl.BlockSpec(shape, lambda r, p, i: (0, 0))
    return pl.pallas_call(
        attend_kernel,
        out_shape=(jax.ShapeDtypeStruct((tokens, QW), BF), jax.ShapeDtypeStruct((TP, tok, QW), BF)),
        grid_spec=pltpu.PrefetchScalarGridSpec(
            num_scalar_prefetch=2,
            grid=(TP,),
            in_specs=[
                pl.BlockSpec((tok, QW), lambda r, p, i: (r, 0)),
                pl.BlockSpec((tok, 2 * HD), lambda r, p, i: (p[r], 0)),
                pl.BlockSpec((tok, 2 * HD), lambda r, p, i: (r, 0)),
                pl.BlockSpec((tok, 1), lambda r, p, i: (r, 0)),
                full((2 * HD, QW)),
                full((2 * HD, QW)),
            ],
            out_specs=(
                pl.BlockSpec((tok, QW), lambda r, p, i: (r, 0)),
                pl.BlockSpec((1, tok, QW), lambda r, p, i: (i[r], 0, 0)),
            ),
        ),
        cost_estimate=cost(4 * tokens * 2 * tok * QW * GROUP, 4 * tokens * QW),
        compiler_params=BIG,
        name="attend",
    )(prev_at, index, q, kv9, kv9, lo_col, ek, ev)


def attend_back_kernel(here_at, prev_at, q_ref, do_ref, prev_ref, here_ref, lo_ref, cos, sin, ek, ev, dq_ref, dkv_ref, carry):
    step = pl.program_id(0)
    tok = q_ref.shape[0]

    @pl.when(step == 0)
    def _():
        carry[...] = jnp.zeros_like(carry)

    @pl.when(step < TP)
    def _():
        two = jnp.concatenate([prev_ref[...], here_ref[...]], axis=0)
        keys = jnp.dot(two, ek[...], preferred_element_type=F32).astype(BF)
        values = jnp.dot(two, ev[...], preferred_element_type=F32).astype(BF)
        q, d_o = q_ref[...], do_ref[0]
        key_at = lax.broadcasted_iota(jnp.int32, (2 * tok, tok), 0)
        row_at = lax.broadcasted_iota(jnp.int32, (2 * tok, tok), 1)
        allowed = (lo_ref[0] <= key_at) & (key_at <= row_at + tok)
        lane = lax.broadcasted_iota(jnp.int32, (tok, QW), 1)
        key_lane = lax.broadcasted_iota(jnp.int32, (2 * tok, QW), 1)
        d_q = jnp.zeros((tok, QW), F32)
        d_k = jnp.zeros((2 * tok, QW), F32)
        d_v = jnp.zeros((2 * tok, QW), F32)
        for h in range(GROUP):
            q_h = jnp.where((lane // HALF) % GROUP == h, q, jnp.zeros_like(q))
            do_h = jnp.where(lane // HD == h, d_o, jnp.zeros_like(d_o))
            k_h = jnp.where((key_lane // HALF) % GROUP == h, keys, jnp.zeros_like(keys))
            s = jnp.where(allowed, mm(keys, q_h, NT) * SCALE, -1e30)
            expo = jnp.exp(s - jnp.max(s, axis=0, keepdims=True))
            probs = expo / jnp.sum(expo, axis=0, keepdims=True)
            d_p = mm(values, do_h, NT)
            shift = jnp.sum(d_p * probs, axis=0, keepdims=True)
            d_s = (probs * (d_p - shift)).astype(BF)
            d_v += mm(probs.astype(BF), do_h, NN)
            d_k += mm(d_s, q_h, NN)
            d_q += mm(d_s, k_h, TN)
        d_q = d_q * SCALE
        a, b = d_q[:, : QW // 2], d_q[:, QW // 2 :]
        c, s = cos[...], sin[...]
        dq_ref[:, : QW // 2] = (a * c + b * s).astype(BF)
        dq_ref[:, QW // 2 :] = (b * c - a * s).astype(BF)
        d_k = d_k * SCALE

        def fold(v):
            v = v + pltpu.roll(v, HD, 1)
            return v + pltpu.roll(v, HALF, 1)

        first, second = fold(d_k[:, : QW // 2]), fold(d_k[:, QW // 2 :])
        whole = d_v[:, : QW // 2] + d_v[:, QW // 2 :]
        whole = whole + pltpu.roll(whole, HD, 1)
        low = lax.broadcasted_iota(jnp.int32, (2 * tok, 2 * HD), 1)
        d_kv = jnp.where(low < HALF, first, jnp.where(low < HD, second, whole))
        dkv_ref[...] = carry[...] + d_kv[:tok]
        carry[...] = d_kv[tok:]

    @pl.when(step == TP)
    def _():
        dkv_ref[...] = carry[...]


def attend_back(here_at, prev_at, q, d_o, kv9, lo_row, cos, sin, ek, ev):
    tokens = q.shape[0]
    tok = tokens // TP
    last = TP - 1
    here = lambda cols: pl.BlockSpec((tok, cols), lambda s, h, p: (h[jnp.minimum(s, last)], 0))
    full = lambda shape: pl.BlockSpec(shape, lambda s, h, p: (0, 0))
    return pl.pallas_call(
        attend_back_kernel,
        out_shape=(
            jax.ShapeDtypeStruct((tokens, QW), BF),
            jax.ShapeDtypeStruct((tokens + tok, 2 * HD), F32),
        ),
        grid_spec=pltpu.PrefetchScalarGridSpec(
            num_scalar_prefetch=2,
            grid=(TP + 1,),
            in_specs=[
                here(QW),
                pl.BlockSpec((1, tok, QW), lambda s, h, p: (jnp.minimum(s, last), 0, 0)),
                pl.BlockSpec((tok, 2 * HD), lambda s, h, p: (p[jnp.minimum(s, last)], 0)),
                here(2 * HD),
                pl.BlockSpec((1, 1, tok), lambda s, h, p: (h[jnp.minimum(s, last)], 0, 0)),
                here(2 * HD),
                here(2 * HD),
                full((2 * HD, QW)),
                full((2 * HD, QW)),
            ],
            out_specs=(
                here(QW),
                pl.BlockSpec((tok, 2 * HD), lambda s, h, p: (jnp.where(s == 0, TP, h[jnp.maximum(s - 1, 0)]), 0)),
            ),
            scratch_shapes=[pltpu.VMEM((tok, 2 * HD), F32)],
        ),
        cost_estimate=cost(10 * tokens * 2 * tok * QW * GROUP, 8 * tokens * QW),
        compiler_params=BIG,
        name="attend_back",
    )(here_at, prev_at, q, d_o, kv9, kv9, lo_row, cos, sin, ek, ev)


def ffn_kernel(count, *refs):
    n2_blocks, dy_blocks = refs[:count], refs[count : 2 * count]
    w, act_out, dgu_out, grad_out, n2, dy, flat, held, n2_sems, dy_sems, out_sems = refs[2 * count :]
    start_rows(n2_blocks, n2, n2_sems)
    start_rows(dy_blocks, dy, dy_sems, dy.shape[0] // TP)
    each = n2.shape[0] // TP
    width = act_out.shape[1]
    two = 2 * width

    def forward(r, carry):
        at = pl.ds(pl.multiple_of(r * each, each), each)
        wait_rows(r, n2, n2_sems)
        wait_rows(r, dy, dy_sems)
        gate_up = jnp.dot(n2[at, :], w[:, :two], preferred_element_type=F32)
        d_act = jnp.dot(dy[at, :], w[:, two:], preferred_element_type=F32)
        g, u = gate_up[:, :width], gate_up[:, width:]
        sg = jax.nn.sigmoid(g)
        gs = g * sg
        act = (gs * u).astype(BF)
        d_g = (d_act * u * (sg * (1.0 + g * (1.0 - sg)))).astype(BF)
        d_u = (d_act * gs).astype(BF)
        act_out[at, :] = act
        dgu_out[at, :width] = d_g
        dgu_out[at, width:] = d_u
        flat[:width, at] = d_g.T
        flat[width:two, at] = d_u.T
        flat[two:, at] = act.T
        return carry

    lax.fori_loop(0, TP, forward, 0)
    planes, _, cols = grad_out.shape

    def leave(z):
        return pltpu.make_async_copy(held.at[lax.rem(z, 2)], grad_out.at[z], out_sems.at[lax.rem(z, 2)])

    def back(z, carry):
        at = pl.ds(pl.multiple_of(z * cols, cols), cols)
        slot = lax.rem(z, 2)

        @pl.when(z >= 2)
        def _():
            leave(z - 2).wait()

        held[slot, :two, :] = jnp.dot(flat[:two, :], n2[:, at], preferred_element_type=F32).astype(BF)
        held[slot, two:, :] = jnp.dot(flat[two:, :], dy[:, at], preferred_element_type=F32).astype(BF)
        leave(z).start()
        return carry

    lax.fori_loop(0, planes, back, 0)
    leave(planes - 2).wait()
    leave(planes - 1).wait()


def ffn_chunk(n2_blocks, dy_blocks, w):
    tokens = TP * n2_blocks[0].shape[0]
    planes = lax.axis_size("z")
    width = w.shape[1] // 3
    return pl.pallas_call(
        functools.partial(ffn_kernel, len(n2_blocks)),
        out_shape=(
            jax.ShapeDtypeStruct((tokens, width), BF),
            jax.ShapeDtypeStruct((tokens, 2 * width), BF),
            jax.ShapeDtypeStruct((planes, 3 * width, D // planes), BF),
        ),
        in_specs=[ANY] * (2 * len(n2_blocks)) + [VMEM],
        out_specs=(VMEM, VMEM, ANY),
        scratch_shapes=[
            pltpu.VMEM((tokens, D), BF),
            pltpu.VMEM((tokens, D), BF),
            pltpu.VMEM((3 * width, tokens), BF),
            pltpu.VMEM((2, 3 * width, D // planes), BF),
            pltpu.SemaphoreType.DMA((TP,)),
            pltpu.SemaphoreType.DMA((TP,)),
            pltpu.SemaphoreType.DMA((2,)),
        ],
        cost_estimate=cost(18 * tokens * D * width, 4 * tokens * D + 12 * width * D),
        compiler_params=BIG,
        name="ffn_chunk",
    )(*n2_blocks, *dy_blocks, w)


def down_kernel(parts, *refs):
    outs = refs[-2:]
    base = refs[2 * parts : -2]
    for at, out in enumerate(outs):
        term = base[at][0] if base else None
        for j in range(parts):
            more = mm(refs[j][0, at], refs[parts + j][...], NT)
            term = more if term is None else term + more
        out[0] = term.astype(out.dtype)


def down(parts, weights, last, groups, base=None, kind=BF):
    count = len(parts)
    tokens = parts[0].shape[0]
    tok = tokens // TP
    widths = [p.shape[1] for p in parts]
    columns = [w.shape[1] // width - 1 if last else 0 for w, width in zip(weights, widths)]
    pairs = [p.reshape(TP // 2, 2, tok, width) for p, width in zip(parts, widths)]
    rows = weights[0].shape[0]
    first, step = groups[0], groups[1] - groups[0]
    return pl.pallas_call(
        functools.partial(down_kernel, count),
        out_shape=[jax.ShapeDtypeStruct((len(groups), tok, rows), kind)] * 2,
        grid=(len(groups),),
        in_specs=[pl.BlockSpec((1, 2, tok, width), lambda s: (first + step * s, 0, 0, 0)) for width in widths]
        + [
            pl.BlockSpec((rows, width), lambda s, c=c: (0, c), pipeline_mode=pl.Buffered(1))
            for width, c in zip(widths, columns)
        ]
        + ([] if base is None else [pl.BlockSpec((1, tok, rows), lambda s: (first + step * s, 0, 0))] * 2),
        out_specs=[pl.BlockSpec((1, tok, rows), lambda s: (s, 0, 0))] * 2,
        cost_estimate=cost(4 * len(groups) * tok * sum(widths) * rows, rows * sum(widths) * 2 + len(groups) * tok * rows * 8),
        compiler_params=BIG,
        name="down",
    )(*pairs, *weights, *(() if base is None else base))


def start_wo(blocks, dst, sems):
    for r, ref in enumerate(blocks):
        pltpu.make_async_copy(ref, dst.at[r], sems.at[r]).start()


def wait_wo(r, dst, sems):
    pltpu.make_async_copy(dst.at[r], dst.at[r], sems.at[r]).wait()


def close_kernel(*refs):
    wo_blocks = refs[:TP]
    index, heads, x, gain, resid_out, n2_out, wo, sems = refs[TP:]
    start_wo(wo_blocks, wo, sems)
    y = x[...].astype(F32)
    for r in range(TP):
        wait_wo(r, wo, sems)
        y += mm(heads[index[r]], wo[r], NT)
    resid_out[...] = y
    n2_out[...] = (y * lax.rsqrt(jnp.mean(y * y, axis=-1, keepdims=True) + NORM_EPS) * gain[...]).astype(BF)


def close_attention(wo_blocks, index, heads, x, gain):
    tok = x.shape[0]
    return pl.pallas_call(
        close_kernel,
        out_shape=(jax.ShapeDtypeStruct((tok, D), F32), jax.ShapeDtypeStruct((tok, D), BF)),
        in_specs=[ANY] * TP + [SMEM] + [VMEM] * 3,
        out_specs=(VMEM, VMEM),
        scratch_shapes=[pltpu.VMEM((TP, D, QW), BF), pltpu.SemaphoreType.DMA((TP,))],
        cost_estimate=cost(2 * tok * D * D, 2 * D * D),
        compiler_params=BIG,
        name="close_attention",
    )(*wo_blocks, index, heads, x, gain)


def open_kernel(*refs):
    wo_blocks = refs[:TP]
    index, own, from_x, from_y, resid, dy, gain, back_out, att_out, heads, wo, sems = refs[TP:]
    start_wo(wo_blocks, wo, sems)
    d_n = own[...].astype(F32) + from_x[...].astype(F32) + from_y[...].astype(F32)
    y = resid[...]
    scale = lax.rsqrt(jnp.mean(y * y, axis=-1, keepdims=True) + NORM_EPS)
    unit = y * scale
    d_unit = d_n * gain[...]
    d_y = dy[...].astype(F32) + scale * (d_unit - unit * jnp.mean(d_unit * unit, axis=-1, keepdims=True))
    back_out[...] = d_y
    att_out[...] = d_y.astype(BF)
    att = att_out[...]
    for r in range(TP):
        wait_wo(r, wo, sems)
        heads[index[r]] = jnp.dot(att, wo[r], preferred_element_type=F32).astype(BF)


def open_attention(wo_blocks, index, terms, resid, dy, gain):
    tok = dy.shape[0]
    return pl.pallas_call(
        open_kernel,
        out_shape=(
            jax.ShapeDtypeStruct((tok, D), F32),
            jax.ShapeDtypeStruct((tok, D), BF),
            jax.ShapeDtypeStruct((TP, tok, QW), BF),
        ),
        in_specs=[ANY] * TP + [SMEM] + [VMEM] * 6,
        out_specs=(VMEM, VMEM, VMEM),
        scratch_shapes=[pltpu.VMEM((TP, D, QW), BF), pltpu.SemaphoreType.DMA((TP,))],
        cost_estimate=cost(2 * tok * D * D, 2 * D * D),
        compiler_params=BIG,
        name="open_attention",
    )(*wo_blocks, index, *terms, resid, dy, gain)


def turn_grad_kernel(count, *refs):
    blocks, left, out, rows, sems = refs[:count], *refs[count:]
    start_rows(blocks, rows, sems)
    for r in range(TP):
        wait_rows(r, rows, sems)
    planes, _, cols = out.shape

    def back(z, carry):
        at = pl.ds(pl.multiple_of(z * cols, cols), cols)
        out[z] = mm(left[...], rows[:, at], TN).astype(BF)
        return carry

    lax.fori_loop(0, planes, back, 0)


def turn_grad(left, blocks):
    tokens, cols = left.shape
    planes = lax.axis_size("z")
    return pl.pallas_call(
        functools.partial(turn_grad_kernel, len(blocks)),
        out_shape=jax.ShapeDtypeStruct((planes, cols, D // planes), BF),
        in_specs=[ANY] * len(blocks) + [VMEM],
        out_specs=VMEM,
        scratch_shapes=[pltpu.VMEM((tokens, D), BF), pltpu.SemaphoreType.DMA((TP,))],
        cost_estimate=cost(2 * tokens * D * cols, 2 * tokens * D),
        compiler_params=BIG,
        name="turn_grad",
    )(*blocks, left)


def after(value, *first):
    return lax.optimization_barrier((value, *first))[0]


def rms_norm(values, scales):
    return values * lax.rsqrt(jnp.mean(values * values, axis=-1, keepdims=True) + NORM_EPS) * scales


def to_pieces(pieces):
    rows, cols = pieces.shape[1:]
    return trade(pieces).reshape(TP * rows, cols)


def sum_z(grad):
    planes, cols, wide = grad.shape
    return lax.psum_scatter(grad.reshape(planes * cols, wide), "z", scatter_dimension=0, tiled=True)


def give_back(summed):
    return trade(turn(summed))


def by_plane(grad):
    planes = lax.axis_size("z")
    return grad.reshape(grad.shape[0], planes, D // planes).transpose(1, 0, 2)


def pick(blocks, at):
    return lax.dynamic_index_in_dim(blocks, at, 0, keepdims=False)


def on_device(hidden_in, segment_ids, w_attn, w_ffn, gains, out_grad):
    tok = hidden_in.shape[0]
    rows = w_attn.shape[0]
    me = lax.axis_index(PLANE)
    z = lax.axis_index("z")
    tokens = TP * tok
    steps = jnp.arange(TP, dtype=jnp.int32)
    rel = me ^ steps
    perm = fold_order()
    ek, ev = spread_kv()

    own_start = (z * TP + me) * tok
    own_lo = segment_ids - own_start + tok
    extra = jnp.zeros((EXTRA, AW), BF)
    extra = extra.at[0, : 2 * rows].set(gains.reshape(-1))
    extra = extra.at[1, :tok].set((own_lo // 2).astype(BF)).at[2, :tok].set((own_lo % 2).astype(BF))

    attn_pieces = cut_attn(w_attn, perm)
    attn_pieces = jnp.concatenate([attn_pieces, jnp.broadcast_to(extra, (TP, *extra.shape))], axis=1)
    attn_rows = to_pieces(attn_pieces)
    both_begun = gather_begin(jnp.concatenate([hidden_in, out_grad], axis=0))
    pieces = cut_ffn(w_ffn)
    rows_0 = to_pieces(after(pieces[0], *both_begun[1:]))
    w_0 = gather_z(rows_0)
    both_blocks = gather_end(*both_begun)
    attn_all = after(gather_z(attn_rows), rows_0).reshape(-1, rows + EXTRA, AW)
    w_own = attn_all[:, :rows].reshape(D, AW)
    wqkv, wo = w_own[:, : QW + 2 * HD], w_own[:, QW + 2 * HD :]
    gains_full = attn_all[:, rows, : 2 * rows].reshape(-1, 2, rows).transpose(1, 0, 2).reshape(2, D).astype(F32)

    plane_lo = attn_rows.reshape(TP, rows + EXTRA, -1)[:, rows + 1 : rows + 3, :tok].astype(jnp.int32)
    lo = jnp.take(2 * plane_lo[:, 0] + plane_lo[:, 1], rel, axis=0)
    positions = jnp.arange(tok, dtype=jnp.int32)[None] + tok - lo
    freqs = 1.0 / ROPE_BASE ** (jnp.arange(HALF, dtype=F32) * (2.0 / HD))
    angles = positions.reshape(tokens).astype(F32)[:, None] * freqs
    cosine = jnp.tile(jnp.cos(angles), (1, GROUP))
    sine = jnp.tile(jnp.sin(angles), (1, GROUP))

    n1, q, kv = norm_qkv(both_blocks, gains_full[:1], attn_all, cosine, sine)
    wo_begun = gather_begin(wo)
    q = after(q, *wo_begun[1:])
    rows_1 = to_pieces(after(pieces[1], n1))
    before = along_z(pick(kv.reshape(TP, tok, 2 * HD), me ^ (TP - 1)), 1)
    kv9 = jnp.concatenate([kv, before], axis=0)
    prev_at = jnp.where(rel == 0, TP, (rel - 1) ^ me)
    mixed, heads = attend(prev_at, rel, q, kv9, lo.reshape(tokens, 1), ek, ev)

    wo_blocks = gather_end(*wo_begun)
    heads = trade(after(heads, rows_1))
    w_1 = gather_z(rows_1)
    x_own = hidden_in.astype(F32)
    residual, normed_two = close_attention(wo_blocks, rel, heads, after(hidden_in, w_0), gains_full[1:])
    n2_blocks = gather_plane(normed_two)

    act_0, d_gu_0, grad_0 = ffn_chunk(n2_blocks, both_blocks, w_0)
    so_far = down([d_gu_0], [w_0], False, (0, 1, 2, 3), kind=F32)
    sum_0 = sum_z(grad_0)
    act_1, d_gu_1, grad_1 = ffn_chunk(n2_blocks, both_blocks, after(w_1, so_far[0]))
    sum_1 = sum_z(grad_1)
    d_n2_terms = scatter_plane(lambda groups: down([d_gu_1], [w_1], False, groups, so_far))
    d_resid, d_att, d_heads = open_attention(wo_blocks, rel, d_n2_terms, residual, out_grad, gains_full[1:])
    d_o = trade(d_heads)
    d_att_begun = gather_begin(after(d_att, d_o))

    here_at = me ^ steps
    prev_abs = jnp.where(steps == 0, TP, (steps - 1) ^ me)
    d_q, d_kv9 = attend_back(here_at, prev_abs, q, after(d_o, sum_0), kv9, lo.reshape(TP, 1, tok), cosine, sine, ek, ev)
    d_att_blocks = gather_end(after(d_att_begun[0], d_q), *d_att_begun[1:])
    wo_grad = turn_grad(mixed, d_att_blocks)
    back = along_z(d_kv9[tokens:].astype(BF), -1)
    last = me ^ (TP - 1)
    d_kv = d_kv9[:tokens].reshape(TP, tok, 2 * HD)
    d_kv = jnp.where((steps == last)[:, None, None], d_kv + back.astype(F32)[None], d_kv).reshape(tokens, 2 * HD)
    c, s = cosine[:, :HALF], sine[:, :HALF]
    a, b = d_kv[:, :HALF], d_kv[:, HALF:HD]
    d_qkv = jnp.concatenate(
        [d_q, (a * c + b * s).astype(BF), (b * c - a * s).astype(BF), d_kv[:, HD:].astype(BF)], axis=1
    )
    qkv_grad = by_plane(mm(d_qkv, n1, TN).astype(BF))
    attn_sum = jnp.concatenate([qkv_grad, wo_grad], axis=1)
    attn_back = give_back(sum_z(attn_sum))
    d_qkv = after(d_qkv, attn_sum)
    d_normed = total(*scatter_plane(lambda groups: down([d_qkv], [wqkv], False, groups)))
    acts = [after(act_0, attn_sum), act_1]
    f_terms = scatter_plane(lambda groups: down(acts, [w_0, w_1], True, groups))
    hidden_out = (residual + total(*f_terms)).astype(BF)
    ffn_back = [give_back(v) for v in (sum_0, sum_1)]
    scale = lax.rsqrt(jnp.mean(x_own * x_own, axis=-1, keepdims=True) + NORM_EPS)
    unit = x_own * scale
    d_unit = d_normed * gains_full[0]
    in_grad = d_resid + scale * (d_unit - unit * jnp.mean(d_unit * unit, axis=-1, keepdims=True))
    ffn_grad, term_two = paste_ffn(ffn_back, w_ffn)
    attn_grad, term_one = paste_attn(attn_back, w_attn, perm)
    gains_grad = jnp.concatenate([term_one, term_two], axis=1).T / gains.astype(F32)
    return hidden_out, in_grad.astype(BF), attn_grad, ffn_grad, gains_grad


def solution(mesh):
    fine = Mesh(mesh.devices.reshape(-1, 2, 2, 2), EVERY)
    rows = P(EVERY, None)
    in_specs = (rows, P(EVERY), rows, rows, P(None, EVERY), rows)
    out_specs = (rows, rows, rows, rows, P(None, EVERY))
    return jax.shard_map(
        on_device, mesh=fine, in_specs=in_specs, out_specs=out_specs, check_vma=False
    )
```

```python
import functools

import jax
import jax.numpy as jnp
from jax import lax
from jax.experimental import pallas as pl
from jax.experimental.pallas import tpu as pltpu
from jax.sharding import Mesh, PartitionSpec as P

D = 2048
H = 32
KV = 8
HD = 64
FF = 8192
GROUP = H // KV
TP = 8
WIDTHS = (512, 512)
CHUNKS = len(WIDTHS)
HALF = HD // 2
QW = GROUP * HD
STARTS = [TP * sum(WIDTHS[:k]) for k in range(CHUNKS)]
EXTRA = 8
AW = 2 * QW + 2 * HD

NORM_EPS = 1e-05
ROPE_BASE = 500000.0
SCALE = HD ** (-0.5)

PLANE = ("y", "x", "c")
EVERY = ("z", "y", "x", "c")
BF = jnp.bfloat16
F32 = jnp.float32
ANY = pl.BlockSpec(memory_space=pl.ANY)
VMEM = pl.BlockSpec(memory_space=pltpu.VMEM)
SMEM = pl.BlockSpec(memory_space=pltpu.SMEM)
BIG = pltpu.CompilerParams(vmem_limit_bytes=56 * 1024 * 1024)


def cost(flops, size):
    return pl.CostEstimate(flops=int(flops), bytes_accessed=int(size), transcendentals=0)


def mm(left, right, dims):
    return lax.dot_general(left, right, (dims, ((), ())), preferred_element_type=F32)


NN = ((1,), (0,))
NT = ((1,), (1,))
TN = ((0,), (0,))


def after(value, *first):
    return lax.optimization_barrier((value, *first))[0]


def rms_norm(values, scales):
    return values * lax.rsqrt(jnp.mean(values * values, axis=-1, keepdims=True) + NORM_EPS) * scales


def swap(value, rel):
    return lax.ppermute(value, PLANE, [(i, i ^ rel) for i in range(TP)])


def swap_across(value):
    return lax.ppermute(value, PLANE, [(i, i ^ (2 + 2 * (i % 2))) for i in range(TP)])


def on_first():
    return lax.axis_index(PLANE) % 2 == 0


def gather_begin(own):
    return own, swap(own, 2), swap(own, 4), swap(own, 1)


def gather_end(own, from_x, from_y, from_c):
    across = swap_across(jnp.where(on_first(), from_y, from_x))
    return [own, from_c, from_x, swap(from_x, 1), from_y, swap(from_y, 1), across, swap(across, 1)]


def gather_plane(own):
    return gather_end(*gather_begin(own))


def add(left, right):
    return (left.astype(F32) + right.astype(F32)).astype(BF)


def scatter_plane(part, wait=()):
    even, odd = part((3, 2))
    both = add(even, swap(odd, 1))
    across, over_y = swap_across(both[0]), both[1]
    even, odd = part((1, 0))
    both = add(even, swap(odd, 1))
    over_x, own = both[0], both[1]
    across = after(across, *wait)
    first = on_first()
    over_x = jnp.where(first, over_x, add(over_x, across))
    over_y = jnp.where(first, add(over_y, across), over_y)
    return (own, swap(over_x, 2), swap(over_y, 4)), (over_x, over_y)


def total(own, from_x, from_y):
    return own.astype(F32) + from_x.astype(F32) + from_y.astype(F32)


def trade(blocks):
    return lax.all_to_all(blocks, PLANE, 0, 0, tiled=True)


def along_z(value, steps):
    count = lax.axis_size("z")
    return lax.ppermute(
        value, "z", [(i, i + steps) for i in range(count) if 0 <= i + steps < count]
    )


def gather_z(own):
    return lax.all_gather(own, "z", axis=0, tiled=True)


def start_rows(refs, dst, sems):
    each = dst.shape[0] // len(refs)
    for r, ref in enumerate(refs):
        pltpu.make_async_copy(ref, dst.at[pl.ds(r * each, each)], sems.at[r]).start()


def wait_rows(r, dst, sems, count=TP):
    each = dst.shape[0] // count
    part = dst.at[pl.ds(pl.multiple_of(r * each, each), each)]
    pltpu.make_async_copy(part, part, sems.at[r]).wait()


def fold_order():
    old = jnp.arange(QW, dtype=jnp.int32)
    new = (old // HALF) % 2 * (GROUP * HALF) + old // HD * HALF + old % HALF
    return (new[:, None] == jnp.arange(QW, dtype=jnp.int32)[None, :]).astype(BF)


def cut_attn_kernel(w_ref, perm_ref, out):
    kv_cols = KV * HD
    for i in range(TP):
        q = jnp.dot(w_ref[:, QW * i : QW * (i + 1)], perm_ref[...], preferred_element_type=F32)
        out[i, :, :QW] = q.astype(BF)
        k = w_ref[:, D + HD * i : D + HD * (i + 1)]
        v = w_ref[:, D + kv_cols + HD * i : D + kv_cols + HD * (i + 1)]
        out[i, :, QW : QW + 2 * HD] = jnp.concatenate([k, v], axis=1)
        out[i, :, QW + 2 * HD :] = w_ref[:, D + 2 * kv_cols + QW * i : D + 2 * kv_cols + QW * (i + 1)]


def cut_attn(w_attn, perm):
    rows = w_attn.shape[0]
    return pl.pallas_call(
        cut_attn_kernel,
        out_shape=jax.ShapeDtypeStruct((TP, rows, AW), BF),
        in_specs=[VMEM, VMEM],
        out_specs=VMEM,
        cost_estimate=cost(0, 2 * w_attn.size * 2),
        name="cut_attn",
    )(w_attn, perm)


def cut_ffn_kernel(w_ref, *outs):
    for k, width in enumerate(WIDTHS):
        for i in range(TP):
            for n in range(3):
                at = n * FF + STARTS[k] + i * width
                outs[k][i, :, n * width : (n + 1) * width] = w_ref[:, at : at + width]


def cut_ffn(w_ffn):
    rows = w_ffn.shape[0]
    return pl.pallas_call(
        cut_ffn_kernel,
        out_shape=[jax.ShapeDtypeStruct((TP, rows, 3 * width), BF) for width in WIDTHS],
        in_specs=[VMEM],
        out_specs=[VMEM] * CHUNKS,
        cost_estimate=cost(0, 2 * w_ffn.size * 2),
        compiler_params=BIG,
        name="cut_ffn",
    )(w_ffn)


def paste_ffn_kernel(*refs):
    pieces, w, out, term = refs[:CHUNKS], *refs[CHUNKS:]
    each = min(WIDTHS)
    total = jnp.zeros((w.shape[0], each), F32)
    for k, width in enumerate(WIDTHS):
        for i in range(TP):
            for n in range(3):
                for part in range(0, width, each):
                    at = n * FF + STARTS[k] + i * width + part
                    grad = pieces[k][i, :, n * width + part : n * width + part + each].astype(F32)
                    out[:, at : at + each] = grad
                    if n < 2:
                        total += grad * w[:, at : at + each].astype(F32)
    term[...] = jnp.sum(total, axis=-1, keepdims=True)


def paste_ffn(pieces, w_ffn):
    rows = w_ffn.shape[0]
    return pl.pallas_call(
        paste_ffn_kernel,
        out_shape=(jax.ShapeDtypeStruct(w_ffn.shape, F32), jax.ShapeDtypeStruct((rows, 1), F32)),
        in_specs=[VMEM] * (CHUNKS + 1),
        out_specs=(VMEM, VMEM),
        cost_estimate=cost(0, 8 * w_ffn.size),
        compiler_params=BIG,
        name="paste_ffn",
    )(*pieces, w_ffn)


def paste_attn_kernel(piece, w, perm, out, term):
    kv_cols = KV * HD
    ones = jnp.zeros((w.shape[0], QW), F32)
    small = jnp.zeros((w.shape[0], HD), F32)
    for i in range(TP):
        q = mm(piece[i, :, :QW], perm[...], NT)
        out[:, QW * i : QW * (i + 1)] = q
        ones += q * w[:, QW * i : QW * (i + 1)].astype(F32)
        kv = piece[i, :, QW : QW + 2 * HD].astype(F32)
        for at, part in ((D + HD * i, kv[:, :HD]), (D + kv_cols + HD * i, kv[:, HD:])):
            out[:, at : at + HD] = part
            small += part * w[:, at : at + HD].astype(F32)
        at = D + 2 * kv_cols + QW * i
        out[:, at : at + QW] = piece[i, :, QW + 2 * HD :].astype(F32)
    term[...] = jnp.sum(ones, axis=-1, keepdims=True) + jnp.sum(small, axis=-1, keepdims=True)


def paste_attn(piece, w_attn, perm):
    rows = w_attn.shape[0]
    return pl.pallas_call(
        paste_attn_kernel,
        out_shape=(jax.ShapeDtypeStruct(w_attn.shape, F32), jax.ShapeDtypeStruct((rows, 1), F32)),
        in_specs=[VMEM] * 3,
        out_specs=(VMEM, VMEM),
        cost_estimate=cost(0, 8 * w_attn.size),
        compiler_params=BIG,
        name="paste_attn",
    )(piece, w_attn, perm)


def turn_kernel(x, out):
    rows = out.shape[1]
    turned = x[...].astype(F32).T.astype(BF)
    for i in range(TP):
        out[i] = turned[rows * i : rows * (i + 1)]


def turn(x):
    cols, wide = x.shape
    return pl.pallas_call(
        turn_kernel,
        out_shape=jax.ShapeDtypeStruct((TP, wide // TP, cols), BF),
        in_specs=[VMEM],
        out_specs=VMEM,
        cost_estimate=cost(0, 4 * x.size),
        compiler_params=BIG,
        name="turn",
    )(x)


def qkv_kernel(count, *refs):
    blocks = refs[:count]
    gain, w_all, cos, sin, n1, q_out, kv_out, x_s, w_s, sems, w_sem = refs[count:]
    w_copy = pltpu.make_async_copy(w_all.at[:, pl.ds(0, w_s.shape[1]), pl.ds(0, w_s.shape[2])], w_s, w_sem)
    w_copy.start()
    start_rows(blocks, x_s, sems)
    each = x_s.shape[0] // count
    lane = lax.broadcasted_iota(jnp.int32, (each, 2 * HD), 1)
    w_copy.wait()

    def step(r, carry):
        at = pl.ds(pl.multiple_of(r * each, each), each)
        wait_rows(r, x_s, sems, count)
        x = x_s[at, :].astype(F32)
        scale = lax.rsqrt(jnp.mean(x * x, axis=-1, keepdims=True) + NORM_EPS)
        normed = (x * scale * gain[...]).astype(BF)
        n1[at, :] = normed
        qkv = jnp.dot(normed, w_s[...].reshape(D, QW + 2 * HD), preferred_element_type=F32)
        c, s = cos[at, :], sin[at, :]
        a, b = qkv[:, : QW // 2], qkv[:, QW // 2 : QW]
        q_out[at, : QW // 2] = (a * c - b * s).astype(BF)
        q_out[at, QW // 2 :] = (b * c + a * s).astype(BF)
        kv = qkv[:, QW:]
        ahead = pltpu.roll(kv, 2 * HD - HALF, 1)
        behind = pltpu.roll(kv, HALF, 1)
        turned = kv * c + jnp.where(lane < HALF, -ahead, behind) * s
        kv_out[at, :] = jnp.where(lane < HD, turned, kv).astype(BF)
        return carry

    lax.fori_loop(0, count, step, 0)


def norm_qkv(blocks, gain, w_all, cos, sin):
    each = w_all.shape[1] - EXTRA
    tokens = cos.shape[0]
    return pl.pallas_call(
        functools.partial(qkv_kernel, len(blocks)),
        out_shape=(
            jax.ShapeDtypeStruct((tokens, D), BF),
            jax.ShapeDtypeStruct((tokens, QW), BF),
            jax.ShapeDtypeStruct((tokens, 2 * HD), BF),
        ),
        in_specs=[ANY] * len(blocks) + [VMEM, ANY, VMEM, VMEM],
        out_specs=(VMEM, VMEM, VMEM),
        scratch_shapes=[
            pltpu.VMEM((tokens, D), BF),
            pltpu.VMEM((w_all.shape[0], each, QW + 2 * HD), BF),
            pltpu.SemaphoreType.DMA((len(blocks),)),
            pltpu.SemaphoreType.DMA,
        ],
        cost_estimate=cost(2 * tokens * D * (QW + 2 * HD), 4 * tokens * D),
        compiler_params=BIG,
        name="norm_qkv",
    )(*blocks, gain, w_all, cos, sin)


def spread_kv():
    src = jnp.arange(2 * HD, dtype=jnp.int32)[:, None]
    col = jnp.arange(QW, dtype=jnp.int32)[None, :]
    key = (src == col // (GROUP * HALF) * HALF + col % HALF).astype(BF)
    value = (src == HD + col % HD).astype(BF)
    return key, value


def attend_kernel(prev_at, index, q_ref, prev_ref, here_ref, lo_ref, ek, ev, o_ref, o_index_ref):
    tok = q_ref.shape[0]
    two = jnp.concatenate([prev_ref[...], here_ref[...]], axis=0)
    keys = jnp.dot(two, ek[...], preferred_element_type=F32).astype(BF)
    values = jnp.dot(two, ev[...], preferred_element_type=F32).astype(BF)
    q = q_ref[...]
    key_at = lax.broadcasted_iota(jnp.int32, (tok, 2 * tok), 1)
    row_at = lax.broadcasted_iota(jnp.int32, (tok, 2 * tok), 0)
    allowed = (lo_ref[...] <= key_at) & (key_at <= row_at + tok)
    q_lane = lax.broadcasted_iota(jnp.int32, (tok, QW), 1)
    v_lane = lax.broadcasted_iota(jnp.int32, (2 * tok, QW), 1)
    total = jnp.zeros((tok, QW), F32)
    for h in range(GROUP):
        mine = jnp.where((q_lane // HALF) % GROUP == h, q, jnp.zeros_like(q))
        s = jnp.where(allowed, mm(mine, keys, NT) * SCALE, -1e30)
        expo = jnp.exp(s - jnp.max(s, axis=-1, keepdims=True))
        probs = (expo / jnp.sum(expo, axis=-1, keepdims=True)).astype(BF)
        total += mm(probs, jnp.where(v_lane // HD == h, values, jnp.zeros_like(values)), NN)
    o_ref[...] = total.astype(BF)
    o_index_ref[0] = o_ref[...]


def attend(prev_at, index, q, kv9, lo_col, ek, ev):
    tokens = q.shape[0]
    tok = tokens // TP
    full = lambda shape: pl.BlockSpec(shape, lambda r, p, i: (0, 0))
    return pl.pallas_call(
        attend_kernel,
        out_shape=(jax.ShapeDtypeStruct((tokens, QW), BF), jax.ShapeDtypeStruct((TP, tok, QW), BF)),
        grid_spec=pltpu.PrefetchScalarGridSpec(
            num_scalar_prefetch=2,
            grid=(TP,),
            in_specs=[
                pl.BlockSpec((tok, QW), lambda r, p, i: (r, 0)),
                pl.BlockSpec((tok, 2 * HD), lambda r, p, i: (p[r], 0)),
                pl.BlockSpec((tok, 2 * HD), lambda r, p, i: (r, 0)),
                pl.BlockSpec((tok, 1), lambda r, p, i: (r, 0)),
                full((2 * HD, QW)),
                full((2 * HD, QW)),
            ],
            out_specs=(
                pl.BlockSpec((tok, QW), lambda r, p, i: (r, 0)),
                pl.BlockSpec((1, tok, QW), lambda r, p, i: (i[r], 0, 0)),
            ),
        ),
        cost_estimate=cost(4 * tokens * 2 * tok * QW * GROUP, 4 * tokens * QW),
        compiler_params=BIG,
        name="attend",
    )(prev_at, index, q, kv9, kv9, lo_col, ek, ev)


def attend_back_kernel(here_at, prev_at, q_ref, do_ref, prev_ref, here_ref, lo_ref, cos, sin, ek, ev, dq_ref, dkv_ref, carry):
    step = pl.program_id(0)
    tok = q_ref.shape[0]

    @pl.when(step == 0)
    def _():
        carry[...] = jnp.zeros_like(carry)

    @pl.when(step < TP)
    def _():
        two = jnp.concatenate([prev_ref[...], here_ref[...]], axis=0)
        keys = jnp.dot(two, ek[...], preferred_element_type=F32).astype(BF)
        values = jnp.dot(two, ev[...], preferred_element_type=F32).astype(BF)
        q, d_o = q_ref[...], do_ref[0]
        key_at = lax.broadcasted_iota(jnp.int32, (2 * tok, tok), 0)
        row_at = lax.broadcasted_iota(jnp.int32, (2 * tok, tok), 1)
        allowed = (lo_ref[0] <= key_at) & (key_at <= row_at + tok)
        lane = lax.broadcasted_iota(jnp.int32, (tok, QW), 1)
        key_lane = lax.broadcasted_iota(jnp.int32, (2 * tok, QW), 1)
        d_q = jnp.zeros((tok, QW), F32)
        d_k = jnp.zeros((2 * tok, QW), F32)
        d_v = jnp.zeros((2 * tok, QW), F32)
        for h in range(GROUP):
            q_h = jnp.where((lane // HALF) % GROUP == h, q, jnp.zeros_like(q))
            do_h = jnp.where(lane // HD == h, d_o, jnp.zeros_like(d_o))
            k_h = jnp.where((key_lane // HALF) % GROUP == h, keys, jnp.zeros_like(keys))
            s = jnp.where(allowed, mm(keys, q_h, NT) * SCALE, -1e30)
            expo = jnp.exp(s - jnp.max(s, axis=0, keepdims=True))
            probs = expo / jnp.sum(expo, axis=0, keepdims=True)
            d_p = mm(values, do_h, NT)
            shift = jnp.sum(d_p * probs, axis=0, keepdims=True)
            d_s = (probs * (d_p - shift)).astype(BF)
            d_v += mm(probs.astype(BF), do_h, NN)
            d_k += mm(d_s, q_h, NN)
            d_q += mm(d_s, k_h, TN)
        d_q = d_q * SCALE
        a, b = d_q[:, : QW // 2], d_q[:, QW // 2 :]
        c, s = cos[...], sin[...]
        dq_ref[:, : QW // 2] = (a * c + b * s).astype(BF)
        dq_ref[:, QW // 2 :] = (b * c - a * s).astype(BF)
        d_k = d_k * SCALE

        def fold(v):
            v = v + pltpu.roll(v, HD, 1)
            return v + pltpu.roll(v, HALF, 1)

        first, second = fold(d_k[:, : QW // 2]), fold(d_k[:, QW // 2 :])
        whole = d_v[:, : QW // 2] + d_v[:, QW // 2 :]
        whole = whole + pltpu.roll(whole, HD, 1)
        low = lax.broadcasted_iota(jnp.int32, (2 * tok, 2 * HD), 1)
        d_kv = jnp.where(low < HALF, first, jnp.where(low < HD, second, whole))
        dkv_ref[...] = carry[...] + d_kv[:tok]
        carry[...] = d_kv[tok:]

    @pl.when(step == TP)
    def _():
        dkv_ref[...] = carry[...]


def attend_back(here_at, prev_at, q, d_o, kv9, lo_row, cos, sin, ek, ev):
    tokens = q.shape[0]
    tok = tokens // TP
    last = TP - 1
    here = lambda cols: pl.BlockSpec((tok, cols), lambda s, h, p: (h[jnp.minimum(s, last)], 0))
    full = lambda shape: pl.BlockSpec(shape, lambda s, h, p: (0, 0))
    return pl.pallas_call(
        attend_back_kernel,
        out_shape=(
            jax.ShapeDtypeStruct((tokens, QW), BF),
            jax.ShapeDtypeStruct((tokens + tok, 2 * HD), F32),
        ),
        grid_spec=pltpu.PrefetchScalarGridSpec(
            num_scalar_prefetch=2,
            grid=(TP + 1,),
            in_specs=[
                here(QW),
                pl.BlockSpec((1, tok, QW), lambda s, h, p: (jnp.minimum(s, last), 0, 0)),
                pl.BlockSpec((tok, 2 * HD), lambda s, h, p: (p[jnp.minimum(s, last)], 0)),
                here(2 * HD),
                pl.BlockSpec((1, 1, tok), lambda s, h, p: (h[jnp.minimum(s, last)], 0, 0)),
                here(2 * HD),
                here(2 * HD),
                full((2 * HD, QW)),
                full((2 * HD, QW)),
            ],
            out_specs=(
                here(QW),
                pl.BlockSpec((tok, 2 * HD), lambda s, h, p: (jnp.where(s == 0, TP, h[jnp.maximum(s - 1, 0)]), 0)),
            ),
            scratch_shapes=[pltpu.VMEM((tok, 2 * HD), F32)],
        ),
        cost_estimate=cost(10 * tokens * 2 * tok * QW * GROUP, 8 * tokens * QW),
        compiler_params=BIG,
        name="attend_back",
    )(here_at, prev_at, q, d_o, kv9, kv9, lo_row, cos, sin, ek, ev)


def ffn_forward(r, n2, dy, w, act_out, dgu_out, flat):
    each = n2.shape[0] // TP
    width = act_out.shape[1]
    two = 2 * width
    at = pl.ds(pl.multiple_of(r * each, each), each)
    gate_up = jnp.dot(n2[at, :], w[:, :two], preferred_element_type=F32)
    d_act = jnp.dot(dy[at, :], w[:, two:], preferred_element_type=F32)
    g, u = gate_up[:, :width], gate_up[:, width:]
    sg = jax.nn.sigmoid(g)
    gs = g * sg
    act = (gs * u).astype(BF)
    d_g = (d_act * u * (sg * (1.0 + g * (1.0 - sg)))).astype(BF)
    d_u = (d_act * gs).astype(BF)
    act_out[at, :] = act
    dgu_out[at, :width] = d_g
    dgu_out[at, width:] = d_u
    flat[:width, at] = d_g.T
    flat[width:two, at] = d_u.T
    flat[two:, at] = act.T


def ffn_back(flat, n2, dy, grad_out, held, out_sems):
    planes, wide, cols = grad_out.shape
    two = 2 * wide // 3

    def leave(z):
        return pltpu.make_async_copy(held.at[lax.rem(z, 2)], grad_out.at[z], out_sems.at[lax.rem(z, 2)])

    def back(z, carry):
        at = pl.ds(pl.multiple_of(z * cols, cols), cols)
        slot = lax.rem(z, 2)

        @pl.when(z >= 2)
        def _():
            leave(z - 2).wait()

        held[slot, :two, :] = jnp.dot(flat[:two, :], n2[:, at], preferred_element_type=F32).astype(BF)
        held[slot, two:, :] = jnp.dot(flat[two:, :], dy[:, at], preferred_element_type=F32).astype(BF)
        leave(z).start()
        return carry

    lax.fori_loop(0, planes, back, 0)
    leave(planes - 2).wait()
    leave(planes - 1).wait()


def ffn_kernel(*refs):
    n2_blocks, dy_blocks = refs[:TP], refs[TP : 2 * TP]
    w, act_out, dgu_out, grad_out, n2, dy, flat, held, n2_sems, dy_sems, out_sems = refs[2 * TP :]
    start_rows(n2_blocks, n2, n2_sems)
    start_rows(dy_blocks, dy, dy_sems)

    def forward(r, carry):
        wait_rows(r, n2, n2_sems)
        wait_rows(r, dy, dy_sems)
        ffn_forward(r, n2, dy, w, act_out, dgu_out, flat)
        return carry

    lax.fori_loop(0, TP, forward, 0)
    ffn_back(flat, n2, dy, grad_out, held, out_sems)


def ffn_forward_kernel(*refs):
    n2_blocks, dy_blocks = refs[:TP], refs[TP : 2 * TP]
    w, act_out, dgu_out, flat, n2, dy, n2_sems, dy_sems = refs[2 * TP :]
    start_rows(n2_blocks, n2, n2_sems)
    start_rows(dy_blocks, dy, dy_sems)

    def forward(r, carry):
        wait_rows(r, n2, n2_sems)
        wait_rows(r, dy, dy_sems)
        ffn_forward(r, n2, dy, w, act_out, dgu_out, flat)
        return carry

    lax.fori_loop(0, TP, forward, 0)


def ffn_back_kernel(*refs):
    n2_blocks, dy_blocks = refs[:TP], refs[TP : 2 * TP]
    flat, grad_out, n2, dy, held, n2_sems, dy_sems, out_sems = refs[2 * TP :]
    start_rows(n2_blocks, n2, n2_sems)
    start_rows(dy_blocks, dy, dy_sems)
    for r in range(TP):
        wait_rows(r, n2, n2_sems)
    for r in range(TP):
        wait_rows(r, dy, dy_sems)
    ffn_back(flat, n2, dy, grad_out, held, out_sems)


def ffn_call(kernel, n2_blocks, dy_blocks, last, outs, flops):
    tokens = TP * n2_blocks[0].shape[0]
    planes = lax.axis_size("z")
    wide = last.shape[1] if 2 not in outs or 0 in outs else last.shape[0]
    width = wide // 3
    shapes, specs, extra, sems = [], [], [], []
    if 0 in outs:
        shapes += [jax.ShapeDtypeStruct((tokens, width), BF), jax.ShapeDtypeStruct((tokens, 2 * width), BF)]
        specs += [VMEM, VMEM]
    if 1 in outs:
        shapes.append(jax.ShapeDtypeStruct((wide, tokens), BF))
        specs.append(VMEM)
    if 2 in outs:
        shapes.append(jax.ShapeDtypeStruct((planes, wide, D // planes), BF))
        specs.append(ANY)
        extra = ([pltpu.VMEM((wide, tokens), BF)] if 0 in outs else []) + [pltpu.VMEM((2, wide, D // planes), BF)]
        sems = [pltpu.SemaphoreType.DMA((2,))]
    return pl.pallas_call(
        kernel,
        out_shape=shapes,
        in_specs=[ANY] * (2 * TP) + [VMEM],
        out_specs=specs,
        scratch_shapes=[pltpu.VMEM((tokens, D), BF), pltpu.VMEM((tokens, D), BF)]
        + extra
        + [pltpu.SemaphoreType.DMA((TP,)), pltpu.SemaphoreType.DMA((TP,))]
        + sems,
        cost_estimate=cost(flops * tokens * D * width, 4 * tokens * D + 12 * width * D),
        compiler_params=BIG,
        name="ffn",
    )(*n2_blocks, *dy_blocks, last)


def down_kernel(parts, *refs):
    outs = refs[-2:]
    base = refs[2 * parts : -2]
    for at, out in enumerate(outs):
        term = base[at][0] if base else None
        for j in range(parts):
            more = mm(refs[j][0, at], refs[parts + j][...], NT)
            term = more if term is None else term + more
        out[0] = term.astype(out.dtype)


def down(parts, weights, last, groups, base=None, kind=BF):
    count = len(parts)
    tokens = parts[0].shape[0]
    tok = tokens // TP
    widths = [p.shape[1] for p in parts]
    columns = [w.shape[1] // width - 1 if last else 0 for w, width in zip(weights, widths)]
    pairs = [p.reshape(TP // 2, 2, tok, width) for p, width in zip(parts, widths)]
    rows = weights[0].shape[0]
    first, step = groups[0], groups[1] - groups[0]
    return pl.pallas_call(
        functools.partial(down_kernel, count),
        out_shape=[jax.ShapeDtypeStruct((len(groups), tok, rows), kind)] * 2,
        grid=(len(groups),),
        in_specs=[pl.BlockSpec((1, 2, tok, width), lambda s: (first + step * s, 0, 0, 0)) for width in widths]
        + [
            pl.BlockSpec((rows, width), lambda s, c=c: (0, c), pipeline_mode=pl.Buffered(1))
            for width, c in zip(widths, columns)
        ]
        + ([] if base is None else [pl.BlockSpec((1, tok, rows), lambda s: (first + step * s, 0, 0))] * 2),
        out_specs=[pl.BlockSpec((1, tok, rows), lambda s: (s, 0, 0))] * 2,
        cost_estimate=cost(4 * len(groups) * tok * sum(widths) * rows, rows * sum(widths) * 2 + len(groups) * tok * rows * 8),
        compiler_params=BIG,
        name="down",
    )(*pairs, *weights, *(() if base is None else base))


def start_wo(blocks, dst, sems):
    for r, ref in enumerate(blocks):
        pltpu.make_async_copy(ref, dst.at[r], sems.at[r]).start()


def wait_wo(r, dst, sems):
    pltpu.make_async_copy(dst.at[r], dst.at[r], sems.at[r]).wait()


def close_kernel(*refs):
    wo_blocks = refs[:TP]
    index, heads, x, gain, resid_out, n2_out, wo, sems = refs[TP:]
    start_wo(wo_blocks, wo, sems)
    y = x[...].astype(F32)
    for r in range(TP):
        wait_wo(r, wo, sems)
        y += mm(heads[index[r]], wo[r], NT)
    resid_out[...] = y
    n2_out[...] = (y * lax.rsqrt(jnp.mean(y * y, axis=-1, keepdims=True) + NORM_EPS) * gain[...]).astype(BF)


def close_attention(wo_blocks, index, heads, x, gain):
    tok = x.shape[0]
    return pl.pallas_call(
        close_kernel,
        out_shape=(jax.ShapeDtypeStruct((tok, D), F32), jax.ShapeDtypeStruct((tok, D), BF)),
        in_specs=[ANY] * TP + [SMEM] + [VMEM] * 3,
        out_specs=(VMEM, VMEM),
        scratch_shapes=[pltpu.VMEM((TP, D, QW), BF), pltpu.SemaphoreType.DMA((TP,))],
        cost_estimate=cost(2 * tok * D * D, 2 * D * D),
        compiler_params=BIG,
        name="close_attention",
    )(*wo_blocks, index, heads, x, gain)


def open_kernel(*refs):
    wo_blocks = refs[:TP]
    index, own, from_x, from_y, resid, dy, gain, back_out, att_out, heads, wo, sems = refs[TP:]
    start_wo(wo_blocks, wo, sems)
    d_n = own[...].astype(F32) + from_x[...].astype(F32) + from_y[...].astype(F32)
    y = resid[...]
    scale = lax.rsqrt(jnp.mean(y * y, axis=-1, keepdims=True) + NORM_EPS)
    unit = y * scale
    d_unit = d_n * gain[...]
    d_y = dy[...].astype(F32) + scale * (d_unit - unit * jnp.mean(d_unit * unit, axis=-1, keepdims=True))
    back_out[...] = d_y
    att_out[...] = d_y.astype(BF)
    att = att_out[...]
    for r in range(TP):
        wait_wo(r, wo, sems)
        heads[index[r]] = jnp.dot(att, wo[r], preferred_element_type=F32).astype(BF)


def open_attention(wo_blocks, index, terms, resid, dy, gain):
    tok = dy.shape[0]
    return pl.pallas_call(
        open_kernel,
        out_shape=(
            jax.ShapeDtypeStruct((tok, D), F32),
            jax.ShapeDtypeStruct((tok, D), BF),
            jax.ShapeDtypeStruct((TP, tok, QW), BF),
        ),
        in_specs=[ANY] * TP + [SMEM] + [VMEM] * 6,
        out_specs=(VMEM, VMEM, VMEM),
        scratch_shapes=[pltpu.VMEM((TP, D, QW), BF), pltpu.SemaphoreType.DMA((TP,))],
        cost_estimate=cost(2 * tok * D * D, 2 * D * D),
        compiler_params=BIG,
        name="open_attention",
    )(*wo_blocks, index, *terms, resid, dy, gain)


def turn_grad_kernel(count, *refs):
    blocks, left, out, rows, sems = refs[:count], *refs[count:]
    start_rows(blocks, rows, sems)
    for r in range(TP):
        wait_rows(r, rows, sems)
    planes, _, cols = out.shape

    def back(z, carry):
        at = pl.ds(pl.multiple_of(z * cols, cols), cols)
        out[z] = mm(left[...], rows[:, at], TN).astype(BF)
        return carry

    lax.fori_loop(0, planes, back, 0)


def turn_grad(left, blocks):
    tokens, cols = left.shape
    planes = lax.axis_size("z")
    return pl.pallas_call(
        functools.partial(turn_grad_kernel, len(blocks)),
        out_shape=jax.ShapeDtypeStruct((planes, cols, D // planes), BF),
        in_specs=[ANY] * len(blocks) + [VMEM],
        out_specs=VMEM,
        scratch_shapes=[pltpu.VMEM((tokens, D), BF), pltpu.SemaphoreType.DMA((TP,))],
        cost_estimate=cost(2 * tokens * D * cols, 2 * tokens * D),
        compiler_params=BIG,
        name="turn_grad",
    )(*blocks, left)


def to_pieces(pieces):
    rows, cols = pieces.shape[1:]
    return trade(pieces).reshape(TP * rows, cols)


def sum_z(grad):
    planes, cols, wide = grad.shape
    return lax.psum_scatter(grad.reshape(planes * cols, wide), "z", scatter_dimension=0, tiled=True)


def give_back(summed):
    return trade(turn(summed))


def by_plane(grad):
    planes = lax.axis_size("z")
    return grad.reshape(grad.shape[0], planes, D // planes).transpose(1, 0, 2)


def pick(blocks, at):
    return lax.dynamic_index_in_dim(blocks, at, 0, keepdims=False)


def on_device(hidden_in, segment_ids, w_attn, w_ffn, gains, out_grad):
    tok = hidden_in.shape[0]
    rows = w_attn.shape[0]
    me = lax.axis_index(PLANE)
    z = lax.axis_index("z")
    tokens = TP * tok
    steps = jnp.arange(TP, dtype=jnp.int32)
    rel = me ^ steps
    perm = fold_order()
    ek, ev = spread_kv()

    own_start = (z * TP + me) * tok
    own_lo = segment_ids - own_start + tok
    extra = jnp.zeros((EXTRA, AW), BF)
    extra = extra.at[0, : 2 * rows].set(gains.reshape(-1))
    extra = extra.at[1, :tok].set((own_lo // 2).astype(BF)).at[2, :tok].set((own_lo % 2).astype(BF))

    attn_pieces = cut_attn(w_attn, perm)
    attn_pieces = jnp.concatenate([attn_pieces, jnp.broadcast_to(extra, (TP, *extra.shape))], axis=1)
    attn_rows = to_pieces(attn_pieces)
    x_begun = gather_begin(hidden_in)
    pieces = cut_ffn(after(w_ffn, attn_rows))
    rows_0 = to_pieces(pieces[0])
    w_0 = gather_z(rows_0)
    x_blocks = gather_end(*x_begun)
    dy_begun = gather_begin(after(out_grad, *x_begun[1:]))
    attn_all = after(gather_z(attn_rows), rows_0).reshape(-1, rows + EXTRA, AW)
    w_own = attn_all[:, :rows].reshape(D, AW)
    wqkv, wo = w_own[:, : QW + 2 * HD], w_own[:, QW + 2 * HD :]
    gains_full = attn_all[:, rows, : 2 * rows].reshape(-1, 2, rows).transpose(1, 0, 2).reshape(2, D).astype(F32)

    plane_lo = attn_rows.reshape(TP, rows + EXTRA, -1)[:, rows + 1 : rows + 3, :tok].astype(jnp.int32)
    lo = jnp.take(2 * plane_lo[:, 0] + plane_lo[:, 1], rel, axis=0)
    positions = jnp.arange(tok, dtype=jnp.int32)[None] + tok - lo
    freqs = 1.0 / ROPE_BASE ** (jnp.arange(HALF, dtype=F32) * (2.0 / HD))
    angles = positions.reshape(tokens).astype(F32)[:, None] * freqs
    cosine = jnp.tile(jnp.cos(angles), (1, GROUP))
    sine = jnp.tile(jnp.sin(angles), (1, GROUP))

    early = 6
    halves = []
    for first, last in ((0, early), (early, TP)):
        at = slice(first * tok, last * tok)
        halves.append(norm_qkv(x_blocks[first:last], gains_full[:1], attn_all, cosine[at], sine[at]))
    (n1, q, kv), (n1_late, q_late, kv_late) = halves
    q, kv = jnp.concatenate([q, q_late], axis=0), jnp.concatenate([kv, kv_late], axis=0)
    wo_begun = gather_begin(wo)
    rows_1 = to_pieces(after(pieces[1], attn_all))
    q = after(q, rows_1, *wo_begun[1:], *dy_begun[1:])
    before = along_z(pick(kv.reshape(TP, tok, 2 * HD), me ^ (TP - 1)), 1)
    kv9 = jnp.concatenate([kv, before], axis=0)
    prev_at = jnp.where(rel == 0, TP, (rel - 1) ^ me)
    mixed, heads = attend(prev_at, rel, q, kv9, lo.reshape(tokens, 1), ek, ev)

    wo_blocks = gather_end(*wo_begun)
    heads = trade(heads)
    dy_blocks = gather_end(*after(dy_begun, mixed))
    w_1 = gather_z(rows_1)
    x_own = hidden_in.astype(F32)
    residual, normed_two = close_attention(wo_blocks, rel, heads, after(hidden_in, w_0), gains_full[1:])
    n2_blocks = gather_plane(normed_two)

    act_0, d_gu_0, grad_0 = ffn_call(ffn_kernel, n2_blocks, dy_blocks, w_0, (0, 2), 18)
    so_far = down([d_gu_0], [w_0], False, (0, 1, 2, 3), kind=F32)
    sum_0 = sum_z(grad_0)
    act_1, d_gu_1, flat_1 = ffn_call(ffn_forward_kernel, n2_blocks, dy_blocks, after(w_1, so_far[0]), (0, 1), 9)
    d_n2_parts = {groups: down([d_gu_1], [w_1], False, groups, so_far) for groups in ((3, 2), (1, 0))}
    d_n2_terms, unused = scatter_plane(d_n2_parts.get)
    (grad_1,) = ffn_call(ffn_back_kernel, n2_blocks, dy_blocks, after(flat_1, d_n2_parts[1, 0][0]), (2,), 9)
    sum_1 = sum_z(grad_1)
    acts, w_all = [after(act_0, grad_1), act_1], [w_0, w_1]
    f_parts = {groups: down(acts, w_all, True, groups) for groups in ((3, 2), (1, 0))}
    d_n2_terms = after(d_n2_terms, *f_parts.values())
    d_resid, d_att, d_heads = open_attention(wo_blocks, rel, d_n2_terms, residual, out_grad, gains_full[1:])
    d_o = trade(d_heads)
    d_att_begun = gather_begin(after(d_att, d_o))
    here_at = me ^ steps
    prev_abs = jnp.where(steps == 0, TP, (steps - 1) ^ me)
    d_q, d_kv9 = attend_back(here_at, prev_abs, q, after(d_o, sum_0), kv9, lo.reshape(TP, 1, tok), cosine, sine, ek, ev)
    f_terms, unused = scatter_plane(lambda groups: after(f_parts[groups], d_heads), (d_q,))
    hidden_out = (residual + total(*f_terms)).astype(BF)
    d_att_blocks = gather_end(*after(d_att_begun, d_q))
    wo_grad = turn_grad(mixed, d_att_blocks)
    back = along_z(d_kv9[tokens:].astype(BF), -1)
    last = me ^ (TP - 1)
    d_kv = d_kv9[:tokens].reshape(TP, tok, 2 * HD)
    d_kv = jnp.where((steps == last)[:, None, None], d_kv + back.astype(F32)[None], d_kv).reshape(tokens, 2 * HD)
    c, s = cosine[:, :HALF], sine[:, :HALF]
    a, b = d_kv[:, :HALF], d_kv[:, HALF:HD]
    d_qkv = jnp.concatenate(
        [d_q, (a * c + b * s).astype(BF), (b * c - a * s).astype(BF), d_kv[:, HD:].astype(BF)], axis=1
    )
    cut = early * tok
    qkv_grad = by_plane((mm(d_qkv[:cut], n1, TN) + mm(d_qkv[cut:], n1_late, TN)).astype(BF))
    attn_sum = jnp.concatenate([qkv_grad, wo_grad], axis=1)
    attn_back = give_back(sum_z(attn_sum))
    d_qkv = after(d_qkv, attn_sum, *f_terms)
    d_n1_terms, unused = scatter_plane(lambda groups: down([d_qkv], [wqkv], False, groups))
    d_normed = total(*d_n1_terms)
    pieces = [give_back(v) for v in (sum_0, sum_1)]
    scale = lax.rsqrt(jnp.mean(x_own * x_own, axis=-1, keepdims=True) + NORM_EPS)
    unit = x_own * scale
    d_unit = d_normed * gains_full[0]
    in_grad = d_resid + scale * (d_unit - unit * jnp.mean(d_unit * unit, axis=-1, keepdims=True))
    ffn_grad, term_two = paste_ffn(pieces, w_ffn)
    attn_grad, term_one = paste_attn(attn_back, w_attn, perm)
    gains_grad = jnp.concatenate([term_one, term_two], axis=1).T / gains.astype(F32)
    return hidden_out, in_grad.astype(BF), attn_grad, ffn_grad, gains_grad


def solution(mesh):
    fine = Mesh(mesh.devices.reshape(-1, 2, 2, 2), EVERY)
    rows = P(EVERY, None)
    in_specs = (rows, P(EVERY), rows, rows, P(None, EVERY), rows)
    out_specs = (rows, rows, rows, rows, P(None, EVERY))
    return jax.shard_map(
        on_device, mesh=fine, in_specs=in_specs, out_specs=out_specs, check_vma=False
    )
```

```python
import functools

import jax
import jax.numpy as jnp
from jax import lax
from jax.experimental import pallas as pl
from jax.experimental.pallas import tpu as pltpu
from jax.sharding import Mesh, PartitionSpec as P

D = 2048
H = 32
KV = 8
HD = 64
FF = 8192
GROUP = H // KV
TP = 8
WIDTHS = (512, 512)
CHUNKS = len(WIDTHS)
HALF = HD // 2
QW = GROUP * HD
STARTS = [TP * sum(WIDTHS[:k]) for k in range(CHUNKS)]
EXTRA = 8
AW = 2 * QW + 2 * HD

NORM_EPS = 1e-05
ROPE_BASE = 500000.0
SCALE = HD ** (-0.5)

PLANE = ("y", "x", "c")
EVERY = ("z", "y", "x", "c")
BF = jnp.bfloat16
F32 = jnp.float32
ANY = pl.BlockSpec(memory_space=pl.ANY)
VMEM = pl.BlockSpec(memory_space=pltpu.VMEM)
SMEM = pl.BlockSpec(memory_space=pltpu.SMEM)
BIG = pltpu.CompilerParams(vmem_limit_bytes=56 * 1024 * 1024)


def cost(flops, size):
    return pl.CostEstimate(flops=int(flops), bytes_accessed=int(size), transcendentals=0)


def mm(left, right, dims):
    return lax.dot_general(left, right, (dims, ((), ())), preferred_element_type=F32)


NN = ((1,), (0,))
NT = ((1,), (1,))
TN = ((0,), (0,))


def after(value, *first):
    return lax.optimization_barrier((value, *first))[0]


def rms_norm(values, scales):
    return values * lax.rsqrt(jnp.mean(values * values, axis=-1, keepdims=True) + NORM_EPS) * scales


def swap(value, rel):
    return lax.ppermute(value, PLANE, [(i, i ^ rel) for i in range(TP)])


def swap_across(value):
    return lax.ppermute(value, PLANE, [(i, i ^ (2 + 2 * (i % 2))) for i in range(TP)])


def on_first():
    return lax.axis_index(PLANE) % 2 == 0


def gather_begin(own):
    return own, swap(own, 2), swap(own, 4), swap(own, 1)


def gather_end(own, from_x, from_y, from_c):
    across = swap_across(jnp.where(on_first(), from_y, from_x))
    return [own, from_c, from_x, swap(from_x, 1), from_y, swap(from_y, 1), across, swap(across, 1)]


def gather_plane(own):
    return gather_end(*gather_begin(own))


def add(left, right):
    return (left.astype(F32) + right.astype(F32)).astype(BF)


def scatter_plane(part, wait=()):
    even, odd = part((3, 2))
    both = add(even, swap(odd, 1))
    across, over_y = swap_across(both[0]), both[1]
    even, odd = part((1, 0))
    both = add(even, swap(odd, 1))
    over_x, own = both[0], both[1]
    across = after(across, *wait)
    first = on_first()
    over_x = jnp.where(first, over_x, add(over_x, across))
    over_y = jnp.where(first, add(over_y, across), over_y)
    return (own, swap(over_x, 2), swap(over_y, 4)), (over_x, over_y)


def total(own, from_x, from_y):
    return own.astype(F32) + from_x.astype(F32) + from_y.astype(F32)


def trade(blocks):
    return lax.all_to_all(blocks, PLANE, 0, 0, tiled=True)


def along_z(value, steps):
    count = lax.axis_size("z")
    return lax.ppermute(
        value, "z", [(i, i + steps) for i in range(count) if 0 <= i + steps < count]
    )


def gather_z(own):
    return lax.all_gather(own, "z", axis=0, tiled=True)


def start_rows(refs, dst, sems):
    each = dst.shape[0] // len(refs)
    for r, ref in enumerate(refs):
        pltpu.make_async_copy(ref, dst.at[pl.ds(r * each, each)], sems.at[r]).start()


def wait_rows(r, dst, sems, count=TP):
    each = dst.shape[0] // count
    part = dst.at[pl.ds(pl.multiple_of(r * each, each), each)]
    pltpu.make_async_copy(part, part, sems.at[r]).wait()


def fold_order():
    old = jnp.arange(QW, dtype=jnp.int32)
    new = (old // HALF) % 2 * (GROUP * HALF) + old // HD * HALF + old % HALF
    return (new[:, None] == jnp.arange(QW, dtype=jnp.int32)[None, :]).astype(BF)


def cut_attn_kernel(w_ref, perm_ref, out):
    kv_cols = KV * HD
    for i in range(TP):
        q = jnp.dot(w_ref[:, QW * i : QW * (i + 1)], perm_ref[...], preferred_element_type=F32)
        out[i, :, :QW] = q.astype(BF)
        k = w_ref[:, D + HD * i : D + HD * (i + 1)]
        v = w_ref[:, D + kv_cols + HD * i : D + kv_cols + HD * (i + 1)]
        out[i, :, QW : QW + 2 * HD] = jnp.concatenate([k, v], axis=1)
        out[i, :, QW + 2 * HD :] = w_ref[:, D + 2 * kv_cols + QW * i : D + 2 * kv_cols + QW * (i + 1)]


def cut_attn(w_attn, perm):
    rows = w_attn.shape[0]
    return pl.pallas_call(
        cut_attn_kernel,
        out_shape=jax.ShapeDtypeStruct((TP, rows, AW), BF),
        in_specs=[VMEM, VMEM],
        out_specs=VMEM,
        cost_estimate=cost(0, 2 * w_attn.size * 2),
        name="cut_attn",
    )(w_attn, perm)


def cut_ffn_kernel(w_ref, *outs):
    for k, width in enumerate(WIDTHS):
        for i in range(TP):
            for n in range(3):
                at = n * FF + STARTS[k] + i * width
                outs[k][i, :, n * width : (n + 1) * width] = w_ref[:, at : at + width]


def cut_ffn(w_ffn):
    rows = w_ffn.shape[0]
    return pl.pallas_call(
        cut_ffn_kernel,
        out_shape=[jax.ShapeDtypeStruct((TP, rows, 3 * width), BF) for width in WIDTHS],
        in_specs=[VMEM],
        out_specs=[VMEM] * CHUNKS,
        cost_estimate=cost(0, 2 * w_ffn.size * 2),
        compiler_params=BIG,
        name="cut_ffn",
    )(w_ffn)


def paste_ffn_kernel(*refs):
    pieces, w, out, term = refs[:CHUNKS], *refs[CHUNKS:]
    each = min(WIDTHS)
    total = jnp.zeros((w.shape[0], each), F32)
    for k, width in enumerate(WIDTHS):
        for i in range(TP):
            for n in range(3):
                for part in range(0, width, each):
                    at = n * FF + STARTS[k] + i * width + part
                    grad = pieces[k][i, :, n * width + part : n * width + part + each].astype(F32)
                    out[:, at : at + each] = grad
                    if n < 2:
                        total += grad * w[:, at : at + each].astype(F32)
    term[...] = jnp.sum(total, axis=-1, keepdims=True)


def paste_ffn(pieces, w_ffn):
    rows = w_ffn.shape[0]
    return pl.pallas_call(
        paste_ffn_kernel,
        out_shape=(jax.ShapeDtypeStruct(w_ffn.shape, F32), jax.ShapeDtypeStruct((rows, 1), F32)),
        in_specs=[VMEM] * (CHUNKS + 1),
        out_specs=(VMEM, VMEM),
        cost_estimate=cost(0, 8 * w_ffn.size),
        compiler_params=BIG,
        name="paste_ffn",
    )(*pieces, w_ffn)


def paste_attn_kernel(piece, w, perm, out, term):
    kv_cols = KV * HD
    ones = jnp.zeros((w.shape[0], QW), F32)
    small = jnp.zeros((w.shape[0], HD), F32)
    for i in range(TP):
        q = mm(piece[i, :, :QW], perm[...], NT)
        out[:, QW * i : QW * (i + 1)] = q
        ones += q * w[:, QW * i : QW * (i + 1)].astype(F32)
        kv = piece[i, :, QW : QW + 2 * HD].astype(F32)
        for at, part in ((D + HD * i, kv[:, :HD]), (D + kv_cols + HD * i, kv[:, HD:])):
            out[:, at : at + HD] = part
            small += part * w[:, at : at + HD].astype(F32)
        at = D + 2 * kv_cols + QW * i
        out[:, at : at + QW] = piece[i, :, QW + 2 * HD :].astype(F32)
    term[...] = jnp.sum(ones, axis=-1, keepdims=True) + jnp.sum(small, axis=-1, keepdims=True)


def paste_attn(piece, w_attn, perm):
    rows = w_attn.shape[0]
    return pl.pallas_call(
        paste_attn_kernel,
        out_shape=(jax.ShapeDtypeStruct(w_attn.shape, F32), jax.ShapeDtypeStruct((rows, 1), F32)),
        in_specs=[VMEM] * 3,
        out_specs=(VMEM, VMEM),
        cost_estimate=cost(0, 8 * w_attn.size),
        compiler_params=BIG,
        name="paste_attn",
    )(piece, w_attn, perm)


def turn_kernel(x, out):
    rows = out.shape[1]
    turned = x[...].astype(F32).T.astype(BF)
    for i in range(TP):
        out[i] = turned[rows * i : rows * (i + 1)]


def turn(x):
    cols, wide = x.shape
    return pl.pallas_call(
        turn_kernel,
        out_shape=jax.ShapeDtypeStruct((TP, wide // TP, cols), BF),
        in_specs=[VMEM],
        out_specs=VMEM,
        cost_estimate=cost(0, 4 * x.size),
        compiler_params=BIG,
        name="turn",
    )(x)


def qkv_kernel(count, *refs):
    blocks = refs[:count]
    gain, w_all, cos, sin, n1, q_out, kv_out, x_s, w_s, sems, w_sem = refs[count:]
    w_copy = pltpu.make_async_copy(w_all.at[:, pl.ds(0, w_s.shape[1]), pl.ds(0, w_s.shape[2])], w_s, w_sem)
    w_copy.start()
    start_rows(blocks, x_s, sems)
    each = x_s.shape[0] // count
    lane = lax.broadcasted_iota(jnp.int32, (each, 2 * HD), 1)
    w_copy.wait()

    def step(r, carry):
        at = pl.ds(pl.multiple_of(r * each, each), each)
        wait_rows(r, x_s, sems, count)
        x = x_s[at, :].astype(F32)
        scale = lax.rsqrt(jnp.mean(x * x, axis=-1, keepdims=True) + NORM_EPS)
        normed = (x * scale * gain[...]).astype(BF)
        n1[at, :] = normed
        qkv = jnp.dot(normed, w_s[...].reshape(D, QW + 2 * HD), preferred_element_type=F32)
        c, s = cos[at, :], sin[at, :]
        a, b = qkv[:, : QW // 2], qkv[:, QW // 2 : QW]
        q_out[at, : QW // 2] = (a * c - b * s).astype(BF)
        q_out[at, QW // 2 :] = (b * c + a * s).astype(BF)
        kv = qkv[:, QW:]
        ahead = pltpu.roll(kv, 2 * HD - HALF, 1)
        behind = pltpu.roll(kv, HALF, 1)
        turned = kv * c + jnp.where(lane < HALF, -ahead, behind) * s
        kv_out[at, :] = jnp.where(lane < HD, turned, kv).astype(BF)
        return carry

    lax.fori_loop(0, count, step, 0)


def norm_qkv(blocks, gain, w_all, cos, sin):
    each = w_all.shape[1] - EXTRA
    tokens = cos.shape[0]
    return pl.pallas_call(
        functools.partial(qkv_kernel, len(blocks)),
        out_shape=(
            jax.ShapeDtypeStruct((tokens, D), BF),
            jax.ShapeDtypeStruct((tokens, QW), BF),
            jax.ShapeDtypeStruct((tokens, 2 * HD), BF),
        ),
        in_specs=[ANY] * len(blocks) + [VMEM, ANY, VMEM, VMEM],
        out_specs=(VMEM, VMEM, VMEM),
        scratch_shapes=[
            pltpu.VMEM((tokens, D), BF),
            pltpu.VMEM((w_all.shape[0], each, QW + 2 * HD), BF),
            pltpu.SemaphoreType.DMA((len(blocks),)),
            pltpu.SemaphoreType.DMA,
        ],
        cost_estimate=cost(2 * tokens * D * (QW + 2 * HD), 4 * tokens * D),
        compiler_params=BIG,
        name="norm_qkv",
    )(*blocks, gain, w_all, cos, sin)


def spread_kv():
    src = jnp.arange(2 * HD, dtype=jnp.int32)[:, None]
    col = jnp.arange(QW, dtype=jnp.int32)[None, :]
    key = (src == col // (GROUP * HALF) * HALF + col % HALF).astype(BF)
    value = (src == HD + col % HD).astype(BF)
    return key, value


def attend_kernel(prev_at, index, q_ref, prev_ref, here_ref, lo_ref, ek, ev, o_ref, o_index_ref):
    tok = q_ref.shape[0]
    two = jnp.concatenate([prev_ref[...], here_ref[...]], axis=0)
    keys = jnp.dot(two, ek[...], preferred_element_type=F32).astype(BF)
    values = jnp.dot(two, ev[...], preferred_element_type=F32).astype(BF)
    q = q_ref[...]
    key_at = lax.broadcasted_iota(jnp.int32, (tok, 2 * tok), 1)
    row_at = lax.broadcasted_iota(jnp.int32, (tok, 2 * tok), 0)
    allowed = (lo_ref[...] <= key_at) & (key_at <= row_at + tok)
    q_lane = lax.broadcasted_iota(jnp.int32, (tok, QW), 1)
    v_lane = lax.broadcasted_iota(jnp.int32, (2 * tok, QW), 1)
    total = jnp.zeros((tok, QW), F32)
    for h in range(GROUP):
        mine = jnp.where((q_lane // HALF) % GROUP == h, q, jnp.zeros_like(q))
        s = jnp.where(allowed, mm(mine, keys, NT) * SCALE, -1e30)
        expo = jnp.exp(s - jnp.max(s, axis=-1, keepdims=True))
        probs = (expo / jnp.sum(expo, axis=-1, keepdims=True)).astype(BF)
        total += mm(probs, jnp.where(v_lane // HD == h, values, jnp.zeros_like(values)), NN)
    o_ref[...] = total.astype(BF)
    o_index_ref[0] = o_ref[...]


def attend(prev_at, index, q, kv9, lo_col, ek, ev):
    tokens = q.shape[0]
    tok = tokens // TP
    full = lambda shape: pl.BlockSpec(shape, lambda r, p, i: (0, 0))
    return pl.pallas_call(
        attend_kernel,
        out_shape=(jax.ShapeDtypeStruct((tokens, QW), BF), jax.ShapeDtypeStruct((TP, tok, QW), BF)),
        grid_spec=pltpu.PrefetchScalarGridSpec(
            num_scalar_prefetch=2,
            grid=(TP,),
            in_specs=[
                pl.BlockSpec((tok, QW), lambda r, p, i: (r, 0)),
                pl.BlockSpec((tok, 2 * HD), lambda r, p, i: (p[r], 0)),
                pl.BlockSpec((tok, 2 * HD), lambda r, p, i: (r, 0)),
                pl.BlockSpec((tok, 1), lambda r, p, i: (r, 0)),
                full((2 * HD, QW)),
                full((2 * HD, QW)),
            ],
            out_specs=(
                pl.BlockSpec((tok, QW), lambda r, p, i: (r, 0)),
                pl.BlockSpec((1, tok, QW), lambda r, p, i: (i[r], 0, 0)),
            ),
        ),
        cost_estimate=cost(4 * tokens * 2 * tok * QW * GROUP, 4 * tokens * QW),
        compiler_params=BIG,
        name="attend",
    )(prev_at, index, q, kv9, kv9, lo_col, ek, ev)


def attend_back_kernel(here_at, prev_at, q_ref, do_ref, prev_ref, here_ref, lo_ref, cos, sin, ek, ev, dq_ref, dkv_ref, carry):
    step = pl.program_id(0)
    tok = q_ref.shape[0]

    @pl.when(step == 0)
    def _():
        carry[...] = jnp.zeros_like(carry)

    @pl.when(step < TP)
    def _():
        two = jnp.concatenate([prev_ref[...], here_ref[...]], axis=0)
        keys = jnp.dot(two, ek[...], preferred_element_type=F32).astype(BF)
        values = jnp.dot(two, ev[...], preferred_element_type=F32).astype(BF)
        q, d_o = q_ref[...], do_ref[0]
        key_at = lax.broadcasted_iota(jnp.int32, (2 * tok, tok), 0)
        row_at = lax.broadcasted_iota(jnp.int32, (2 * tok, tok), 1)
        allowed = (lo_ref[0] <= key_at) & (key_at <= row_at + tok)
        lane = lax.broadcasted_iota(jnp.int32, (tok, QW), 1)
        key_lane = lax.broadcasted_iota(jnp.int32, (2 * tok, QW), 1)
        d_q = jnp.zeros((tok, QW), F32)
        d_k = jnp.zeros((2 * tok, QW), F32)
        d_v = jnp.zeros((2 * tok, QW), F32)
        for h in range(GROUP):
            q_h = jnp.where((lane // HALF) % GROUP == h, q, jnp.zeros_like(q))
            do_h = jnp.where(lane // HD == h, d_o, jnp.zeros_like(d_o))
            k_h = jnp.where((key_lane // HALF) % GROUP == h, keys, jnp.zeros_like(keys))
            s = jnp.where(allowed, mm(keys, q_h, NT) * SCALE, -1e30)
            expo = jnp.exp(s - jnp.max(s, axis=0, keepdims=True))
            probs = expo / jnp.sum(expo, axis=0, keepdims=True)
            d_p = mm(values, do_h, NT)
            shift = jnp.sum(d_p * probs, axis=0, keepdims=True)
            d_s = (probs * (d_p - shift)).astype(BF)
            d_v += mm(probs.astype(BF), do_h, NN)
            d_k += mm(d_s, q_h, NN)
            d_q += mm(d_s, k_h, TN)
        d_q = d_q * SCALE
        a, b = d_q[:, : QW // 2], d_q[:, QW // 2 :]
        c, s = cos[...], sin[...]
        dq_ref[:, : QW // 2] = (a * c + b * s).astype(BF)
        dq_ref[:, QW // 2 :] = (b * c - a * s).astype(BF)
        d_k = d_k * SCALE

        def fold(v):
            v = v + pltpu.roll(v, HD, 1)
            return v + pltpu.roll(v, HALF, 1)

        first, second = fold(d_k[:, : QW // 2]), fold(d_k[:, QW // 2 :])
        whole = d_v[:, : QW // 2] + d_v[:, QW // 2 :]
        whole = whole + pltpu.roll(whole, HD, 1)
        low = lax.broadcasted_iota(jnp.int32, (2 * tok, 2 * HD), 1)
        d_kv = jnp.where(low < HALF, first, jnp.where(low < HD, second, whole))
        dkv_ref[...] = carry[...] + d_kv[:tok]
        carry[...] = d_kv[tok:]

    @pl.when(step == TP)
    def _():
        dkv_ref[...] = carry[...]


def attend_back(here_at, prev_at, q, d_o, kv9, lo_row, cos, sin, ek, ev):
    tokens = q.shape[0]
    tok = tokens // TP
    last = TP - 1
    here = lambda cols: pl.BlockSpec((tok, cols), lambda s, h, p: (h[jnp.minimum(s, last)], 0))
    full = lambda shape: pl.BlockSpec(shape, lambda s, h, p: (0, 0))
    return pl.pallas_call(
        attend_back_kernel,
        out_shape=(
            jax.ShapeDtypeStruct((tokens, QW), BF),
            jax.ShapeDtypeStruct((tokens + tok, 2 * HD), F32),
        ),
        grid_spec=pltpu.PrefetchScalarGridSpec(
            num_scalar_prefetch=2,
            grid=(TP + 1,),
            in_specs=[
                here(QW),
                pl.BlockSpec((1, tok, QW), lambda s, h, p: (jnp.minimum(s, last), 0, 0)),
                pl.BlockSpec((tok, 2 * HD), lambda s, h, p: (p[jnp.minimum(s, last)], 0)),
                here(2 * HD),
                pl.BlockSpec((1, 1, tok), lambda s, h, p: (h[jnp.minimum(s, last)], 0, 0)),
                here(2 * HD),
                here(2 * HD),
                full((2 * HD, QW)),
                full((2 * HD, QW)),
            ],
            out_specs=(
                here(QW),
                pl.BlockSpec((tok, 2 * HD), lambda s, h, p: (jnp.where(s == 0, TP, h[jnp.maximum(s - 1, 0)]), 0)),
            ),
            scratch_shapes=[pltpu.VMEM((tok, 2 * HD), F32)],
        ),
        cost_estimate=cost(10 * tokens * 2 * tok * QW * GROUP, 8 * tokens * QW),
        compiler_params=BIG,
        name="attend_back",
    )(here_at, prev_at, q, d_o, kv9, kv9, lo_row, cos, sin, ek, ev)


def ffn_forward(r, n2, dy, w, act_out, dgu_out, flat):
    each = n2.shape[0] // TP
    width = act_out.shape[1]
    two = 2 * width
    at = pl.ds(pl.multiple_of(r * each, each), each)
    gate_up = jnp.dot(n2[at, :], w[:, :two], preferred_element_type=F32)
    d_act = jnp.dot(dy[at, :], w[:, two:], preferred_element_type=F32)
    g, u = gate_up[:, :width], gate_up[:, width:]
    sg = jax.nn.sigmoid(g)
    gs = g * sg
    act = (gs * u).astype(BF)
    d_g = (d_act * u * (sg * (1.0 + g * (1.0 - sg)))).astype(BF)
    d_u = (d_act * gs).astype(BF)
    act_out[at, :] = act
    dgu_out[at, :width] = d_g
    dgu_out[at, width:] = d_u
    flat[:width, at] = d_g.T
    flat[width:two, at] = d_u.T
    flat[two:, at] = act.T


def ffn_back(flat, n2, dy, grad_out, held, out_sems):
    planes, wide, cols = grad_out.shape
    two = 2 * wide // 3

    def leave(z):
        return pltpu.make_async_copy(held.at[lax.rem(z, 2)], grad_out.at[z], out_sems.at[lax.rem(z, 2)])

    def back(z, carry):
        at = pl.ds(pl.multiple_of(z * cols, cols), cols)
        slot = lax.rem(z, 2)

        @pl.when(z >= 2)
        def _():
            leave(z - 2).wait()

        held[slot, :two, :] = jnp.dot(flat[:two, :], n2[:, at], preferred_element_type=F32).astype(BF)
        held[slot, two:, :] = jnp.dot(flat[two:, :], dy[:, at], preferred_element_type=F32).astype(BF)
        leave(z).start()
        return carry

    lax.fori_loop(0, planes, back, 0)
    leave(planes - 2).wait()
    leave(planes - 1).wait()


def ffn_kernel(*refs):
    n2_blocks, dy_blocks = refs[:TP], refs[TP : 2 * TP]
    w, act_out, dgu_out, grad_out, n2, dy, flat, held, n2_sems, dy_sems, out_sems = refs[2 * TP :]
    start_rows(n2_blocks, n2, n2_sems)
    start_rows(dy_blocks, dy, dy_sems)

    def forward(r, carry):
        wait_rows(r, n2, n2_sems)
        wait_rows(r, dy, dy_sems)
        ffn_forward(r, n2, dy, w, act_out, dgu_out, flat)
        return carry

    lax.fori_loop(0, TP, forward, 0)
    ffn_back(flat, n2, dy, grad_out, held, out_sems)


def ffn_forward_kernel(*refs):
    n2_blocks, dy_blocks = refs[:TP], refs[TP : 2 * TP]
    w, act_out, dgu_out, flat, n2, dy, n2_sems, dy_sems = refs[2 * TP :]
    start_rows(n2_blocks, n2, n2_sems)
    start_rows(dy_blocks, dy, dy_sems)

    def forward(r, carry):
        wait_rows(r, n2, n2_sems)
        wait_rows(r, dy, dy_sems)
        ffn_forward(r, n2, dy, w, act_out, dgu_out, flat)
        return carry

    lax.fori_loop(0, TP, forward, 0)


def ffn_back_kernel(*refs):
    n2_blocks, dy_blocks = refs[:TP], refs[TP : 2 * TP]
    flat, grad_out, n2, dy, held, n2_sems, dy_sems, out_sems = refs[2 * TP :]
    start_rows(n2_blocks, n2, n2_sems)
    start_rows(dy_blocks, dy, dy_sems)
    for r in range(TP):
        wait_rows(r, n2, n2_sems)
    for r in range(TP):
        wait_rows(r, dy, dy_sems)
    ffn_back(flat, n2, dy, grad_out, held, out_sems)


def ffn_call(kernel, n2_blocks, dy_blocks, last, outs, flops):
    tokens = TP * n2_blocks[0].shape[0]
    planes = lax.axis_size("z")
    wide = last.shape[1] if 2 not in outs or 0 in outs else last.shape[0]
    width = wide // 3
    shapes, specs, extra, sems = [], [], [], []
    if 0 in outs:
        shapes += [jax.ShapeDtypeStruct((tokens, width), BF), jax.ShapeDtypeStruct((tokens, 2 * width), BF)]
        specs += [VMEM, VMEM]
    if 1 in outs:
        shapes.append(jax.ShapeDtypeStruct((wide, tokens), BF))
        specs.append(VMEM)
    if 2 in outs:
        shapes.append(jax.ShapeDtypeStruct((planes, wide, D // planes), BF))
        specs.append(ANY)
        extra = ([pltpu.VMEM((wide, tokens), BF)] if 0 in outs else []) + [pltpu.VMEM((2, wide, D // planes), BF)]
        sems = [pltpu.SemaphoreType.DMA((2,))]
    return pl.pallas_call(
        kernel,
        out_shape=shapes,
        in_specs=[ANY] * (2 * TP) + [VMEM],
        out_specs=specs,
        scratch_shapes=[pltpu.VMEM((tokens, D), BF), pltpu.VMEM((tokens, D), BF)]
        + extra
        + [pltpu.SemaphoreType.DMA((TP,)), pltpu.SemaphoreType.DMA((TP,))]
        + sems,
        cost_estimate=cost(flops * tokens * D * width, 4 * tokens * D + 12 * width * D),
        compiler_params=BIG,
        name="ffn",
    )(*n2_blocks, *dy_blocks, last)


def down_kernel(parts, *refs):
    outs = refs[-2:]
    base = refs[2 * parts : -2]
    for at, out in enumerate(outs):
        term = base[at][0] if base else None
        for j in range(parts):
            more = mm(refs[j][0, at], refs[parts + j][...], NT)
            term = more if term is None else term + more
        out[0] = term.astype(out.dtype)


def down(parts, weights, last, groups, base=None, kind=BF):
    count = len(parts)
    tokens = parts[0].shape[0]
    tok = tokens // TP
    widths = [p.shape[1] for p in parts]
    columns = [w.shape[1] // width - 1 if last else 0 for w, width in zip(weights, widths)]
    pairs = [p.reshape(TP // 2, 2, tok, width) for p, width in zip(parts, widths)]
    rows = weights[0].shape[0]
    first, step = groups[0], groups[1] - groups[0]
    return pl.pallas_call(
        functools.partial(down_kernel, count),
        out_shape=[jax.ShapeDtypeStruct((len(groups), tok, rows), kind)] * 2,
        grid=(len(groups),),
        in_specs=[pl.BlockSpec((1, 2, tok, width), lambda s: (first + step * s, 0, 0, 0)) for width in widths]
        + [
            pl.BlockSpec((rows, width), lambda s, c=c: (0, c), pipeline_mode=pl.Buffered(1))
            for width, c in zip(widths, columns)
        ]
        + ([] if base is None else [pl.BlockSpec((1, tok, rows), lambda s: (first + step * s, 0, 0))] * 2),
        out_specs=[pl.BlockSpec((1, tok, rows), lambda s: (s, 0, 0))] * 2,
        cost_estimate=cost(4 * len(groups) * tok * sum(widths) * rows, rows * sum(widths) * 2 + len(groups) * tok * rows * 8),
        compiler_params=BIG,
        name="down",
    )(*pairs, *weights, *(() if base is None else base))


def start_wo(blocks, dst, sems):
    for r, ref in enumerate(blocks):
        pltpu.make_async_copy(ref, dst.at[r], sems.at[r]).start()


def wait_wo(r, dst, sems):
    pltpu.make_async_copy(dst.at[r], dst.at[r], sems.at[r]).wait()


def close_kernel(*refs):
    wo_blocks = refs[:TP]
    index, heads, x, gain, resid_out, n2_out, wo, sems = refs[TP:]
    start_wo(wo_blocks, wo, sems)
    y = x[...].astype(F32)
    for r in range(TP):
        wait_wo(r, wo, sems)
        y += mm(heads[index[r]], wo[r], NT)
    resid_out[...] = y
    n2_out[...] = (y * lax.rsqrt(jnp.mean(y * y, axis=-1, keepdims=True) + NORM_EPS) * gain[...]).astype(BF)


def close_attention(wo_blocks, index, heads, x, gain):
    tok = x.shape[0]
    return pl.pallas_call(
        close_kernel,
        out_shape=(jax.ShapeDtypeStruct((tok, D), F32), jax.ShapeDtypeStruct((tok, D), BF)),
        in_specs=[ANY] * TP + [SMEM] + [VMEM] * 3,
        out_specs=(VMEM, VMEM),
        scratch_shapes=[pltpu.VMEM((TP, D, QW), BF), pltpu.SemaphoreType.DMA((TP,))],
        cost_estimate=cost(2 * tok * D * D, 2 * D * D),
        compiler_params=BIG,
        name="close_attention",
    )(*wo_blocks, index, heads, x, gain)


def open_kernel(*refs):
    wo_blocks = refs[:TP]
    index, own, from_x, from_y, resid, dy, gain, back_out, att_out, heads, wo, sems = refs[TP:]
    start_wo(wo_blocks, wo, sems)
    d_n = own[...].astype(F32) + from_x[...].astype(F32) + from_y[...].astype(F32)
    y = resid[...]
    scale = lax.rsqrt(jnp.mean(y * y, axis=-1, keepdims=True) + NORM_EPS)
    unit = y * scale
    d_unit = d_n * gain[...]
    d_y = dy[...].astype(F32) + scale * (d_unit - unit * jnp.mean(d_unit * unit, axis=-1, keepdims=True))
    back_out[...] = d_y
    att_out[...] = d_y.astype(BF)
    att = att_out[...]
    for r in range(TP):
        wait_wo(r, wo, sems)
        heads[index[r]] = jnp.dot(att, wo[r], preferred_element_type=F32).astype(BF)


def open_attention(wo_blocks, index, terms, resid, dy, gain):
    tok = dy.shape[0]
    return pl.pallas_call(
        open_kernel,
        out_shape=(
            jax.ShapeDtypeStruct((tok, D), F32),
            jax.ShapeDtypeStruct((tok, D), BF),
            jax.ShapeDtypeStruct((TP, tok, QW), BF),
        ),
        in_specs=[ANY] * TP + [SMEM] + [VMEM] * 6,
        out_specs=(VMEM, VMEM, VMEM),
        scratch_shapes=[pltpu.VMEM((TP, D, QW), BF), pltpu.SemaphoreType.DMA((TP,))],
        cost_estimate=cost(2 * tok * D * D, 2 * D * D),
        compiler_params=BIG,
        name="open_attention",
    )(*wo_blocks, index, *terms, resid, dy, gain)


def turn_grad_kernel(count, *refs):
    blocks, left, out, rows, sems = refs[:count], *refs[count:]
    start_rows(blocks, rows, sems)
    for r in range(TP):
        wait_rows(r, rows, sems)
    planes, _, cols = out.shape

    def back(z, carry):
        at = pl.ds(pl.multiple_of(z * cols, cols), cols)
        out[z] = mm(left[...], rows[:, at], TN).astype(BF)
        return carry

    lax.fori_loop(0, planes, back, 0)


def turn_grad(left, blocks):
    tokens, cols = left.shape
    planes = lax.axis_size("z")
    return pl.pallas_call(
        functools.partial(turn_grad_kernel, len(blocks)),
        out_shape=jax.ShapeDtypeStruct((planes, cols, D // planes), BF),
        in_specs=[ANY] * len(blocks) + [VMEM],
        out_specs=VMEM,
        scratch_shapes=[pltpu.VMEM((tokens, D), BF), pltpu.SemaphoreType.DMA((TP,))],
        cost_estimate=cost(2 * tokens * D * cols, 2 * tokens * D),
        compiler_params=BIG,
        name="turn_grad",
    )(*blocks, left)


def to_pieces(pieces):
    rows, cols = pieces.shape[1:]
    return trade(pieces).reshape(TP * rows, cols)


def sum_z(grad):
    planes, cols, wide = grad.shape
    return lax.psum_scatter(grad.reshape(planes * cols, wide), "z", scatter_dimension=0, tiled=True)


def give_back(summed):
    return trade(turn(summed))


def by_plane(grad):
    planes = lax.axis_size("z")
    return grad.reshape(grad.shape[0], planes, D // planes).transpose(1, 0, 2)


def pick(blocks, at):
    return lax.dynamic_index_in_dim(blocks, at, 0, keepdims=False)


def on_device(hidden_in, segment_ids, w_attn, w_ffn, gains, out_grad):
    tok = hidden_in.shape[0]
    rows = w_attn.shape[0]
    me = lax.axis_index(PLANE)
    z = lax.axis_index("z")
    tokens = TP * tok
    steps = jnp.arange(TP, dtype=jnp.int32)
    rel = me ^ steps
    perm = fold_order()
    ek, ev = spread_kv()

    own_start = (z * TP + me) * tok
    own_lo = segment_ids - own_start + tok
    extra = jnp.zeros((EXTRA, AW), BF)
    extra = extra.at[0, : 2 * rows].set(gains.reshape(-1))
    extra = extra.at[1, :tok].set((own_lo // 2).astype(BF)).at[2, :tok].set((own_lo % 2).astype(BF))

    attn_pieces = cut_attn(w_attn, perm)
    attn_pieces = jnp.concatenate([attn_pieces, jnp.broadcast_to(extra, (TP, *extra.shape))], axis=1)
    attn_rows = to_pieces(attn_pieces)
    x_begun = gather_begin(hidden_in)
    pieces = cut_ffn(after(w_ffn, attn_rows))
    rows_0 = to_pieces(pieces[0])
    w_0 = gather_z(rows_0)
    x_blocks = gather_end(*x_begun)
    dy_begun = gather_begin(after(out_grad, *x_begun[1:]))
    attn_all = after(gather_z(attn_rows), rows_0).reshape(-1, rows + EXTRA, AW)
    w_own = attn_all[:, :rows].reshape(D, AW)
    wqkv, wo = w_own[:, : QW + 2 * HD], w_own[:, QW + 2 * HD :]
    gains_full = attn_all[:, rows, : 2 * rows].reshape(-1, 2, rows).transpose(1, 0, 2).reshape(2, D).astype(F32)

    plane_lo = attn_rows.reshape(TP, rows + EXTRA, -1)[:, rows + 1 : rows + 3, :tok].astype(jnp.int32)
    lo = jnp.take(2 * plane_lo[:, 0] + plane_lo[:, 1], rel, axis=0)
    positions = jnp.arange(tok, dtype=jnp.int32)[None] + tok - lo
    freqs = 1.0 / ROPE_BASE ** (jnp.arange(HALF, dtype=F32) * (2.0 / HD))
    angles = positions.reshape(tokens).astype(F32)[:, None] * freqs
    cosine = jnp.tile(jnp.cos(angles), (1, GROUP))
    sine = jnp.tile(jnp.sin(angles), (1, GROUP))

    early = 6
    halves = []
    for first, last in ((0, early), (early, TP)):
        at = slice(first * tok, last * tok)
        halves.append(norm_qkv(x_blocks[first:last], gains_full[:1], attn_all, cosine[at], sine[at]))
    (n1, q, kv), (n1_late, q_late, kv_late) = halves
    q, kv = jnp.concatenate([q, q_late], axis=0), jnp.concatenate([kv, kv_late], axis=0)
    wo_begun = gather_begin(wo)
    rows_1 = to_pieces(after(pieces[1], attn_all))
    q = after(q, rows_1, *wo_begun[1:], *dy_begun[1:])
    before = along_z(pick(kv.reshape(TP, tok, 2 * HD), me ^ (TP - 1)), 1)
    kv9 = jnp.concatenate([kv, before], axis=0)
    prev_at = jnp.where(rel == 0, TP, (rel - 1) ^ me)
    mixed, heads = attend(prev_at, rel, q, kv9, lo.reshape(tokens, 1), ek, ev)

    wo_blocks = gather_end(*wo_begun)
    heads = trade(heads)
    dy_blocks = gather_end(*after(dy_begun, mixed))
    w_1 = gather_z(rows_1)
    x_own = hidden_in.astype(F32)
    residual, normed_two = close_attention(wo_blocks, rel, heads, after(hidden_in, w_0), gains_full[1:])
    n2_blocks = gather_plane(normed_two)

    act_0, d_gu_0, grad_0 = ffn_call(ffn_kernel, n2_blocks, dy_blocks, w_0, (0, 2), 18)
    so_far = down([d_gu_0], [w_0], False, (0, 1, 2, 3), kind=F32)
    sum_0 = sum_z(grad_0)
    act_1, d_gu_1, flat_1 = ffn_call(ffn_forward_kernel, n2_blocks, dy_blocks, after(w_1, so_far[0]), (0, 1), 9)
    d_n2_parts = {groups: down([d_gu_1], [w_1], False, groups, so_far) for groups in ((3, 2), (1, 0))}
    d_n2_terms, unused = scatter_plane(d_n2_parts.get)
    (grad_1,) = ffn_call(ffn_back_kernel, n2_blocks, dy_blocks, after(flat_1, d_n2_parts[1, 0][0]), (2,), 9)
    sum_1 = sum_z(grad_1)
    acts, w_all = [after(act_0, grad_1), act_1], [w_0, w_1]
    f_parts = {groups: down(acts, w_all, True, groups) for groups in ((3, 2), (1, 0))}
    d_n2_terms = after(d_n2_terms, *f_parts.values())
    d_resid, d_att, d_heads = open_attention(wo_blocks, rel, d_n2_terms, residual, out_grad, gains_full[1:])
    d_o = trade(d_heads)
    d_att_begun = gather_begin(after(d_att, d_o))
    here_at = me ^ steps
    prev_abs = jnp.where(steps == 0, TP, (steps - 1) ^ me)
    d_q, d_kv9 = attend_back(here_at, prev_abs, q, after(d_o, sum_0), kv9, lo.reshape(TP, 1, tok), cosine, sine, ek, ev)
    f_terms, unused = scatter_plane(lambda groups: after(f_parts[groups], d_heads), (d_q,))
    hidden_out = (residual + total(*f_terms)).astype(BF)
    d_att_blocks = gather_end(*after(d_att_begun, d_q))
    wo_grad = turn_grad(mixed, d_att_blocks)
    back = along_z(d_kv9[tokens:].astype(BF), -1)
    last = me ^ (TP - 1)
    d_kv = d_kv9[:tokens].reshape(TP, tok, 2 * HD)
    d_kv = jnp.where((steps == last)[:, None, None], d_kv + back.astype(F32)[None], d_kv).reshape(tokens, 2 * HD)
    c, s = cosine[:, :HALF], sine[:, :HALF]
    a, b = d_kv[:, :HALF], d_kv[:, HALF:HD]
    d_qkv = jnp.concatenate(
        [d_q, (a * c + b * s).astype(BF), (b * c - a * s).astype(BF), d_kv[:, HD:].astype(BF)], axis=1
    )
    cut = early * tok
    qkv_grad = by_plane((mm(d_qkv[:cut], n1, TN) + mm(d_qkv[cut:], n1_late, TN)).astype(BF))
    attn_sum = jnp.concatenate([qkv_grad, wo_grad], axis=1)
    turned = turn(sum_z(attn_sum))
    attn_back = trade(turned)
    d_qkv = after(d_qkv, attn_sum, *f_terms)
    d_n1_terms, unused = scatter_plane(lambda groups: down([d_qkv], [wqkv], False, groups))
    d_normed = total(*d_n1_terms)
    pieces = [give_back(sum_0), give_back(sum_1)]
    pieces[1] = after(pieces[1], turned)
    scale = lax.rsqrt(jnp.mean(x_own * x_own, axis=-1, keepdims=True) + NORM_EPS)
    unit = x_own * scale
    d_unit = d_normed * gains_full[0]
    in_grad = d_resid + scale * (d_unit - unit * jnp.mean(d_unit * unit, axis=-1, keepdims=True))
    ffn_grad, term_two = paste_ffn(pieces, w_ffn)
    attn_grad, term_one = paste_attn(attn_back, w_attn, perm)
    gains_grad = jnp.concatenate([term_one, term_two], axis=1).T / gains.astype(F32)
    return hidden_out, in_grad.astype(BF), attn_grad, ffn_grad, gains_grad


def solution(mesh):
    fine = Mesh(mesh.devices.reshape(-1, 2, 2, 2), EVERY)
    rows = P(EVERY, None)
    in_specs = (rows, P(EVERY), rows, rows, P(None, EVERY), rows)
    out_specs = (rows, rows, rows, rows, P(None, EVERY))
    return jax.shard_map(
        on_device, mesh=fine, in_specs=in_specs, out_specs=out_specs, check_vma=False
    )
```

```python
import functools

import jax
import jax.numpy as jnp
from jax import lax
from jax.experimental import pallas as pl
from jax.experimental.pallas import tpu as pltpu
from jax.sharding import Mesh, PartitionSpec as P

D = 2048
H = 32
KV = 8
HD = 64
FF = 8192
GROUP = H // KV
TP = 8
WIDTHS = (512, 512)
CHUNKS = len(WIDTHS)
HALF = HD // 2
QW = GROUP * HD
STARTS = [TP * sum(WIDTHS[:k]) for k in range(CHUNKS)]
EXTRA = 8
AW = 2 * QW + 2 * HD

NORM_EPS = 1e-05
ROPE_BASE = 500000.0
SCALE = HD ** (-0.5)

PLANE = ("y", "x", "c")
EVERY = ("z", "y", "x", "c")
BF = jnp.bfloat16
F32 = jnp.float32
ANY = pl.BlockSpec(memory_space=pl.ANY)
VMEM = pl.BlockSpec(memory_space=pltpu.VMEM)
SMEM = pl.BlockSpec(memory_space=pltpu.SMEM)
BIG = pltpu.CompilerParams(vmem_limit_bytes=56 * 1024 * 1024)


def cost(flops, size):
    return pl.CostEstimate(flops=int(flops), bytes_accessed=int(size), transcendentals=0)


def mm(left, right, dims):
    return lax.dot_general(left, right, (dims, ((), ())), preferred_element_type=F32)


NN = ((1,), (0,))
NT = ((1,), (1,))
TN = ((0,), (0,))


def after(value, *first):
    return lax.optimization_barrier((value, *first))[0]


def rms_norm(values, scales):
    return values * lax.rsqrt(jnp.mean(values * values, axis=-1, keepdims=True) + NORM_EPS) * scales


def swap(value, rel):
    return lax.ppermute(value, PLANE, [(i, i ^ rel) for i in range(TP)])


def swap_across(value):
    return lax.ppermute(value, PLANE, [(i, i ^ (2 + 2 * (i % 2))) for i in range(TP)])


def on_first():
    return lax.axis_index(PLANE) % 2 == 0


def gather_begin(own):
    return own, swap(own, 2), swap(own, 4), swap(own, 1)


def gather_end(own, from_x, from_y, from_c):
    across = swap_across(jnp.where(on_first(), from_y, from_x))
    return [own, from_c, from_x, swap(from_x, 1), from_y, swap(from_y, 1), across, swap(across, 1)]


def gather_plane(own):
    return gather_end(*gather_begin(own))


def add(left, right):
    return (left.astype(F32) + right.astype(F32)).astype(BF)


def scatter_plane(part, wait=()):
    even, odd = part((3, 2))
    both = add(even, swap(odd, 1))
    across, over_y = swap_across(both[0]), both[1]
    even, odd = part((1, 0))
    both = add(even, swap(odd, 1))
    over_x, own = both[0], both[1]
    across = after(across, *wait)
    first = on_first()
    over_x = jnp.where(first, over_x, add(over_x, across))
    over_y = jnp.where(first, add(over_y, across), over_y)
    return (own, swap(over_x, 2), swap(over_y, 4)), (over_x, over_y)


def total(own, from_x, from_y):
    return own.astype(F32) + from_x.astype(F32) + from_y.astype(F32)


def trade(blocks):
    return lax.all_to_all(blocks, PLANE, 0, 0, tiled=True)


def along_z(value, steps):
    count = lax.axis_size("z")
    return lax.ppermute(
        value, "z", [(i, i + steps) for i in range(count) if 0 <= i + steps < count]
    )


def gather_z(own):
    return lax.all_gather(own, "z", axis=0, tiled=True)


def start_rows(refs, dst, sems):
    each = dst.shape[0] // len(refs)
    for r, ref in enumerate(refs):
        pltpu.make_async_copy(ref, dst.at[pl.ds(r * each, each)], sems.at[r]).start()


def wait_rows(r, dst, sems, count=TP):
    each = dst.shape[0] // count
    part = dst.at[pl.ds(pl.multiple_of(r * each, each), each)]
    pltpu.make_async_copy(part, part, sems.at[r]).wait()


def fold_order():
    old = jnp.arange(QW, dtype=jnp.int32)
    new = (old // HALF) % 2 * (GROUP * HALF) + old // HD * HALF + old % HALF
    return (new[:, None] == jnp.arange(QW, dtype=jnp.int32)[None, :]).astype(BF)


def cut_attn_kernel(w_ref, perm_ref, out):
    kv_cols = KV * HD
    for i in range(TP):
        q = jnp.dot(w_ref[:, QW * i : QW * (i + 1)], perm_ref[...], preferred_element_type=F32)
        out[i, :, :QW] = q.astype(BF)
        k = w_ref[:, D + HD * i : D + HD * (i + 1)]
        v = w_ref[:, D + kv_cols + HD * i : D + kv_cols + HD * (i + 1)]
        out[i, :, QW : QW + 2 * HD] = jnp.concatenate([k, v], axis=1)
        out[i, :, QW + 2 * HD :] = w_ref[:, D + 2 * kv_cols + QW * i : D + 2 * kv_cols + QW * (i + 1)]


def cut_attn(w_attn, perm):
    rows = w_attn.shape[0]
    return pl.pallas_call(
        cut_attn_kernel,
        out_shape=jax.ShapeDtypeStruct((TP, rows, AW), BF),
        in_specs=[VMEM, VMEM],
        out_specs=VMEM,
        cost_estimate=cost(0, 2 * w_attn.size * 2),
        name="cut_attn",
    )(w_attn, perm)


def cut_ffn_kernel(w_ref, *outs):
    for k, width in enumerate(WIDTHS):
        for i in range(TP):
            for n in range(3):
                at = n * FF + STARTS[k] + i * width
                outs[k][i, :, n * width : (n + 1) * width] = w_ref[:, at : at + width]


def cut_ffn(w_ffn):
    rows = w_ffn.shape[0]
    return pl.pallas_call(
        cut_ffn_kernel,
        out_shape=[jax.ShapeDtypeStruct((TP, rows, 3 * width), BF) for width in WIDTHS],
        in_specs=[VMEM],
        out_specs=[VMEM] * CHUNKS,
        cost_estimate=cost(0, 2 * w_ffn.size * 2),
        compiler_params=BIG,
        name="cut_ffn",
    )(w_ffn)


def paste_ffn_kernel(*refs):
    pieces, w, out, term = refs[:CHUNKS], *refs[CHUNKS:]
    each = min(WIDTHS)
    total = jnp.zeros((w.shape[0], each), F32)
    for k, width in enumerate(WIDTHS):
        for i in range(TP):
            for n in range(3):
                for part in range(0, width, each):
                    at = n * FF + STARTS[k] + i * width + part
                    grad = pieces[k][i, :, n * width + part : n * width + part + each].astype(F32)
                    out[:, at : at + each] = grad
                    if n < 2:
                        total += grad * w[:, at : at + each].astype(F32)
    term[...] = jnp.sum(total, axis=-1, keepdims=True)


def paste_ffn(pieces, w_ffn):
    rows = w_ffn.shape[0]
    return pl.pallas_call(
        paste_ffn_kernel,
        out_shape=(jax.ShapeDtypeStruct(w_ffn.shape, F32), jax.ShapeDtypeStruct((rows, 1), F32)),
        in_specs=[VMEM] * (CHUNKS + 1),
        out_specs=(VMEM, VMEM),
        cost_estimate=cost(0, 8 * w_ffn.size),
        compiler_params=BIG,
        name="paste_ffn",
    )(*pieces, w_ffn)


def paste_attn_kernel(piece, w, perm, out, term):
    kv_cols = KV * HD
    ones = jnp.zeros((w.shape[0], QW), F32)
    small = jnp.zeros((w.shape[0], HD), F32)
    for i in range(TP):
        q = mm(piece[i, :, :QW], perm[...], NT)
        out[:, QW * i : QW * (i + 1)] = q
        ones += q * w[:, QW * i : QW * (i + 1)].astype(F32)
        kv = piece[i, :, QW : QW + 2 * HD].astype(F32)
        for at, part in ((D + HD * i, kv[:, :HD]), (D + kv_cols + HD * i, kv[:, HD:])):
            out[:, at : at + HD] = part
            small += part * w[:, at : at + HD].astype(F32)
        at = D + 2 * kv_cols + QW * i
        out[:, at : at + QW] = piece[i, :, QW + 2 * HD :].astype(F32)
    term[...] = jnp.sum(ones, axis=-1, keepdims=True) + jnp.sum(small, axis=-1, keepdims=True)


def paste_attn(piece, w_attn, perm):
    rows = w_attn.shape[0]
    return pl.pallas_call(
        paste_attn_kernel,
        out_shape=(jax.ShapeDtypeStruct(w_attn.shape, F32), jax.ShapeDtypeStruct((rows, 1), F32)),
        in_specs=[VMEM] * 3,
        out_specs=(VMEM, VMEM),
        cost_estimate=cost(0, 8 * w_attn.size),
        compiler_params=BIG,
        name="paste_attn",
    )(piece, w_attn, perm)


def turn_kernel(x, out):
    rows = out.shape[1]
    turned = x[...].astype(F32).T.astype(BF)
    for i in range(TP):
        out[i] = turned[rows * i : rows * (i + 1)]


def turn(x):
    cols, wide = x.shape
    return pl.pallas_call(
        turn_kernel,
        out_shape=jax.ShapeDtypeStruct((TP, wide // TP, cols), BF),
        in_specs=[VMEM],
        out_specs=VMEM,
        cost_estimate=cost(0, 4 * x.size),
        compiler_params=BIG,
        name="turn",
    )(x)


def qkv_kernel(count, *refs):
    blocks = refs[:count]
    gain, w_all, cos, sin, n1, q_out, kv_out, x_s, w_s, sems, w_sem = refs[count:]
    w_copy = pltpu.make_async_copy(w_all.at[:, pl.ds(0, w_s.shape[1]), pl.ds(0, w_s.shape[2])], w_s, w_sem)
    w_copy.start()
    start_rows(blocks, x_s, sems)
    each = x_s.shape[0] // count
    lane = lax.broadcasted_iota(jnp.int32, (each, 2 * HD), 1)
    w_copy.wait()

    def step(r, carry):
        at = pl.ds(pl.multiple_of(r * each, each), each)
        wait_rows(r, x_s, sems, count)
        x = x_s[at, :].astype(F32)
        scale = lax.rsqrt(jnp.mean(x * x, axis=-1, keepdims=True) + NORM_EPS)
        normed = (x * scale * gain[...]).astype(BF)
        n1[at, :] = normed
        qkv = jnp.dot(normed, w_s[...].reshape(D, QW + 2 * HD), preferred_element_type=F32)
        c, s = cos[at, :], sin[at, :]
        a, b = qkv[:, : QW // 2], qkv[:, QW // 2 : QW]
        q_out[at, : QW // 2] = (a * c - b * s).astype(BF)
        q_out[at, QW // 2 :] = (b * c + a * s).astype(BF)
        kv = qkv[:, QW:]
        ahead = pltpu.roll(kv, 2 * HD - HALF, 1)
        behind = pltpu.roll(kv, HALF, 1)
        turned = kv * c + jnp.where(lane < HALF, -ahead, behind) * s
        kv_out[at, :] = jnp.where(lane < HD, turned, kv).astype(BF)
        return carry

    lax.fori_loop(0, count, step, 0)


def norm_qkv(blocks, gain, w_all, cos, sin):
    each = w_all.shape[1] - EXTRA
    tokens = cos.shape[0]
    return pl.pallas_call(
        functools.partial(qkv_kernel, len(blocks)),
        out_shape=(
            jax.ShapeDtypeStruct((tokens, D), BF),
            jax.ShapeDtypeStruct((tokens, QW), BF),
            jax.ShapeDtypeStruct((tokens, 2 * HD), BF),
        ),
        in_specs=[ANY] * len(blocks) + [VMEM, ANY, VMEM, VMEM],
        out_specs=(VMEM, VMEM, VMEM),
        scratch_shapes=[
            pltpu.VMEM((tokens, D), BF),
            pltpu.VMEM((w_all.shape[0], each, QW + 2 * HD), BF),
            pltpu.SemaphoreType.DMA((len(blocks),)),
            pltpu.SemaphoreType.DMA,
        ],
        cost_estimate=cost(2 * tokens * D * (QW + 2 * HD), 4 * tokens * D),
        compiler_params=BIG,
        name="norm_qkv",
    )(*blocks, gain, w_all, cos, sin)


def spread_kv():
    src = jnp.arange(2 * HD, dtype=jnp.int32)[:, None]
    col = jnp.arange(QW, dtype=jnp.int32)[None, :]
    key = (src == col // (GROUP * HALF) * HALF + col % HALF).astype(BF)
    value = (src == HD + col % HD).astype(BF)
    return key, value


def attend_kernel(prev_at, index, q_ref, prev_ref, here_ref, lo_ref, ek, ev, o_ref, o_index_ref):
    tok = q_ref.shape[0]
    two = jnp.concatenate([prev_ref[...], here_ref[...]], axis=0)
    keys = jnp.dot(two, ek[...], preferred_element_type=F32).astype(BF)
    values = jnp.dot(two, ev[...], preferred_element_type=F32).astype(BF)
    q = q_ref[...]
    key_at = lax.broadcasted_iota(jnp.int32, (tok, 2 * tok), 1)
    row_at = lax.broadcasted_iota(jnp.int32, (tok, 2 * tok), 0)
    allowed = (lo_ref[...] <= key_at) & (key_at <= row_at + tok)
    q_lane = lax.broadcasted_iota(jnp.int32, (tok, QW), 1)
    v_lane = lax.broadcasted_iota(jnp.int32, (2 * tok, QW), 1)
    total = jnp.zeros((tok, QW), F32)
    for h in range(GROUP):
        mine = jnp.where((q_lane // HALF) % GROUP == h, q, jnp.zeros_like(q))
        s = jnp.where(allowed, mm(mine, keys, NT) * SCALE, -1e30)
        expo = jnp.exp(s - jnp.max(s, axis=-1, keepdims=True))
        probs = (expo / jnp.sum(expo, axis=-1, keepdims=True)).astype(BF)
        total += mm(probs, jnp.where(v_lane // HD == h, values, jnp.zeros_like(values)), NN)
    o_ref[...] = total.astype(BF)
    o_index_ref[0] = o_ref[...]


def attend(prev_at, index, q, kv9, lo_col, ek, ev):
    tokens = q.shape[0]
    tok = tokens // TP
    full = lambda shape: pl.BlockSpec(shape, lambda r, p, i: (0, 0))
    return pl.pallas_call(
        attend_kernel,
        out_shape=(jax.ShapeDtypeStruct((tokens, QW), BF), jax.ShapeDtypeStruct((TP, tok, QW), BF)),
        grid_spec=pltpu.PrefetchScalarGridSpec(
            num_scalar_prefetch=2,
            grid=(TP,),
            in_specs=[
                pl.BlockSpec((tok, QW), lambda r, p, i: (r, 0)),
                pl.BlockSpec((tok, 2 * HD), lambda r, p, i: (p[r], 0)),
                pl.BlockSpec((tok, 2 * HD), lambda r, p, i: (r, 0)),
                pl.BlockSpec((tok, 1), lambda r, p, i: (r, 0)),
                full((2 * HD, QW)),
                full((2 * HD, QW)),
            ],
            out_specs=(
                pl.BlockSpec((tok, QW), lambda r, p, i: (r, 0)),
                pl.BlockSpec((1, tok, QW), lambda r, p, i: (i[r], 0, 0)),
            ),
        ),
        cost_estimate=cost(4 * tokens * 2 * tok * QW * GROUP, 4 * tokens * QW),
        compiler_params=BIG,
        name="attend",
    )(prev_at, index, q, kv9, kv9, lo_col, ek, ev)


def attend_back_kernel(here_at, prev_at, q_ref, do_ref, prev_ref, here_ref, lo_ref, cos, sin, ek, ev, dq_ref, dkv_ref, carry):
    step = pl.program_id(0)
    tok = q_ref.shape[0]

    @pl.when(step == 0)
    def _():
        carry[...] = jnp.zeros_like(carry)

    @pl.when(step < TP)
    def _():
        two = jnp.concatenate([prev_ref[...], here_ref[...]], axis=0)
        keys = jnp.dot(two, ek[...], preferred_element_type=F32).astype(BF)
        values = jnp.dot(two, ev[...], preferred_element_type=F32).astype(BF)
        q, d_o = q_ref[...], do_ref[0]
        key_at = lax.broadcasted_iota(jnp.int32, (2 * tok, tok), 0)
        row_at = lax.broadcasted_iota(jnp.int32, (2 * tok, tok), 1)
        allowed = (lo_ref[0] <= key_at) & (key_at <= row_at + tok)
        lane = lax.broadcasted_iota(jnp.int32, (tok, QW), 1)
        key_lane = lax.broadcasted_iota(jnp.int32, (2 * tok, QW), 1)
        d_q = jnp.zeros((tok, QW), F32)
        d_k = jnp.zeros((2 * tok, QW), F32)
        d_v = jnp.zeros((2 * tok, QW), F32)
        for h in range(GROUP):
            q_h = jnp.where((lane // HALF) % GROUP == h, q, jnp.zeros_like(q))
            do_h = jnp.where(lane // HD == h, d_o, jnp.zeros_like(d_o))
            k_h = jnp.where((key_lane // HALF) % GROUP == h, keys, jnp.zeros_like(keys))
            s = jnp.where(allowed, mm(keys, q_h, NT) * SCALE, -1e30)
            expo = jnp.exp(s - jnp.max(s, axis=0, keepdims=True))
            probs = expo / jnp.sum(expo, axis=0, keepdims=True)
            d_p = mm(values, do_h, NT)
            shift = jnp.sum(d_p * probs, axis=0, keepdims=True)
            d_s = (probs * (d_p - shift)).astype(BF)
            d_v += mm(probs.astype(BF), do_h, NN)
            d_k += mm(d_s, q_h, NN)
            d_q += mm(d_s, k_h, TN)
        d_q = d_q * SCALE
        a, b = d_q[:, : QW // 2], d_q[:, QW // 2 :]
        c, s = cos[...], sin[...]
        dq_ref[:, : QW // 2] = (a * c + b * s).astype(BF)
        dq_ref[:, QW // 2 :] = (b * c - a * s).astype(BF)
        d_k = d_k * SCALE

        def fold(v):
            v = v + pltpu.roll(v, HD, 1)
            return v + pltpu.roll(v, HALF, 1)

        first, second = fold(d_k[:, : QW // 2]), fold(d_k[:, QW // 2 :])
        whole = d_v[:, : QW // 2] + d_v[:, QW // 2 :]
        whole = whole + pltpu.roll(whole, HD, 1)
        low = lax.broadcasted_iota(jnp.int32, (2 * tok, 2 * HD), 1)
        d_kv = jnp.where(low < HALF, first, jnp.where(low < HD, second, whole))
        dkv_ref[...] = carry[...] + d_kv[:tok]
        carry[...] = d_kv[tok:]

    @pl.when(step == TP)
    def _():
        dkv_ref[...] = carry[...]


def attend_back(here_at, prev_at, q, d_o, kv9, lo_row, cos, sin, ek, ev):
    tokens = q.shape[0]
    tok = tokens // TP
    last = TP - 1
    here = lambda cols: pl.BlockSpec((tok, cols), lambda s, h, p: (h[jnp.minimum(s, last)], 0))
    full = lambda shape: pl.BlockSpec(shape, lambda s, h, p: (0, 0))
    return pl.pallas_call(
        attend_back_kernel,
        out_shape=(
            jax.ShapeDtypeStruct((tokens, QW), BF),
            jax.ShapeDtypeStruct((tokens + tok, 2 * HD), F32),
        ),
        grid_spec=pltpu.PrefetchScalarGridSpec(
            num_scalar_prefetch=2,
            grid=(TP + 1,),
            in_specs=[
                here(QW),
                pl.BlockSpec((1, tok, QW), lambda s, h, p: (jnp.minimum(s, last), 0, 0)),
                pl.BlockSpec((tok, 2 * HD), lambda s, h, p: (p[jnp.minimum(s, last)], 0)),
                here(2 * HD),
                pl.BlockSpec((1, 1, tok), lambda s, h, p: (h[jnp.minimum(s, last)], 0, 0)),
                here(2 * HD),
                here(2 * HD),
                full((2 * HD, QW)),
                full((2 * HD, QW)),
            ],
            out_specs=(
                here(QW),
                pl.BlockSpec((tok, 2 * HD), lambda s, h, p: (jnp.where(s == 0, TP, h[jnp.maximum(s - 1, 0)]), 0)),
            ),
            scratch_shapes=[pltpu.VMEM((tok, 2 * HD), F32)],
        ),
        cost_estimate=cost(10 * tokens * 2 * tok * QW * GROUP, 8 * tokens * QW),
        compiler_params=BIG,
        name="attend_back",
    )(here_at, prev_at, q, d_o, kv9, kv9, lo_row, cos, sin, ek, ev)


def ffn_forward(r, n2, dy, w, act_out, dgu_out, flat):
    each = n2.shape[0] // TP
    width = act_out.shape[1]
    two = 2 * width
    at = pl.ds(pl.multiple_of(r * each, each), each)
    gate_up = jnp.dot(n2[at, :], w[:, :two], preferred_element_type=F32)
    d_act = jnp.dot(dy[at, :], w[:, two:], preferred_element_type=F32)
    g, u = gate_up[:, :width], gate_up[:, width:]
    sg = jax.nn.sigmoid(g)
    gs = g * sg
    act = (gs * u).astype(BF)
    d_g = (d_act * u * (sg * (1.0 + g * (1.0 - sg)))).astype(BF)
    d_u = (d_act * gs).astype(BF)
    act_out[at, :] = act
    dgu_out[at, :width] = d_g
    dgu_out[at, width:] = d_u
    flat[:width, at] = d_g.T
    flat[width:two, at] = d_u.T
    flat[two:, at] = act.T


def ffn_back(flat, n2, dy, grad_out, held, out_sems):
    planes, wide, cols = grad_out.shape
    two = 2 * wide // 3

    def leave(z):
        return pltpu.make_async_copy(held.at[lax.rem(z, 2)], grad_out.at[z], out_sems.at[lax.rem(z, 2)])

    def back(z, carry):
        at = pl.ds(pl.multiple_of(z * cols, cols), cols)
        slot = lax.rem(z, 2)

        @pl.when(z >= 2)
        def _():
            leave(z - 2).wait()

        held[slot, :two, :] = jnp.dot(flat[:two, :], n2[:, at], preferred_element_type=F32).astype(BF)
        held[slot, two:, :] = jnp.dot(flat[two:, :], dy[:, at], preferred_element_type=F32).astype(BF)
        leave(z).start()
        return carry

    lax.fori_loop(0, planes, back, 0)
    leave(planes - 2).wait()
    leave(planes - 1).wait()


def ffn_kernel(*refs):
    n2_blocks, dy_blocks = refs[:TP], refs[TP : 2 * TP]
    w, act_out, dgu_out, grad_out, n2, dy, flat, held, n2_sems, dy_sems, out_sems = refs[2 * TP :]
    start_rows(n2_blocks, n2, n2_sems)
    start_rows(dy_blocks, dy, dy_sems)

    def forward(r, carry):
        wait_rows(r, n2, n2_sems)
        wait_rows(r, dy, dy_sems)
        ffn_forward(r, n2, dy, w, act_out, dgu_out, flat)
        return carry

    lax.fori_loop(0, TP, forward, 0)
    ffn_back(flat, n2, dy, grad_out, held, out_sems)


def ffn_forward_kernel(*refs):
    n2_blocks, dy_blocks = refs[:TP], refs[TP : 2 * TP]
    w, act_out, dgu_out, flat, n2, dy, n2_sems, dy_sems = refs[2 * TP :]
    start_rows(n2_blocks, n2, n2_sems)
    start_rows(dy_blocks, dy, dy_sems)

    def forward(r, carry):
        wait_rows(r, n2, n2_sems)
        wait_rows(r, dy, dy_sems)
        ffn_forward(r, n2, dy, w, act_out, dgu_out, flat)
        return carry

    lax.fori_loop(0, TP, forward, 0)


def ffn_back_kernel(*refs):
    n2_blocks, dy_blocks = refs[:TP], refs[TP : 2 * TP]
    flat, grad_out, n2, dy, held, n2_sems, dy_sems, out_sems = refs[2 * TP :]
    start_rows(n2_blocks, n2, n2_sems)
    start_rows(dy_blocks, dy, dy_sems)
    for r in range(TP):
        wait_rows(r, n2, n2_sems)
    for r in range(TP):
        wait_rows(r, dy, dy_sems)
    ffn_back(flat, n2, dy, grad_out, held, out_sems)


def ffn_call(kernel, n2_blocks, dy_blocks, last, outs, flops):
    tokens = TP * n2_blocks[0].shape[0]
    planes = lax.axis_size("z")
    wide = last.shape[1] if 2 not in outs or 0 in outs else last.shape[0]
    width = wide // 3
    shapes, specs, extra, sems = [], [], [], []
    if 0 in outs:
        shapes += [jax.ShapeDtypeStruct((tokens, width), BF), jax.ShapeDtypeStruct((tokens, 2 * width), BF)]
        specs += [VMEM, VMEM]
    if 1 in outs:
        shapes.append(jax.ShapeDtypeStruct((wide, tokens), BF))
        specs.append(VMEM)
    if 2 in outs:
        shapes.append(jax.ShapeDtypeStruct((planes, wide, D // planes), BF))
        specs.append(ANY)
        extra = ([pltpu.VMEM((wide, tokens), BF)] if 0 in outs else []) + [pltpu.VMEM((2, wide, D // planes), BF)]
        sems = [pltpu.SemaphoreType.DMA((2,))]
    return pl.pallas_call(
        kernel,
        out_shape=shapes,
        in_specs=[ANY] * (2 * TP) + [VMEM],
        out_specs=specs,
        scratch_shapes=[pltpu.VMEM((tokens, D), BF), pltpu.VMEM((tokens, D), BF)]
        + extra
        + [pltpu.SemaphoreType.DMA((TP,)), pltpu.SemaphoreType.DMA((TP,))]
        + sems,
        cost_estimate=cost(flops * tokens * D * width, 4 * tokens * D + 12 * width * D),
        compiler_params=BIG,
        name="ffn",
    )(*n2_blocks, *dy_blocks, last)


def down_kernel(parts, *refs):
    outs = refs[-2:]
    base = refs[2 * parts : -2]
    for at, out in enumerate(outs):
        term = base[at][0] if base else None
        for j in range(parts):
            more = mm(refs[j][0, at], refs[parts + j][...], NT)
            term = more if term is None else term + more
        out[0] = term.astype(out.dtype)


def down(parts, weights, last, groups, base=None, kind=BF):
    count = len(parts)
    tokens = parts[0].shape[0]
    tok = tokens // TP
    widths = [p.shape[1] for p in parts]
    columns = [w.shape[1] // width - 1 if last else 0 for w, width in zip(weights, widths)]
    pairs = [p.reshape(TP // 2, 2, tok, width) for p, width in zip(parts, widths)]
    rows = weights[0].shape[0]
    first, step = groups[0], groups[1] - groups[0]
    return pl.pallas_call(
        functools.partial(down_kernel, count),
        out_shape=[jax.ShapeDtypeStruct((len(groups), tok, rows), kind)] * 2,
        grid=(len(groups),),
        in_specs=[pl.BlockSpec((1, 2, tok, width), lambda s: (first + step * s, 0, 0, 0)) for width in widths]
        + [
            pl.BlockSpec((rows, width), lambda s, c=c: (0, c), pipeline_mode=pl.Buffered(1))
            for width, c in zip(widths, columns)
        ]
        + ([] if base is None else [pl.BlockSpec((1, tok, rows), lambda s: (first + step * s, 0, 0))] * 2),
        out_specs=[pl.BlockSpec((1, tok, rows), lambda s: (s, 0, 0))] * 2,
        cost_estimate=cost(4 * len(groups) * tok * sum(widths) * rows, rows * sum(widths) * 2 + len(groups) * tok * rows * 8),
        compiler_params=BIG,
        name="down",
    )(*pairs, *weights, *(() if base is None else base))


def start_wo(blocks, dst, sems):
    for r, ref in enumerate(blocks):
        pltpu.make_async_copy(ref, dst.at[r], sems.at[r]).start()


def wait_wo(r, dst, sems):
    pltpu.make_async_copy(dst.at[r], dst.at[r], sems.at[r]).wait()


def close_kernel(*refs):
    wo_blocks = refs[:TP]
    index, heads, x, gain, resid_out, n2_out, wo, sems = refs[TP:]
    start_wo(wo_blocks, wo, sems)
    y = x[...].astype(F32)
    for r in range(TP):
        wait_wo(r, wo, sems)
        y += mm(heads[index[r]], wo[r], NT)
    resid_out[...] = y
    n2_out[...] = (y * lax.rsqrt(jnp.mean(y * y, axis=-1, keepdims=True) + NORM_EPS) * gain[...]).astype(BF)


def close_attention(wo_blocks, index, heads, x, gain):
    tok = x.shape[0]
    return pl.pallas_call(
        close_kernel,
        out_shape=(jax.ShapeDtypeStruct((tok, D), F32), jax.ShapeDtypeStruct((tok, D), BF)),
        in_specs=[ANY] * TP + [SMEM] + [VMEM] * 3,
        out_specs=(VMEM, VMEM),
        scratch_shapes=[pltpu.VMEM((TP, D, QW), BF), pltpu.SemaphoreType.DMA((TP,))],
        cost_estimate=cost(2 * tok * D * D, 2 * D * D),
        compiler_params=BIG,
        name="close_attention",
    )(*wo_blocks, index, heads, x, gain)


def open_kernel(*refs):
    wo_blocks = refs[:TP]
    index, own, from_x, from_y, resid, dy, gain, back_out, att_out, heads, wo, sems = refs[TP:]
    start_wo(wo_blocks, wo, sems)
    d_n = own[...].astype(F32) + from_x[...].astype(F32) + from_y[...].astype(F32)
    y = resid[...]
    scale = lax.rsqrt(jnp.mean(y * y, axis=-1, keepdims=True) + NORM_EPS)
    unit = y * scale
    d_unit = d_n * gain[...]
    d_y = dy[...].astype(F32) + scale * (d_unit - unit * jnp.mean(d_unit * unit, axis=-1, keepdims=True))
    back_out[...] = d_y
    att_out[...] = d_y.astype(BF)
    att = att_out[...]
    for r in range(TP):
        wait_wo(r, wo, sems)
        heads[index[r]] = jnp.dot(att, wo[r], preferred_element_type=F32).astype(BF)


def open_attention(wo_blocks, index, terms, resid, dy, gain):
    tok = dy.shape[0]
    return pl.pallas_call(
        open_kernel,
        out_shape=(
            jax.ShapeDtypeStruct((tok, D), F32),
            jax.ShapeDtypeStruct((tok, D), BF),
            jax.ShapeDtypeStruct((TP, tok, QW), BF),
        ),
        in_specs=[ANY] * TP + [SMEM] + [VMEM] * 6,
        out_specs=(VMEM, VMEM, VMEM),
        scratch_shapes=[pltpu.VMEM((TP, D, QW), BF), pltpu.SemaphoreType.DMA((TP,))],
        cost_estimate=cost(2 * tok * D * D, 2 * D * D),
        compiler_params=BIG,
        name="open_attention",
    )(*wo_blocks, index, *terms, resid, dy, gain)


def turn_grad_kernel(count, *refs):
    blocks, left, out, rows, sems = refs[:count], *refs[count:]
    start_rows(blocks, rows, sems)
    for r in range(TP):
        wait_rows(r, rows, sems)
    planes, _, cols = out.shape

    def back(z, carry):
        at = pl.ds(pl.multiple_of(z * cols, cols), cols)
        out[z] = mm(left[...], rows[:, at], TN).astype(BF)
        return carry

    lax.fori_loop(0, planes, back, 0)


def turn_grad(left, blocks):
    tokens, cols = left.shape
    planes = lax.axis_size("z")
    return pl.pallas_call(
        functools.partial(turn_grad_kernel, len(blocks)),
        out_shape=jax.ShapeDtypeStruct((planes, cols, D // planes), BF),
        in_specs=[ANY] * len(blocks) + [VMEM],
        out_specs=VMEM,
        scratch_shapes=[pltpu.VMEM((tokens, D), BF), pltpu.SemaphoreType.DMA((TP,))],
        cost_estimate=cost(2 * tokens * D * cols, 2 * tokens * D),
        compiler_params=BIG,
        name="turn_grad",
    )(*blocks, left)


def to_pieces(pieces):
    rows, cols = pieces.shape[1:]
    return trade(pieces).reshape(TP * rows, cols)


def sum_z(grad):
    planes, cols, wide = grad.shape
    return lax.psum_scatter(grad.reshape(planes * cols, wide), "z", scatter_dimension=0, tiled=True)


def give_back(summed):
    return trade(turn(summed))


def by_plane(grad):
    planes = lax.axis_size("z")
    return grad.reshape(grad.shape[0], planes, D // planes).transpose(1, 0, 2)


def pick(blocks, at):
    return lax.dynamic_index_in_dim(blocks, at, 0, keepdims=False)


def on_device(hidden_in, segment_ids, w_attn, w_ffn, gains, out_grad):
    tok = hidden_in.shape[0]
    rows = w_attn.shape[0]
    me = lax.axis_index(PLANE)
    z = lax.axis_index("z")
    tokens = TP * tok
    steps = jnp.arange(TP, dtype=jnp.int32)
    rel = me ^ steps
    perm = fold_order()
    ek, ev = spread_kv()

    own_start = (z * TP + me) * tok
    own_lo = segment_ids - own_start + tok
    extra = jnp.zeros((EXTRA, AW), BF)
    extra = extra.at[0, : 2 * rows].set(gains.reshape(-1))
    extra = extra.at[1, :tok].set((own_lo // 2).astype(BF)).at[2, :tok].set((own_lo % 2).astype(BF))

    attn_pieces = cut_attn(w_attn, perm)
    attn_pieces = jnp.concatenate([attn_pieces, jnp.broadcast_to(extra, (TP, *extra.shape))], axis=1)
    attn_rows = to_pieces(attn_pieces)
    x_begun = gather_begin(hidden_in)
    pieces = cut_ffn(after(w_ffn, attn_rows))
    rows_0 = to_pieces(pieces[0])
    w_0 = gather_z(rows_0)
    x_blocks = gather_end(*x_begun)
    dy_begun = gather_begin(after(out_grad, *x_begun[1:]))
    attn_all = after(gather_z(attn_rows), rows_0).reshape(-1, rows + EXTRA, AW)
    w_own = attn_all[:, :rows].reshape(D, AW)
    wqkv, wo = w_own[:, : QW + 2 * HD], w_own[:, QW + 2 * HD :]
    gains_full = attn_all[:, rows, : 2 * rows].reshape(-1, 2, rows).transpose(1, 0, 2).reshape(2, D).astype(F32)

    plane_lo = attn_rows.reshape(TP, rows + EXTRA, -1)[:, rows + 1 : rows + 3, :tok].astype(jnp.int32)
    lo = jnp.take(2 * plane_lo[:, 0] + plane_lo[:, 1], rel, axis=0)
    positions = jnp.arange(tok, dtype=jnp.int32)[None] + tok - lo
    freqs = 1.0 / ROPE_BASE ** (jnp.arange(HALF, dtype=F32) * (2.0 / HD))
    angles = positions.reshape(tokens).astype(F32)[:, None] * freqs
    cosine = jnp.tile(jnp.cos(angles), (1, GROUP))
    sine = jnp.tile(jnp.sin(angles), (1, GROUP))

    early = 6
    halves = []
    for first, last in ((0, early), (early, TP)):
        at = slice(first * tok, last * tok)
        halves.append(norm_qkv(x_blocks[first:last], gains_full[:1], attn_all, cosine[at], sine[at]))
    (n1, q, kv), (n1_late, q_late, kv_late) = halves
    q, kv = jnp.concatenate([q, q_late], axis=0), jnp.concatenate([kv, kv_late], axis=0)
    wo_begun = gather_begin(wo)
    rows_1 = to_pieces(after(pieces[1], attn_all))
    q = after(q, rows_1, *wo_begun[1:], *dy_begun[1:])
    before = along_z(pick(kv.reshape(TP, tok, 2 * HD), me ^ (TP - 1)), 1)
    kv9 = jnp.concatenate([kv, before], axis=0)
    prev_at = jnp.where(rel == 0, TP, (rel - 1) ^ me)
    mixed, heads = attend(prev_at, rel, q, kv9, lo.reshape(tokens, 1), ek, ev)

    wo_blocks = gather_end(*wo_begun)
    heads = trade(heads)
    dy_blocks = gather_end(*after(dy_begun, mixed))
    w_1 = gather_z(rows_1)
    x_own = hidden_in.astype(F32)
    residual, normed_two = close_attention(wo_blocks, rel, heads, after(hidden_in, w_0), gains_full[1:])
    n2_blocks = gather_plane(normed_two)

    act_0, d_gu_0, grad_0 = ffn_call(ffn_kernel, n2_blocks, dy_blocks, w_0, (0, 2), 18)
    so_far = down([d_gu_0], [w_0], False, (0, 1, 2, 3), kind=F32)
    sum_0 = sum_z(grad_0)
    act_1, d_gu_1, flat_1 = ffn_call(ffn_forward_kernel, n2_blocks, dy_blocks, after(w_1, so_far[0]), (0, 1), 9)
    d_n2_parts = {groups: down([d_gu_1], [w_1], False, groups, so_far) for groups in ((3, 2), (1, 0))}
    d_n2_terms, unused = scatter_plane(d_n2_parts.get)
    (grad_1,) = ffn_call(ffn_back_kernel, n2_blocks, dy_blocks, after(flat_1, d_n2_parts[1, 0][0]), (2,), 9)
    sum_1 = sum_z(grad_1)
    acts, w_all = [after(act_0, grad_1), act_1], [w_0, w_1]
    f_parts = {groups: down(acts, w_all, True, groups) for groups in ((3, 2), (1, 0))}
    d_n2_terms = after(d_n2_terms, *f_parts.values())
    d_resid, d_att, d_heads = open_attention(wo_blocks, rel, d_n2_terms, residual, out_grad, gains_full[1:])
    d_o = trade(d_heads)
    d_att_begun = gather_begin(after(d_att, d_o))
    here_at = me ^ steps
    prev_abs = jnp.where(steps == 0, TP, (steps - 1) ^ me)
    turned_0 = turn(sum_0)
    d_q, d_kv9 = attend_back(here_at, prev_abs, q, after(d_o, turned_0), kv9, lo.reshape(TP, 1, tok), cosine, sine, ek, ev)
    f_terms, unused = scatter_plane(lambda groups: after(f_parts[groups], d_heads), (d_q,))
    hidden_out = (residual + total(*f_terms)).astype(BF)
    d_att_blocks = gather_end(*after(d_att_begun, d_q))
    piece_0 = trade(turned_0)
    wo_grad = turn_grad(after(mixed, piece_0), d_att_blocks)
    back = along_z(d_kv9[tokens:].astype(BF), -1)
    last = me ^ (TP - 1)
    d_kv = d_kv9[:tokens].reshape(TP, tok, 2 * HD)
    d_kv = jnp.where((steps == last)[:, None, None], d_kv + back.astype(F32)[None], d_kv).reshape(tokens, 2 * HD)
    c, s = cosine[:, :HALF], sine[:, :HALF]
    a, b = d_kv[:, :HALF], d_kv[:, HALF:HD]
    d_qkv = jnp.concatenate(
        [d_q, (a * c + b * s).astype(BF), (b * c - a * s).astype(BF), d_kv[:, HD:].astype(BF)], axis=1
    )
    cut = early * tok
    qkv_grad = by_plane((mm(d_qkv[:cut], n1, TN) + mm(d_qkv[cut:], n1_late, TN)).astype(BF))
    attn_sum = jnp.concatenate([qkv_grad, wo_grad], axis=1)
    turned = turn(sum_z(attn_sum))
    attn_back = trade(turned)
    d_qkv = after(d_qkv, attn_sum, *f_terms)
    d_n1_terms, unused = scatter_plane(lambda groups: down([d_qkv], [wqkv], False, groups))
    d_normed = total(*d_n1_terms)
    pieces = [piece_0, give_back(sum_1)]
    pieces[1] = after(pieces[1], turned)
    scale = lax.rsqrt(jnp.mean(x_own * x_own, axis=-1, keepdims=True) + NORM_EPS)
    unit = x_own * scale
    d_unit = d_normed * gains_full[0]
    in_grad = d_resid + scale * (d_unit - unit * jnp.mean(d_unit * unit, axis=-1, keepdims=True))
    ffn_grad, term_two = paste_ffn(pieces, w_ffn)
    attn_grad, term_one = paste_attn(attn_back, w_attn, perm)
    gains_grad = jnp.concatenate([term_one, term_two], axis=1).T / gains.astype(F32)
    return hidden_out, in_grad.astype(BF), attn_grad, ffn_grad, gains_grad


def solution(mesh):
    fine = Mesh(mesh.devices.reshape(-1, 2, 2, 2), EVERY)
    rows = P(EVERY, None)
    in_specs = (rows, P(EVERY), rows, rows, P(None, EVERY), rows)
    out_specs = (rows, rows, rows, rows, P(None, EVERY))
    return jax.shard_map(
        on_device, mesh=fine, in_specs=in_specs, out_specs=out_specs, check_vma=False
    )
```

```python
import functools

import jax
import jax.numpy as jnp
from jax import lax
from jax.experimental import pallas as pl
from jax.experimental.pallas import tpu as pltpu
from jax.sharding import Mesh, PartitionSpec as P

D = 2048
H = 32
KV = 8
HD = 64
FF = 8192
GROUP = H // KV
TP = 8
WIDTHS = (512, 512)
CHUNKS = len(WIDTHS)
HALF = HD // 2
QW = GROUP * HD
STARTS = [TP * sum(WIDTHS[:k]) for k in range(CHUNKS)]
EXTRA = 8
AW = 2 * QW + 2 * HD

NORM_EPS = 1e-05
ROPE_BASE = 500000.0
SCALE = HD ** (-0.5)

PLANE = ("y", "x", "c")
EVERY = ("z", "y", "x", "c")
BF = jnp.bfloat16
F32 = jnp.float32
ANY = pl.BlockSpec(memory_space=pl.ANY)
VMEM = pl.BlockSpec(memory_space=pltpu.VMEM)
SMEM = pl.BlockSpec(memory_space=pltpu.SMEM)
BIG = pltpu.CompilerParams(vmem_limit_bytes=56 * 1024 * 1024)


def cost(flops, size):
    return pl.CostEstimate(flops=int(flops), bytes_accessed=int(size), transcendentals=0)


def mm(left, right, dims):
    return lax.dot_general(left, right, (dims, ((), ())), preferred_element_type=F32)


NN = ((1,), (0,))
NT = ((1,), (1,))
TN = ((0,), (0,))


def after(value, *first):
    return lax.optimization_barrier((value, *first))[0]


def rms_norm(values, scales):
    return values * lax.rsqrt(jnp.mean(values * values, axis=-1, keepdims=True) + NORM_EPS) * scales


def swap(value, rel):
    return lax.ppermute(value, PLANE, [(i, i ^ rel) for i in range(TP)])


def swap_across(value):
    return lax.ppermute(value, PLANE, [(i, i ^ (2 + 2 * (i % 2))) for i in range(TP)])


def on_first():
    return lax.axis_index(PLANE) % 2 == 0


def gather_begin(own):
    return own, swap(own, 2), swap(own, 4), swap(own, 1)


def gather_end(own, from_x, from_y, from_c):
    across = swap_across(jnp.where(on_first(), from_y, from_x))
    return [own, from_c, from_x, swap(from_x, 1), from_y, swap(from_y, 1), across, swap(across, 1)]


def gather_plane(own):
    return gather_end(*gather_begin(own))


def add(left, right):
    return (left.astype(F32) + right.astype(F32)).astype(BF)


def scatter_plane(part, wait=()):
    even, odd = part((3, 2))
    both = add(even, after(swap(odd, 1), *wait))
    across, over_y = swap_across(both[0]), both[1]
    even, odd = part((1, 0))
    both = add(even, after(swap(odd, 1), *wait))
    over_x, own = both[0], both[1]
    first = on_first()
    over_x = jnp.where(first, over_x, add(over_x, across))
    over_y = jnp.where(first, add(over_y, across), over_y)
    return (own, swap(over_x, 2), swap(over_y, 4)), (over_x, over_y)


def total(own, from_x, from_y):
    return own.astype(F32) + from_x.astype(F32) + from_y.astype(F32)


def trade(blocks):
    return lax.all_to_all(blocks, PLANE, 0, 0, tiled=True)


def along_z(value, steps):
    count = lax.axis_size("z")
    return lax.ppermute(
        value, "z", [(i, i + steps) for i in range(count) if 0 <= i + steps < count]
    )


def gather_z(own):
    return lax.all_gather(own, "z", axis=0, tiled=True)


def start_rows(refs, dst, sems):
    each = dst.shape[0] // len(refs)
    for r, ref in enumerate(refs):
        pltpu.make_async_copy(ref, dst.at[pl.ds(r * each, each)], sems.at[r]).start()


def wait_rows(r, dst, sems, count=TP):
    each = dst.shape[0] // count
    part = dst.at[pl.ds(pl.multiple_of(r * each, each), each)]
    pltpu.make_async_copy(part, part, sems.at[r]).wait()


def fold_order():
    old = jnp.arange(QW, dtype=jnp.int32)
    new = (old // HALF) % 2 * (GROUP * HALF) + old // HD * HALF + old % HALF
    return (new[:, None] == jnp.arange(QW, dtype=jnp.int32)[None, :]).astype(BF)


def cut_attn_kernel(w_ref, perm_ref, out):
    kv_cols = KV * HD
    for i in range(TP):
        q = jnp.dot(w_ref[:, QW * i : QW * (i + 1)], perm_ref[...], preferred_element_type=F32)
        out[i, :, :QW] = q.astype(BF)
        k = w_ref[:, D + HD * i : D + HD * (i + 1)]
        v = w_ref[:, D + kv_cols + HD * i : D + kv_cols + HD * (i + 1)]
        out[i, :, QW : QW + 2 * HD] = jnp.concatenate([k, v], axis=1)
        out[i, :, QW + 2 * HD :] = w_ref[:, D + 2 * kv_cols + QW * i : D + 2 * kv_cols + QW * (i + 1)]


def cut_attn(w_attn, perm):
    rows = w_attn.shape[0]
    return pl.pallas_call(
        cut_attn_kernel,
        out_shape=jax.ShapeDtypeStruct((TP, rows, AW), BF),
        in_specs=[VMEM, VMEM],
        out_specs=VMEM,
        cost_estimate=cost(0, 2 * w_attn.size * 2),
        name="cut_attn",
    )(w_attn, perm)


def cut_ffn_kernel(w_ref, *outs):
    for k, width in enumerate(WIDTHS):
        for i in range(TP):
            for n in range(3):
                at = n * FF + STARTS[k] + i * width
                outs[k][i, :, n * width : (n + 1) * width] = w_ref[:, at : at + width]


def cut_ffn(w_ffn):
    rows = w_ffn.shape[0]
    return pl.pallas_call(
        cut_ffn_kernel,
        out_shape=[jax.ShapeDtypeStruct((TP, rows, 3 * width), BF) for width in WIDTHS],
        in_specs=[VMEM],
        out_specs=[VMEM] * CHUNKS,
        cost_estimate=cost(0, 2 * w_ffn.size * 2),
        compiler_params=BIG,
        name="cut_ffn",
    )(w_ffn)


def paste_ffn_kernel(*refs):
    pieces, w, out, term = refs[:CHUNKS], *refs[CHUNKS:]
    each = min(WIDTHS)
    total = jnp.zeros((w.shape[0], each), F32)
    for k, width in enumerate(WIDTHS):
        for i in range(TP):
            for n in range(3):
                for part in range(0, width, each):
                    at = n * FF + STARTS[k] + i * width + part
                    grad = pieces[k][i, :, n * width + part : n * width + part + each].astype(F32)
                    out[:, at : at + each] = grad
                    if n < 2:
                        total += grad * w[:, at : at + each].astype(F32)
    term[...] = jnp.sum(total, axis=-1, keepdims=True)


def paste_ffn(pieces, w_ffn):
    rows = w_ffn.shape[0]
    return pl.pallas_call(
        paste_ffn_kernel,
        out_shape=(jax.ShapeDtypeStruct(w_ffn.shape, F32), jax.ShapeDtypeStruct((rows, 1), F32)),
        in_specs=[VMEM] * (CHUNKS + 1),
        out_specs=(VMEM, VMEM),
        cost_estimate=cost(0, 8 * w_ffn.size),
        compiler_params=BIG,
        name="paste_ffn",
    )(*pieces, w_ffn)


def paste_attn_kernel(piece, w, perm, out, term):
    kv_cols = KV * HD
    ones = jnp.zeros((w.shape[0], QW), F32)
    small = jnp.zeros((w.shape[0], HD), F32)
    for i in range(TP):
        q = mm(piece[i, :, :QW], perm[...], NT)
        out[:, QW * i : QW * (i + 1)] = q
        ones += q * w[:, QW * i : QW * (i + 1)].astype(F32)
        kv = piece[i, :, QW : QW + 2 * HD].astype(F32)
        for at, part in ((D + HD * i, kv[:, :HD]), (D + kv_cols + HD * i, kv[:, HD:])):
            out[:, at : at + HD] = part
            small += part * w[:, at : at + HD].astype(F32)
        at = D + 2 * kv_cols + QW * i
        out[:, at : at + QW] = piece[i, :, QW + 2 * HD :].astype(F32)
    term[...] = jnp.sum(ones, axis=-1, keepdims=True) + jnp.sum(small, axis=-1, keepdims=True)


def paste_attn(piece, w_attn, perm):
    rows = w_attn.shape[0]
    return pl.pallas_call(
        paste_attn_kernel,
        out_shape=(jax.ShapeDtypeStruct(w_attn.shape, F32), jax.ShapeDtypeStruct((rows, 1), F32)),
        in_specs=[VMEM] * 3,
        out_specs=(VMEM, VMEM),
        cost_estimate=cost(0, 8 * w_attn.size),
        compiler_params=BIG,
        name="paste_attn",
    )(piece, w_attn, perm)


def turn_kernel(x, out):
    rows = out.shape[1]
    turned = x[...].astype(F32).T.astype(BF)
    for i in range(TP):
        out[i] = turned[rows * i : rows * (i + 1)]


def turn(x):
    cols, wide = x.shape
    return pl.pallas_call(
        turn_kernel,
        out_shape=jax.ShapeDtypeStruct((TP, wide // TP, cols), BF),
        in_specs=[VMEM],
        out_specs=VMEM,
        cost_estimate=cost(0, 4 * x.size),
        compiler_params=BIG,
        name="turn",
    )(x)


def qkv_kernel(count, *refs):
    blocks = refs[:count]
    gain, w_all, cos, sin, n1, q_out, kv_out, x_s, w_s, sems, w_sem = refs[count:]
    w_copy = pltpu.make_async_copy(w_all.at[:, pl.ds(0, w_s.shape[1]), pl.ds(0, w_s.shape[2])], w_s, w_sem)
    w_copy.start()
    start_rows(blocks, x_s, sems)
    each = x_s.shape[0] // count
    lane = lax.broadcasted_iota(jnp.int32, (each, 2 * HD), 1)
    w_copy.wait()

    def step(r, carry):
        at = pl.ds(pl.multiple_of(r * each, each), each)
        wait_rows(r, x_s, sems, count)
        x = x_s[at, :].astype(F32)
        scale = lax.rsqrt(jnp.mean(x * x, axis=-1, keepdims=True) + NORM_EPS)
        normed = (x * scale * gain[...]).astype(BF)
        n1[at, :] = normed
        qkv = jnp.dot(normed, w_s[...].reshape(D, QW + 2 * HD), preferred_element_type=F32)
        c, s = cos[at, :], sin[at, :]
        a, b = qkv[:, : QW // 2], qkv[:, QW // 2 : QW]
        q_out[at, : QW // 2] = (a * c - b * s).astype(BF)
        q_out[at, QW // 2 :] = (b * c + a * s).astype(BF)
        kv = qkv[:, QW:]
        ahead = pltpu.roll(kv, 2 * HD - HALF, 1)
        behind = pltpu.roll(kv, HALF, 1)
        turned = kv * c + jnp.where(lane < HALF, -ahead, behind) * s
        kv_out[at, :] = jnp.where(lane < HD, turned, kv).astype(BF)
        return carry

    lax.fori_loop(0, count, step, 0)


def norm_qkv(blocks, gain, w_all, cos, sin):
    each = w_all.shape[1] - EXTRA
    tokens = cos.shape[0]
    return pl.pallas_call(
        functools.partial(qkv_kernel, len(blocks)),
        out_shape=(
            jax.ShapeDtypeStruct((tokens, D), BF),
            jax.ShapeDtypeStruct((tokens, QW), BF),
            jax.ShapeDtypeStruct((tokens, 2 * HD), BF),
        ),
        in_specs=[ANY] * len(blocks) + [VMEM, ANY, VMEM, VMEM],
        out_specs=(VMEM, VMEM, VMEM),
        scratch_shapes=[
            pltpu.VMEM((tokens, D), BF),
            pltpu.VMEM((w_all.shape[0], each, QW + 2 * HD), BF),
            pltpu.SemaphoreType.DMA((len(blocks),)),
            pltpu.SemaphoreType.DMA,
        ],
        cost_estimate=cost(2 * tokens * D * (QW + 2 * HD), 4 * tokens * D),
        compiler_params=BIG,
        name="norm_qkv",
    )(*blocks, gain, w_all, cos, sin)


def spread_kv():
    src = jnp.arange(2 * HD, dtype=jnp.int32)[:, None]
    col = jnp.arange(QW, dtype=jnp.int32)[None, :]
    key = (src == col // (GROUP * HALF) * HALF + col % HALF).astype(BF)
    value = (src == HD + col % HD).astype(BF)
    return key, value


def attend_kernel(prev_at, index, q_ref, prev_ref, here_ref, lo_ref, ek, ev, o_ref, o_index_ref):
    tok = q_ref.shape[0]
    two = jnp.concatenate([prev_ref[...], here_ref[...]], axis=0)
    keys = jnp.dot(two, ek[...], preferred_element_type=F32).astype(BF)
    values = jnp.dot(two, ev[...], preferred_element_type=F32).astype(BF)
    q = q_ref[...]
    key_at = lax.broadcasted_iota(jnp.int32, (tok, 2 * tok), 1)
    row_at = lax.broadcasted_iota(jnp.int32, (tok, 2 * tok), 0)
    allowed = (lo_ref[...] <= key_at) & (key_at <= row_at + tok)
    q_lane = lax.broadcasted_iota(jnp.int32, (tok, QW), 1)
    v_lane = lax.broadcasted_iota(jnp.int32, (2 * tok, QW), 1)
    total = jnp.zeros((tok, QW), F32)
    for h in range(GROUP):
        mine = jnp.where((q_lane // HALF) % GROUP == h, q, jnp.zeros_like(q))
        s = jnp.where(allowed, mm(mine, keys, NT) * SCALE, -1e30)
        expo = jnp.exp(s - jnp.max(s, axis=-1, keepdims=True))
        probs = (expo / jnp.sum(expo, axis=-1, keepdims=True)).astype(BF)
        total += mm(probs, jnp.where(v_lane // HD == h, values, jnp.zeros_like(values)), NN)
    o_ref[...] = total.astype(BF)
    o_index_ref[0] = o_ref[...]


def attend(prev_at, index, q, kv9, lo_col, ek, ev):
    tokens = q.shape[0]
    tok = tokens // TP
    full = lambda shape: pl.BlockSpec(shape, lambda r, p, i: (0, 0))
    return pl.pallas_call(
        attend_kernel,
        out_shape=(jax.ShapeDtypeStruct((tokens, QW), BF), jax.ShapeDtypeStruct((TP, tok, QW), BF)),
        grid_spec=pltpu.PrefetchScalarGridSpec(
            num_scalar_prefetch=2,
            grid=(TP,),
            in_specs=[
                pl.BlockSpec((tok, QW), lambda r, p, i: (r, 0)),
                pl.BlockSpec((tok, 2 * HD), lambda r, p, i: (p[r], 0)),
                pl.BlockSpec((tok, 2 * HD), lambda r, p, i: (r, 0)),
                pl.BlockSpec((tok, 1), lambda r, p, i: (r, 0)),
                full((2 * HD, QW)),
                full((2 * HD, QW)),
            ],
            out_specs=(
                pl.BlockSpec((tok, QW), lambda r, p, i: (r, 0)),
                pl.BlockSpec((1, tok, QW), lambda r, p, i: (i[r], 0, 0)),
            ),
        ),
        cost_estimate=cost(4 * tokens * 2 * tok * QW * GROUP, 4 * tokens * QW),
        compiler_params=BIG,
        name="attend",
    )(prev_at, index, q, kv9, kv9, lo_col, ek, ev)


def attend_back_kernel(here_at, prev_at, q_ref, do_ref, prev_ref, here_ref, lo_ref, cos, sin, ek, ev, dq_ref, dkv_ref, carry):
    step = pl.program_id(0)
    tok = q_ref.shape[0]

    @pl.when(step == 0)
    def _():
        carry[...] = jnp.zeros_like(carry)

    @pl.when(step < TP)
    def _():
        two = jnp.concatenate([prev_ref[...], here_ref[...]], axis=0)
        keys = jnp.dot(two, ek[...], preferred_element_type=F32).astype(BF)
        values = jnp.dot(two, ev[...], preferred_element_type=F32).astype(BF)
        q, d_o = q_ref[...], do_ref[0]
        key_at = lax.broadcasted_iota(jnp.int32, (2 * tok, tok), 0)
        row_at = lax.broadcasted_iota(jnp.int32, (2 * tok, tok), 1)
        allowed = (lo_ref[0] <= key_at) & (key_at <= row_at + tok)
        lane = lax.broadcasted_iota(jnp.int32, (tok, QW), 1)
        key_lane = lax.broadcasted_iota(jnp.int32, (2 * tok, QW), 1)
        d_q = jnp.zeros((tok, QW), F32)
        d_k = jnp.zeros((2 * tok, QW), F32)
        d_v = jnp.zeros((2 * tok, QW), F32)
        for h in range(GROUP):
            q_h = jnp.where((lane // HALF) % GROUP == h, q, jnp.zeros_like(q))
            do_h = jnp.where(lane // HD == h, d_o, jnp.zeros_like(d_o))
            k_h = jnp.where((key_lane // HALF) % GROUP == h, keys, jnp.zeros_like(keys))
            s = jnp.where(allowed, mm(keys, q_h, NT) * SCALE, -1e30)
            expo = jnp.exp(s - jnp.max(s, axis=0, keepdims=True))
            probs = expo / jnp.sum(expo, axis=0, keepdims=True)
            d_p = mm(values, do_h, NT)
            shift = jnp.sum(d_p * probs, axis=0, keepdims=True)
            d_s = (probs * (d_p - shift)).astype(BF)
            d_v += mm(probs.astype(BF), do_h, NN)
            d_k += mm(d_s, q_h, NN)
            d_q += mm(d_s, k_h, TN)
        d_q = d_q * SCALE
        a, b = d_q[:, : QW // 2], d_q[:, QW // 2 :]
        c, s = cos[...], sin[...]
        dq_ref[:, : QW // 2] = (a * c + b * s).astype(BF)
        dq_ref[:, QW // 2 :] = (b * c - a * s).astype(BF)
        d_k = d_k * SCALE

        def fold(v):
            v = v + pltpu.roll(v, HD, 1)
            return v + pltpu.roll(v, HALF, 1)

        first, second = fold(d_k[:, : QW // 2]), fold(d_k[:, QW // 2 :])
        whole = d_v[:, : QW // 2] + d_v[:, QW // 2 :]
        whole = whole + pltpu.roll(whole, HD, 1)
        low = lax.broadcasted_iota(jnp.int32, (2 * tok, 2 * HD), 1)
        d_kv = jnp.where(low < HALF, first, jnp.where(low < HD, second, whole))
        dkv_ref[...] = carry[...] + d_kv[:tok]
        carry[...] = d_kv[tok:]

    @pl.when(step == TP)
    def _():
        dkv_ref[...] = carry[...]


def attend_back(here_at, prev_at, q, d_o, kv9, lo_row, cos, sin, ek, ev):
    tokens = q.shape[0]
    tok = tokens // TP
    last = TP - 1
    here = lambda cols: pl.BlockSpec((tok, cols), lambda s, h, p: (h[jnp.minimum(s, last)], 0))
    full = lambda shape: pl.BlockSpec(shape, lambda s, h, p: (0, 0))
    return pl.pallas_call(
        attend_back_kernel,
        out_shape=(
            jax.ShapeDtypeStruct((tokens, QW), BF),
            jax.ShapeDtypeStruct((tokens + tok, 2 * HD), F32),
        ),
        grid_spec=pltpu.PrefetchScalarGridSpec(
            num_scalar_prefetch=2,
            grid=(TP + 1,),
            in_specs=[
                here(QW),
                pl.BlockSpec((1, tok, QW), lambda s, h, p: (jnp.minimum(s, last), 0, 0)),
                pl.BlockSpec((tok, 2 * HD), lambda s, h, p: (p[jnp.minimum(s, last)], 0)),
                here(2 * HD),
                pl.BlockSpec((1, 1, tok), lambda s, h, p: (h[jnp.minimum(s, last)], 0, 0)),
                here(2 * HD),
                here(2 * HD),
                full((2 * HD, QW)),
                full((2 * HD, QW)),
            ],
            out_specs=(
                here(QW),
                pl.BlockSpec((tok, 2 * HD), lambda s, h, p: (jnp.where(s == 0, TP, h[jnp.maximum(s - 1, 0)]), 0)),
            ),
            scratch_shapes=[pltpu.VMEM((tok, 2 * HD), F32)],
        ),
        cost_estimate=cost(10 * tokens * 2 * tok * QW * GROUP, 8 * tokens * QW),
        compiler_params=BIG,
        name="attend_back",
    )(here_at, prev_at, q, d_o, kv9, kv9, lo_row, cos, sin, ek, ev)


def ffn_forward(r, n2, dy, w, act_out, dgu_out, flat):
    each = n2.shape[0] // TP
    width = act_out.shape[1]
    two = 2 * width
    at = pl.ds(pl.multiple_of(r * each, each), each)
    gate_up = jnp.dot(n2[at, :], w[:, :two], preferred_element_type=F32)
    d_act = jnp.dot(dy[at, :], w[:, two:], preferred_element_type=F32)
    g, u = gate_up[:, :width], gate_up[:, width:]
    sg = jax.nn.sigmoid(g)
    gs = g * sg
    act = (gs * u).astype(BF)
    d_g = (d_act * u * (sg * (1.0 + g * (1.0 - sg)))).astype(BF)
    d_u = (d_act * gs).astype(BF)
    act_out[at, :] = act
    dgu_out[at, :width] = d_g
    dgu_out[at, width:] = d_u
    flat[:width, at] = d_g.T
    flat[width:two, at] = d_u.T
    flat[two:, at] = act.T


def ffn_back(flat, n2, dy, grad_out, held, out_sems):
    planes, wide, cols = grad_out.shape
    two = 2 * wide // 3

    def leave(z):
        return pltpu.make_async_copy(held.at[lax.rem(z, 2)], grad_out.at[z], out_sems.at[lax.rem(z, 2)])

    def back(z, carry):
        at = pl.ds(pl.multiple_of(z * cols, cols), cols)
        slot = lax.rem(z, 2)

        @pl.when(z >= 2)
        def _():
            leave(z - 2).wait()

        held[slot, :two, :] = jnp.dot(flat[:two, :], n2[:, at], preferred_element_type=F32).astype(BF)
        held[slot, two:, :] = jnp.dot(flat[two:, :], dy[:, at], preferred_element_type=F32).astype(BF)
        leave(z).start()
        return carry

    lax.fori_loop(0, planes, back, 0)
    leave(planes - 2).wait()
    leave(planes - 1).wait()


def ffn_kernel(*refs):
    n2_blocks, dy_blocks = refs[:TP], refs[TP : 2 * TP]
    w, act_out, dgu_out, grad_out, n2, dy, flat, held, n2_sems, dy_sems, out_sems = refs[2 * TP :]
    start_rows(n2_blocks, n2, n2_sems)
    start_rows(dy_blocks, dy, dy_sems)

    def forward(r, carry):
        wait_rows(r, n2, n2_sems)
        wait_rows(r, dy, dy_sems)
        ffn_forward(r, n2, dy, w, act_out, dgu_out, flat)
        return carry

    lax.fori_loop(0, TP, forward, 0)
    ffn_back(flat, n2, dy, grad_out, held, out_sems)


def ffn_forward_kernel(*refs):
    n2_blocks, dy_blocks = refs[:TP], refs[TP : 2 * TP]
    w, act_out, dgu_out, flat, n2, dy, n2_sems, dy_sems = refs[2 * TP :]
    start_rows(n2_blocks, n2, n2_sems)
    start_rows(dy_blocks, dy, dy_sems)

    def forward(r, carry):
        wait_rows(r, n2, n2_sems)
        wait_rows(r, dy, dy_sems)
        ffn_forward(r, n2, dy, w, act_out, dgu_out, flat)
        return carry

    lax.fori_loop(0, TP, forward, 0)


def ffn_back_kernel(*refs):
    n2_blocks, dy_blocks = refs[:TP], refs[TP : 2 * TP]
    flat, grad_out, n2, dy, held, n2_sems, dy_sems, out_sems = refs[2 * TP :]
    start_rows(n2_blocks, n2, n2_sems)
    start_rows(dy_blocks, dy, dy_sems)
    for r in range(TP):
        wait_rows(r, n2, n2_sems)
    for r in range(TP):
        wait_rows(r, dy, dy_sems)
    ffn_back(flat, n2, dy, grad_out, held, out_sems)


def ffn_call(kernel, n2_blocks, dy_blocks, last, outs, flops):
    tokens = TP * n2_blocks[0].shape[0]
    planes = lax.axis_size("z")
    wide = last.shape[1] if 2 not in outs or 0 in outs else last.shape[0]
    width = wide // 3
    shapes, specs, extra, sems = [], [], [], []
    if 0 in outs:
        shapes += [jax.ShapeDtypeStruct((tokens, width), BF), jax.ShapeDtypeStruct((tokens, 2 * width), BF)]
        specs += [VMEM, VMEM]
    if 1 in outs:
        shapes.append(jax.ShapeDtypeStruct((wide, tokens), BF))
        specs.append(VMEM)
    if 2 in outs:
        shapes.append(jax.ShapeDtypeStruct((planes, wide, D // planes), BF))
        specs.append(ANY)
        extra = ([pltpu.VMEM((wide, tokens), BF)] if 0 in outs else []) + [pltpu.VMEM((2, wide, D // planes), BF)]
        sems = [pltpu.SemaphoreType.DMA((2,))]
    return pl.pallas_call(
        kernel,
        out_shape=shapes,
        in_specs=[ANY] * (2 * TP) + [VMEM],
        out_specs=specs,
        scratch_shapes=[pltpu.VMEM((tokens, D), BF), pltpu.VMEM((tokens, D), BF)]
        + extra
        + [pltpu.SemaphoreType.DMA((TP,)), pltpu.SemaphoreType.DMA((TP,))]
        + sems,
        cost_estimate=cost(flops * tokens * D * width, 4 * tokens * D + 12 * width * D),
        compiler_params=BIG,
        name="ffn",
    )(*n2_blocks, *dy_blocks, last)


def down_kernel(parts, *refs):
    outs = refs[-2:]
    base = refs[2 * parts : -2]
    for at, out in enumerate(outs):
        term = base[at][0] if base else None
        for j in range(parts):
            more = mm(refs[j][0, at], refs[parts + j][...], NT)
            term = more if term is None else term + more
        out[0] = term.astype(out.dtype)


def down(parts, weights, last, groups, base=None, kind=BF):
    count = len(parts)
    tokens = parts[0].shape[0]
    tok = tokens // TP
    widths = [p.shape[1] for p in parts]
    columns = [w.shape[1] // width - 1 if last else 0 for w, width in zip(weights, widths)]
    pairs = [p.reshape(TP // 2, 2, tok, width) for p, width in zip(parts, widths)]
    rows = weights[0].shape[0]
    first, step = groups[0], groups[1] - groups[0]
    return pl.pallas_call(
        functools.partial(down_kernel, count),
        out_shape=[jax.ShapeDtypeStruct((len(groups), tok, rows), kind)] * 2,
        grid=(len(groups),),
        in_specs=[pl.BlockSpec((1, 2, tok, width), lambda s: (first + step * s, 0, 0, 0)) for width in widths]
        + [
            pl.BlockSpec((rows, width), lambda s, c=c: (0, c), pipeline_mode=pl.Buffered(1))
            for width, c in zip(widths, columns)
        ]
        + ([] if base is None else [pl.BlockSpec((1, tok, rows), lambda s: (first + step * s, 0, 0))] * 2),
        out_specs=[pl.BlockSpec((1, tok, rows), lambda s: (s, 0, 0))] * 2,
        cost_estimate=cost(4 * len(groups) * tok * sum(widths) * rows, rows * sum(widths) * 2 + len(groups) * tok * rows * 8),
        compiler_params=BIG,
        name="down",
    )(*pairs, *weights, *(() if base is None else base))


def start_wo(blocks, dst, sems):
    for r, ref in enumerate(blocks):
        pltpu.make_async_copy(ref, dst.at[r], sems.at[r]).start()


def wait_wo(r, dst, sems):
    pltpu.make_async_copy(dst.at[r], dst.at[r], sems.at[r]).wait()


def close_kernel(*refs):
    wo_blocks = refs[:TP]
    index, heads, x, gain, resid_out, n2_out, wo, sems = refs[TP:]
    start_wo(wo_blocks, wo, sems)
    y = x[...].astype(F32)
    for r in range(TP):
        wait_wo(r, wo, sems)
        y += mm(heads[index[r]], wo[r], NT)
    resid_out[...] = y
    n2_out[...] = (y * lax.rsqrt(jnp.mean(y * y, axis=-1, keepdims=True) + NORM_EPS) * gain[...]).astype(BF)


def close_attention(wo_blocks, index, heads, x, gain):
    tok = x.shape[0]
    return pl.pallas_call(
        close_kernel,
        out_shape=(jax.ShapeDtypeStruct((tok, D), F32), jax.ShapeDtypeStruct((tok, D), BF)),
        in_specs=[ANY] * TP + [SMEM] + [VMEM] * 3,
        out_specs=(VMEM, VMEM),
        scratch_shapes=[pltpu.VMEM((TP, D, QW), BF), pltpu.SemaphoreType.DMA((TP,))],
        cost_estimate=cost(2 * tok * D * D, 2 * D * D),
        compiler_params=BIG,
        name="close_attention",
    )(*wo_blocks, index, heads, x, gain)


def open_kernel(*refs):
    wo_blocks = refs[:TP]
    index, own, from_x, from_y, resid, dy, gain, back_out, att_out, heads, wo, sems = refs[TP:]
    start_wo(wo_blocks, wo, sems)
    d_n = own[...].astype(F32) + from_x[...].astype(F32) + from_y[...].astype(F32)
    y = resid[...]
    scale = lax.rsqrt(jnp.mean(y * y, axis=-1, keepdims=True) + NORM_EPS)
    unit = y * scale
    d_unit = d_n * gain[...]
    d_y = dy[...].astype(F32) + scale * (d_unit - unit * jnp.mean(d_unit * unit, axis=-1, keepdims=True))
    back_out[...] = d_y
    att_out[...] = d_y.astype(BF)
    att = att_out[...]
    for r in range(TP):
        wait_wo(r, wo, sems)
        heads[index[r]] = jnp.dot(att, wo[r], preferred_element_type=F32).astype(BF)


def open_attention(wo_blocks, index, terms, resid, dy, gain):
    tok = dy.shape[0]
    return pl.pallas_call(
        open_kernel,
        out_shape=(
            jax.ShapeDtypeStruct((tok, D), F32),
            jax.ShapeDtypeStruct((tok, D), BF),
            jax.ShapeDtypeStruct((TP, tok, QW), BF),
        ),
        in_specs=[ANY] * TP + [SMEM] + [VMEM] * 6,
        out_specs=(VMEM, VMEM, VMEM),
        scratch_shapes=[pltpu.VMEM((TP, D, QW), BF), pltpu.SemaphoreType.DMA((TP,))],
        cost_estimate=cost(2 * tok * D * D, 2 * D * D),
        compiler_params=BIG,
        name="open_attention",
    )(*wo_blocks, index, *terms, resid, dy, gain)


def turn_grad_kernel(count, *refs):
    blocks, left, out, rows, sems = refs[:count], *refs[count:]
    start_rows(blocks, rows, sems)
    for r in range(TP):
        wait_rows(r, rows, sems)
    planes, _, cols = out.shape

    def back(z, carry):
        at = pl.ds(pl.multiple_of(z * cols, cols), cols)
        out[z] = mm(left[...], rows[:, at], TN).astype(BF)
        return carry

    lax.fori_loop(0, planes, back, 0)


def turn_grad(left, blocks):
    tokens, cols = left.shape
    planes = lax.axis_size("z")
    return pl.pallas_call(
        functools.partial(turn_grad_kernel, len(blocks)),
        out_shape=jax.ShapeDtypeStruct((planes, cols, D // planes), BF),
        in_specs=[ANY] * len(blocks) + [VMEM],
        out_specs=VMEM,
        scratch_shapes=[pltpu.VMEM((tokens, D), BF), pltpu.SemaphoreType.DMA((TP,))],
        cost_estimate=cost(2 * tokens * D * cols, 2 * tokens * D),
        compiler_params=BIG,
        name="turn_grad",
    )(*blocks, left)


def to_pieces(pieces):
    rows, cols = pieces.shape[1:]
    return trade(pieces).reshape(TP * rows, cols)


def sum_z(grad):
    planes, cols, wide = grad.shape
    return lax.psum_scatter(grad.reshape(planes * cols, wide), "z", scatter_dimension=0, tiled=True)


def give_back(summed):
    return trade(turn(summed))


def by_plane(grad):
    planes = lax.axis_size("z")
    return grad.reshape(grad.shape[0], planes, D // planes).transpose(1, 0, 2)


def pick(blocks, at):
    return lax.dynamic_index_in_dim(blocks, at, 0, keepdims=False)


def on_device(hidden_in, segment_ids, w_attn, w_ffn, gains, out_grad):
    tok = hidden_in.shape[0]
    rows = w_attn.shape[0]
    me = lax.axis_index(PLANE)
    z = lax.axis_index("z")
    tokens = TP * tok
    steps = jnp.arange(TP, dtype=jnp.int32)
    rel = me ^ steps
    perm = fold_order()
    ek, ev = spread_kv()

    own_start = (z * TP + me) * tok
    own_lo = segment_ids - own_start + tok
    extra = jnp.zeros((EXTRA, AW), BF)
    extra = extra.at[0, : 2 * rows].set(gains.reshape(-1))
    extra = extra.at[1, :tok].set((own_lo // 2).astype(BF)).at[2, :tok].set((own_lo % 2).astype(BF))

    attn_pieces = cut_attn(w_attn, perm)
    attn_pieces = jnp.concatenate([attn_pieces, jnp.broadcast_to(extra, (TP, *extra.shape))], axis=1)
    attn_rows = to_pieces(attn_pieces)
    x_begun = gather_begin(hidden_in)
    pieces = cut_ffn(after(w_ffn, attn_rows))
    rows_0 = to_pieces(pieces[0])
    w_0 = gather_z(rows_0)
    x_blocks = gather_end(*x_begun)
    dy_begun = gather_begin(after(out_grad, *x_begun[1:]))
    attn_all = after(gather_z(attn_rows), rows_0).reshape(-1, rows + EXTRA, AW)
    w_own = attn_all[:, :rows].reshape(D, AW)
    wqkv, wo = w_own[:, : QW + 2 * HD], w_own[:, QW + 2 * HD :]
    gains_full = attn_all[:, rows, : 2 * rows].reshape(-1, 2, rows).transpose(1, 0, 2).reshape(2, D).astype(F32)

    plane_lo = attn_rows.reshape(TP, rows + EXTRA, -1)[:, rows + 1 : rows + 3, :tok].astype(jnp.int32)
    lo = jnp.take(2 * plane_lo[:, 0] + plane_lo[:, 1], rel, axis=0)
    positions = jnp.arange(tok, dtype=jnp.int32)[None] + tok - lo
    freqs = 1.0 / ROPE_BASE ** (jnp.arange(HALF, dtype=F32) * (2.0 / HD))
    angles = positions.reshape(tokens).astype(F32)[:, None] * freqs
    cosine = jnp.tile(jnp.cos(angles), (1, GROUP))
    sine = jnp.tile(jnp.sin(angles), (1, GROUP))

    early = 6
    halves = []
    for first, last in ((0, early), (early, TP)):
        at = slice(first * tok, last * tok)
        halves.append(norm_qkv(x_blocks[first:last], gains_full[:1], attn_all, cosine[at], sine[at]))
    (n1, q, kv), (n1_late, q_late, kv_late) = halves
    q, kv = jnp.concatenate([q, q_late], axis=0), jnp.concatenate([kv, kv_late], axis=0)
    wo_begun = gather_begin(wo)
    rows_1 = to_pieces(after(pieces[1], attn_all))
    q = after(q, rows_1, *wo_begun[1:], *dy_begun[1:])
    before = along_z(pick(kv.reshape(TP, tok, 2 * HD), me ^ (TP - 1)), 1)
    kv9 = jnp.concatenate([kv, before], axis=0)
    prev_at = jnp.where(rel == 0, TP, (rel - 1) ^ me)
    mixed, heads = attend(prev_at, rel, q, kv9, lo.reshape(tokens, 1), ek, ev)

    wo_blocks = gather_end(*wo_begun)
    heads = trade(heads)
    dy_blocks = gather_end(*after(dy_begun, mixed))
    w_1 = gather_z(rows_1)
    x_own = hidden_in.astype(F32)
    residual, normed_two = close_attention(wo_blocks, rel, heads, after(hidden_in, w_0), gains_full[1:])
    n2_blocks = gather_plane(normed_two)

    act_0, d_gu_0, grad_0 = ffn_call(ffn_kernel, n2_blocks, dy_blocks, w_0, (0, 2), 18)
    so_far = down([d_gu_0], [w_0], False, (0, 1, 2, 3), kind=F32)
    sum_0 = sum_z(grad_0)
    act_1, d_gu_1, flat_1 = ffn_call(ffn_forward_kernel, n2_blocks, dy_blocks, after(w_1, so_far[0]), (0, 1), 9)
    d_n2_parts = {groups: down([d_gu_1], [w_1], False, groups, so_far) for groups in ((3, 2), (1, 0))}
    d_n2_terms, unused = scatter_plane(d_n2_parts.get)
    (grad_1,) = ffn_call(ffn_back_kernel, n2_blocks, dy_blocks, after(flat_1, d_n2_parts[1, 0][0]), (2,), 9)
    sum_1 = sum_z(grad_1)
    acts, w_all = [after(act_0, grad_1), act_1], [w_0, w_1]
    f_parts = {groups: down(acts, w_all, True, groups) for groups in ((3, 2), (1, 0))}
    d_n2_terms = after(d_n2_terms, *f_parts.values())
    d_resid, d_att, d_heads = open_attention(wo_blocks, rel, d_n2_terms, residual, out_grad, gains_full[1:])
    d_o = trade(d_heads)
    d_att_begun = gather_begin(after(d_att, d_o))
    here_at = me ^ steps
    prev_abs = jnp.where(steps == 0, TP, (steps - 1) ^ me)
    turned_0 = turn(sum_0)
    d_q, d_kv9 = attend_back(here_at, prev_abs, q, after(d_o, turned_0), kv9, lo.reshape(TP, 1, tok), cosine, sine, ek, ev)
    f_terms, unused = scatter_plane(lambda groups: after(f_parts[groups], d_heads), (d_q,))
    hidden_out = (residual + total(*f_terms)).astype(BF)
    d_att_blocks = gather_end(*after(d_att_begun, d_q))
    piece_0 = trade(turned_0)
    wo_grad = turn_grad(after(mixed, piece_0), d_att_blocks)
    back = along_z(d_kv9[tokens:].astype(BF), -1)
    last = me ^ (TP - 1)
    d_kv = d_kv9[:tokens].reshape(TP, tok, 2 * HD)
    d_kv = jnp.where((steps == last)[:, None, None], d_kv + back.astype(F32)[None], d_kv).reshape(tokens, 2 * HD)
    c, s = cosine[:, :HALF], sine[:, :HALF]
    a, b = d_kv[:, :HALF], d_kv[:, HALF:HD]
    d_qkv = jnp.concatenate(
        [d_q, (a * c + b * s).astype(BF), (b * c - a * s).astype(BF), d_kv[:, HD:].astype(BF)], axis=1
    )
    cut = early * tok
    qkv_grad = by_plane((mm(d_qkv[:cut], n1, TN) + mm(d_qkv[cut:], n1_late, TN)).astype(BF))
    attn_sum = jnp.concatenate([qkv_grad, wo_grad], axis=1)
    turned = turn(sum_z(attn_sum))
    attn_back = trade(turned)
    d_qkv = after(d_qkv, attn_sum, *f_terms)
    d_n1_terms, unused = scatter_plane(lambda groups: down([d_qkv], [wqkv], False, groups))
    d_normed = total(*d_n1_terms)
    pieces = [piece_0, give_back(sum_1)]
    pieces[1] = after(pieces[1], turned)
    scale = lax.rsqrt(jnp.mean(x_own * x_own, axis=-1, keepdims=True) + NORM_EPS)
    unit = x_own * scale
    d_unit = d_normed * gains_full[0]
    in_grad = d_resid + scale * (d_unit - unit * jnp.mean(d_unit * unit, axis=-1, keepdims=True))
    ffn_grad, term_two = paste_ffn(pieces, w_ffn)
    attn_grad, term_one = paste_attn(attn_back, w_attn, perm)
    gains_grad = jnp.concatenate([term_one, term_two], axis=1).T / gains.astype(F32)
    return hidden_out, in_grad.astype(BF), attn_grad, ffn_grad, gains_grad


def solution(mesh):
    fine = Mesh(mesh.devices.reshape(-1, 2, 2, 2), EVERY)
    rows = P(EVERY, None)
    in_specs = (rows, P(EVERY), rows, rows, P(None, EVERY), rows)
    out_specs = (rows, rows, rows, rows, P(None, EVERY))
    return jax.shard_map(
        on_device, mesh=fine, in_specs=in_specs, out_specs=out_specs, check_vma=False
    )
```
